256 devices in a mesh: view: 8 (over x, core), gs: 32 (over z, y).
Axes of the slice: x: 4, y: 4, z: 8, core: 2. Of those that a mesh axis runs over, the one named last changes fastest.
Arguments:
- params: float32 [59, 262144], P(None, 'gs'), as said below
- cam_pos: float32 [8, 3], P('view'), may hold values from -0.03 to 0.03
- req_ids: int32 [8, 32, 32, 64], P('view', 'gs'), may hold values from 0 to 8191, as said below
- tile_slots: int32 [8, 512, 64], P('view', 'gs'), may hold values from 0 to 2047, as said below
- tile_len: int32 [8, 512], P('view', 'gs'), may hold values from 1 to 64, as said below
- cotangent: float32 [8, 3, 131072], P('view', None, 'gs'), may hold values from -6 to 6
Outputs:
- rendered: float32 [8, 3, 131072], P('view', None, 'gs')
- grads: float32 [59, 262144], P(None, ('gs', 'view'))
The draws below stay inside these ranges and needn't reach their ends.
Inputs may be any that keep to these rules, and one draw needn't show every extreme that they name: `req_ids`: within each view, renderer and owner the 64 ids are distinct, and within a view two renderers never ask an owner for the same id. `tile_slots`: the 64 slots of a tile's list are distinct, and within a view no slot stands in two lists of the same renderer. `tile_len`: the first tile of every renderer has all 64 entries live. `params`: row 0 within [-3.4, 3.4], row 1 within [-3.4 h, 3.4 h] with h = 2, row 2 within [2, 4], rows 3 to 5 within [log 0.02, log 0.12], row 6 within [1, 2], rows 7 to 9 within [-1, 1], row 10 within [-4.5, 1].
All inputs are finite; a program needn't handle non-finite values.
Results may differ from the reference program's by a relative error of at most 0.0003.
Values sent between devices are 32-bit elements; how exact they have to be, the bound alone decides.
A program may use at most 64 MiB of HBM per device.

```python
import jax
import jax.numpy as jnp
from jax import lax

NPARAM = 59
G_DEV = 8192
K = 64
TILES_DEV = 16
VIEWS = 8
RANKS = 32
CAP = 64
G_TOTAL = 262144
PIX = 131072


def owner_layout(key):
    keys = jax.random.split(jax.random.fold_in(key, 101), RANKS)

    def shuffled(owner_key):
        return jax.random.permutation(owner_key, G_DEV)
    return jax.vmap(shuffled)(keys).astype(jnp.int32)


def distinct_order(key, shape, count):
    scores = jax.random.randint(key, shape + (count,), 0, 4096, dtype=jnp.int32)
    scores = scores * count + jnp.arange(count, dtype=jnp.int32)
    return jnp.argsort(scores, axis=-1).astype(jnp.int32)


def request_layout(key):
    per_tile = CAP // TILES_DEV
    spread = G_DEV // (RANKS * TILES_DEV)
    layout = owner_layout(key)
    picked = distinct_order(jax.random.fold_in(key, 103), (VIEWS, RANKS, RANKS, TILES_DEV), spread)[..., :per_tile]
    region = jnp.arange(RANKS, dtype=jnp.int32)[:, None] * TILES_DEV + jnp.arange(TILES_DEV, dtype=jnp.int32)[None, :]
    where = region[None, :, None, :, None] * spread + picked
    owner_index = jnp.broadcast_to(jnp.arange(RANKS, dtype=jnp.int32)[None, None, :, None, None], where.shape)
    chosen = layout[owner_index, where].reshape(VIEWS, RANKS, RANKS, CAP)
    placing = distinct_order(jax.random.fold_in(key, 107), (VIEWS, RANKS, RANKS), CAP)
    inverse = jnp.argsort(placing, axis=-1).astype(jnp.int32)
    requests = jnp.take_along_axis(chosen, inverse, axis=-1)
    return (requests.astype(jnp.int32), placing)


def draw_params(key, part):
    layout = owner_layout(key)
    key = jax.random.fold_in(key, 5)
    spread = G_DEV // (RANKS * TILES_DEV)
    n_rows = TILES_DEV * RANKS // 16
    position = jnp.argsort(layout, axis=-1).astype(jnp.int32)
    home = (position // spread).reshape(G_TOTAL)
    keys = jax.random.split(key, 10)
    inside = jax.random.uniform(keys[0], (2, G_TOTAL), jnp.float32)
    depth = 2.0 + 2.0 * jax.random.uniform(keys[1], (1, G_TOTAL), jnp.float32)
    scale_unit = jax.random.uniform(keys[2], (3, G_TOTAL), jnp.float32)
    logit_unit = jax.random.uniform(keys[3], (1, G_TOTAL), jnp.float32)
    quat_w = 1.0 + jax.random.uniform(keys[4], (1, G_TOTAL), jnp.float32)
    quat_v = jax.random.uniform(keys[5], (3, G_TOTAL), jnp.float32, -1.0, 1.0)
    reach = 14.0 + 20.0 * jax.random.uniform(keys[8], (G_TOTAL,), jnp.float32)
    faraway = jax.random.bernoulli(keys[9], 0.5, (G_TOTAL,))
    harmonics = 0.5 * jax.random.normal(keys[6], (48, G_TOTAL), jnp.float32)
    log_scales = -3.912 + 1.7918 * scale_unit
    logits = jnp.where(faraway[None, :], -1.0, -4.5) + 2.0 * logit_unit
    column = (home % 16).astype(jnp.float32)
    screen_inner = (16.0 * column + 16.0 * inside[0]) / 128.0 - 1.0
    screen_y = (16.0 * (home // 16).astype(jnp.float32) + 16.0 * inside[1]) / 128.0 - n_rows / 16.0
    left_half = home % 16 < 8
    edge = jnp.where(left_half, (16.0 * column + 15.5) / 128.0 - 1.0, (16.0 * column + 0.5) / 128.0 - 1.0)
    squares = jnp.exp(2.0 * log_scales)
    quat_norm = jnp.sqrt(quat_w[0] * quat_w[0] + jnp.sum(quat_v * quat_v, axis=0))
    unit_w = quat_w[0] / quat_norm
    unit_x = quat_v[0] / quat_norm
    unit_y = quat_v[1] / quat_norm
    unit_z = quat_v[2] / quat_norm
    rot_xa = 1.0 - 2.0 * (unit_y * unit_y + unit_z * unit_z)
    rot_xb = 2.0 * (unit_x * unit_y - unit_w * unit_z)
    rot_xc = 2.0 * (unit_x * unit_z + unit_w * unit_y)
    rot_za = 2.0 * (unit_x * unit_z - unit_w * unit_y)
    rot_zb = 2.0 * (unit_y * unit_z + unit_w * unit_x)
    rot_zc = 1.0 - 2.0 * (unit_x * unit_x + unit_y * unit_y)
    sigma_xx = rot_xa * rot_xa * squares[0] + rot_xb * rot_xb * squares[1] + rot_xc * rot_xc * squares[2]
    sigma_xz = rot_xa * rot_za * squares[0] + rot_xb * rot_zb * squares[1] + rot_xc * rot_zc * squares[2]
    sigma_zz = rot_za * rot_za * squares[0] + rot_zb * rot_zb * squares[1] + rot_zc * rot_zc * squares[2]
    jac_x = 1.2 / depth[0]
    jac_z = -edge / depth[0]
    cov_xx = jac_x * jac_x * sigma_xx + 2.0 * jac_x * jac_z * sigma_xz + jac_z * jac_z * sigma_zz + 0.3 / 16384.0
    offset = jnp.sqrt(reach * cov_xx)
    screen_outer = jnp.where(left_half, edge + offset, edge - offset)
    screen_x = jnp.where(faraway, screen_outer, screen_inner)
    means = jnp.stack([screen_x, screen_y], axis=0) * depth / 1.2
    return jnp.concatenate([means, depth, log_scales, quat_w, quat_v, logits, harmonics], axis=0)


def draw_req_ids(key, part):
    requests, placing = request_layout(key)
    return requests


def draw_tile_slots(key, part):
    requests, placing = request_layout(key)
    key = jax.random.fold_in(key, 13)
    per_tile = CAP // TILES_DEV
    slots = placing.reshape(VIEWS, RANKS, RANKS, TILES_DEV, per_tile) + (jnp.arange(RANKS, dtype=jnp.int32) * CAP)[None, None, :, None, None]
    slots = slots.transpose(0, 1, 3, 2, 4).reshape(VIEWS, RANKS, TILES_DEV, RANKS * per_tile)
    order = distinct_order(key, (VIEWS, RANKS, TILES_DEV), RANKS * per_tile)[..., :K]
    lists = jnp.take_along_axis(slots, order, axis=-1)
    return lists.reshape(VIEWS, RANKS * TILES_DEV, K).astype(jnp.int32)


def draw_tile_len(key, part):
    key = jax.random.fold_in(key, 17)
    key_cap, key_len = jax.random.split(key)
    device_cap = jax.random.randint(key_cap, (VIEWS, RANKS, 1), K // 4, K + 1)
    lengths = jax.random.randint(key_len, (VIEWS, RANKS, TILES_DEV), 1, device_cap + 1)
    lengths = lengths.at[:, :, 0].set(K)
    return lengths.reshape(VIEWS, RANKS * TILES_DEV).astype(jnp.int32)


def block_levels(own_key, shape, cuts, least, top_value):
    factor_of = 1.0
    for axis_at, shards_of in cuts:
        heights = jax.random.uniform(jax.random.fold_in(jax.random.fold_in(own_key, 6), axis_at), (shards_of,), jnp.float32, least / len(cuts), top_value / len(cuts))
        factor_of = factor_of * jnp.repeat(jnp.exp(heights), shape[axis_at] // shards_of).reshape((-1,) + (1,) * (len(shape) - 1 - axis_at))
    return factor_of


def normal_values(stream_key, extent, scale, bound, cuts=(), kind=jnp.bfloat16):
    result = jax.random.normal(stream_key, extent, jnp.float32) * scale
    if len(cuts) > 0:
        result = block_levels(stream_key, extent, cuts, -0.22, 0.18) * result
    return jnp.clip(result, min=-bound, max=bound).astype(kind)


def setup_inputs(seed: int = 0) -> dict:
    seeds = jax.random.split(jax.random.key(seed), 7)
    params = draw_params(jax.random.fold_in(seeds[6], 71), 0)
    cam_pos = jnp.clip(jax.random.uniform(seeds[1], (VIEWS, 3), jnp.float32, -0.03, 0.03) * block_levels(seeds[1], (VIEWS, 3), ((0, 8),), -0.4, 0.0), -0.03, 0.03)
    req_ids = draw_req_ids(jax.random.fold_in(seeds[6], 71), 0)
    tile_slots = draw_tile_slots(jax.random.fold_in(seeds[6], 71), 0)
    tile_len = draw_tile_len(jax.random.fold_in(seeds[6], 71), 0)
    cotangent = normal_values(seeds[5], (VIEWS, 3, PIX), 1.0, 6.0, ((0, 8), (2, 32)), jnp.float32)
    return dict(params=params, cam_pos=cam_pos, req_ids=req_ids, tile_slots=tile_slots, tile_len=tile_len, cotangent=cotangent)


focal = 1.2
dilate = 0.3 / 16384.0
sh_zero = 0.28209479177387814
sh_one = 0.4886025119029199
sh_two = [1.0925484305920792, -1.0925484305920792, 0.31539156525252005, -1.0925484305920792, 0.5462742152960396]
sh_three = [-0.5900435899266435, 2.890611442640554, -0.4570457994644658, 0.3731763325901154, -0.4570457994644658, 1.445305721320277, -0.5900435899266435]

def slot_features(gathered, camera):
    rel = gathered[0:3] - camera[:, None]
    pos_x = rel[0]
    pos_y = rel[1]
    depth = rel[2]
    scales = jnp.exp(gathered[3:6])
    quat = gathered[6:10]
    quat_norm = jnp.sqrt(lax.optimization_barrier(jnp.sum(quat * quat, axis=0)))
    quat_w = quat[0] / quat_norm
    quat_x = quat[1] / quat_norm
    quat_y = quat[2] / quat_norm
    quat_z = quat[3] / quat_norm
    rotation = [[1 - 2 * (quat_y * quat_y + quat_z * quat_z), 2 * (quat_x * quat_y - quat_w * quat_z), 2 * (quat_x * quat_z + quat_w * quat_y)], [2 * (quat_x * quat_y + quat_w * quat_z), 1 - 2 * (quat_x * quat_x + quat_z * quat_z), 2 * (quat_y * quat_z - quat_w * quat_x)], [2 * (quat_x * quat_z - quat_w * quat_y), 2 * (quat_y * quat_z + quat_w * quat_x), 1 - 2 * (quat_x * quat_x + quat_y * quat_y)]]
    factor = [[rotation[row][col] * scales[col] for col in range(3)] for row in range(3)]
    sigma = [[factor[row][0] * factor[col][0] + factor[row][1] * factor[col][1] + factor[row][2] * factor[col][2] for col in range(3)] for row in range(3)]
    inv_depth = 1.0 / depth
    zeros_row = jnp.zeros_like(depth)
    jacobian = [[focal * inv_depth, zeros_row, -focal * pos_x * inv_depth * inv_depth], [zeros_row, focal * inv_depth, -focal * pos_y * inv_depth * inv_depth]]
    middle = [[jacobian[row][0] * sigma[0][col] + jacobian[row][1] * sigma[1][col] + jacobian[row][2] * sigma[2][col] for col in range(3)] for row in range(2)]
    cov = [[middle[row][0] * jacobian[col][0] + middle[row][1] * jacobian[col][1] + middle[row][2] * jacobian[col][2] for col in range(2)] for row in range(2)]
    cov_a = cov[0][0] + dilate
    cov_b = cov[0][1]
    cov_c = cov[1][1] + dilate
    determinant = cov_a * cov_c - cov_b * cov_b
    conic_a = cov_c / determinant
    conic_b = -cov_b / determinant
    conic_c = cov_a / determinant
    center_x = focal * pos_x * inv_depth
    center_y = focal * pos_y * inv_depth
    opacity = jax.nn.sigmoid(gathered[10])
    distance = jnp.sqrt(pos_x * pos_x + pos_y * pos_y + depth * depth)
    dir_x = pos_x / distance
    dir_y = pos_y / distance
    dir_z = depth / distance
    sq_x = dir_x * dir_x
    sq_y = dir_y * dir_y
    sq_z = dir_z * dir_z
    basis = jnp.stack([jnp.full_like(dir_x, sh_zero), -sh_one * dir_y, sh_one * dir_z, -sh_one * dir_x, sh_two[0] * dir_x * dir_y, sh_two[1] * dir_y * dir_z, sh_two[2] * (2 * sq_z - sq_x - sq_y), sh_two[3] * dir_x * dir_z, sh_two[4] * (sq_x - sq_y), sh_three[0] * dir_y * (3 * sq_x - sq_y), sh_three[1] * dir_x * dir_y * dir_z, sh_three[2] * dir_y * (4 * sq_z - sq_x - sq_y), sh_three[3] * dir_z * (2 * sq_z - 3 * sq_x - 3 * sq_y), sh_three[4] * dir_x * (4 * sq_z - sq_x - sq_y), sh_three[5] * dir_z * (sq_x - sq_y), sh_three[6] * dir_x * (sq_x - 3 * sq_y)], axis=0)
    harmonics = gathered[11:59].reshape(3, 16, -1)
    color = jnp.einsum('cks,ks->cs', harmonics, basis, precision=lax.Precision.HIGHEST) + 0.5
    geometry = jnp.stack([center_x, center_y, conic_a, conic_b, conic_c, opacity], axis=0)
    return jnp.concatenate([geometry, color], axis=0)

def render(features, slots, lengths, tile_ids, n_rows):
    entries = jnp.take(features, slots, axis=1)
    lane = jnp.arange(256, dtype=jnp.int32)
    column = tile_ids % 16
    row_of = tile_ids // 16
    pixel_x = ((column[:, None] * 16 + lane[None, :] % 16).astype(jnp.float32) + 0.5) / 128.0 - 1.0
    pixel_y = ((row_of[:, None] * 16 + lane[None, :] // 16).astype(jnp.float32) + 0.5) / 128.0 - n_rows / 16.0
    off_x = pixel_x[:, None, :] - entries[0][:, :, None]
    off_y = pixel_y[:, None, :] - entries[1][:, :, None]
    quadric = entries[2][:, :, None] * off_x * off_x + 2.0 * entries[3][:, :, None] * off_x * off_y + entries[4][:, :, None] * off_y * off_y
    live = (jnp.arange(slots.shape[1], dtype=jnp.int32)[None, :] < lengths[:, None]).astype(jnp.float32)
    strength = entries[5] * live
    alpha = strength[:, :, None] * jnp.exp(-0.5 * quadric)
    through = jnp.cumprod(1.0 - alpha, axis=1)
    before = jnp.concatenate([jnp.ones_like(through[:, :1]), through[:, :-1]], axis=1)
    blend = before * alpha
    colors = jnp.einsum('ctk,tkp->ctp', entries[6:9], blend, precision=lax.Precision.HIGHEST)
    return colors.reshape(3, -1)

def reference(params, cam_pos, req_ids, tile_slots, tile_len, cotangent):
    n_rows = TILES_DEV * RANKS // 16
    offsets = jnp.arange(RANKS, dtype=jnp.int32)[:, None] * G_DEV

    def per_view(total, view_items):
        view_req, view_slots, view_len, view_cot, camera = view_items
        slots_rank = view_slots.reshape(RANKS, TILES_DEV, K)
        len_rank = view_len.reshape(RANKS, TILES_DEV)
        cot_rank = view_cot.reshape(3, RANKS, TILES_DEV * 256).transpose(1, 0, 2)

        def per_rank(acc, rank_items):
            rank_req, rank_slots, rank_len, rank_cot, rank_index = rank_items
            global_ids = (offsets + rank_req).reshape(-1).astype(jnp.int32)
            gathered = params[:, global_ids]
            tile_ids = rank_index * TILES_DEV + jnp.arange(TILES_DEV, dtype=jnp.int32)

            def local(columns):
                return render(slot_features(columns, camera), rank_slots, rank_len, tile_ids, n_rows)
            picture, pullback = jax.vjp(local, gathered)
            grad_slots = pullback(rank_cot)[0]
            acc = acc.at[:, global_ids].add(grad_slots)
            return (acc, picture)
        ranks = jnp.arange(RANKS, dtype=jnp.int32)
        total, pictures = lax.scan(per_rank, total, (view_req, slots_rank, len_rank, cot_rank, ranks))
        return (total, pictures.transpose(1, 0, 2).reshape(3, -1))
    start = jnp.zeros((NPARAM, G_TOTAL), jnp.float32)
    grads, rendered = lax.scan(per_view, start, (req_ids, tile_slots, tile_len, cotangent, cam_pos))
    return (rendered, grads)
```

```python
import functools

import jax
import jax.numpy as jnp
from jax import lax
from jax.experimental import pallas as pl
from jax.experimental.pallas import tpu as pltpu
from jax.sharding import PartitionSpec as P

MESH = pl.DeviceIdType.MESH
F32 = jnp.float32
BF16 = jnp.bfloat16
TILES = 16
ENTRIES = 64
ROWS = TILES * ENTRIES
PIXELS = 256
CAP = 64
LANES = 128

focal = 1.2 * 128.0
dilate = 0.3
sh_zero = 0.28209479177387814
sh_one = 0.4886025119029199
sh_two = [
    1.0925484305920792,
    -1.0925484305920792,
    0.31539156525252005,
    -1.0925484305920792,
    0.5462742152960396,
]
sh_three = [
    -0.5900435899266435,
    2.890611442640554,
    -0.4570457994644658,
    0.3731763325901154,
    -0.4570457994644658,
    1.445305721320277,
    -0.5900435899266435,
]


def covariance(log_scales, quat):
    squares = [jnp.exp(2.0 * value) for value in log_scales]
    norm_sq = quat[0] * quat[0] + quat[1] * quat[1] + quat[2] * quat[2] + quat[3] * quat[3]
    inv_norm = 1.0 / jnp.sqrt(norm_sq)
    w, x, y, z = [value * inv_norm for value in quat]
    rotation = [
        [1 - 2 * (y * y + z * z), 2 * (x * y - w * z), 2 * (x * z + w * y)],
        [2 * (x * y + w * z), 1 - 2 * (x * x + z * z), 2 * (y * z - w * x)],
        [2 * (x * z - w * y), 2 * (y * z + w * x), 1 - 2 * (x * x + y * y)],
    ]
    scaled = [[rotation[i][j] * squares[j] for j in range(3)] for i in range(3)]

    def entry(i, j):
        return (
            scaled[i][0] * rotation[j][0]
            + scaled[i][1] * rotation[j][1]
            + scaled[i][2] * rotation[j][2]
        )

    return [entry(0, 0), entry(0, 1), entry(0, 2), entry(1, 1), entry(1, 2), entry(2, 2)]


def geometry(x, y, z, sigma):
    s00, s01, s02, s11, s12, s22 = sigma
    inv_z = 1.0 / z
    jac = focal * inv_z
    center_x = jac * x
    center_y = jac * y
    jac_x = -center_x * inv_z
    jac_y = -center_y * inv_z
    jac_sq = jac * jac
    cov_a = jac_sq * s00 + 2.0 * (jac * jac_x) * s02 + jac_x * jac_x * s22 + dilate
    cov_b = jac_sq * s01 + jac * (jac_y * s02 + jac_x * s12) + jac_x * jac_y * s22
    cov_c = jac_sq * s11 + 2.0 * (jac * jac_y) * s12 + jac_y * jac_y * s22 + dilate
    inv_det = 1.0 / (cov_a * cov_c - cov_b * cov_b)
    return center_x, center_y, cov_c * inv_det, -cov_b * inv_det, cov_a * inv_det


def harmonic_basis(x, y, z):
    inv_distance = 1.0 / jnp.sqrt(x * x + y * y + z * z)
    dx = x * inv_distance
    dy = y * inv_distance
    dz = z * inv_distance
    xx = dx * dx
    yy = dy * dy
    zz = dz * dz
    xy = dx * dy
    yz = dy * dz
    xz = dx * dz
    return [
        -sh_one * dy,
        sh_one * dz,
        -sh_one * dx,
        sh_two[0] * xy,
        sh_two[1] * yz,
        sh_two[2] * (2 * zz - xx - yy),
        sh_two[3] * xz,
        sh_two[4] * (xx - yy),
        sh_three[0] * dy * (3 * xx - yy),
        sh_three[1] * xy * dz,
        sh_three[2] * dy * (4 * zz - xx - yy),
        sh_three[3] * dz * (2 * zz - 3 * xx - 3 * yy),
        sh_three[4] * dx * (4 * zz - xx - yy),
        sh_three[5] * dz * (xx - yy),
        sh_three[6] * dx * (xx - 3 * yy),
    ]


def pieces(value, count):
    out = []
    for at in range(count):
        piece = value.astype(BF16)
        out.append(piece)
        if at + 1 < count:
            value = value - piece.astype(F32)
    return out


def dot(left, right, dims):
    return lax.dot_general(left, right, ((dims[0], dims[1]), ((), ())), preferred_element_type=F32)


def iota(shape, axis):
    return lax.broadcasted_iota(jnp.int32, shape, axis)


def kernel(
    owners,
    views,
    params_ref,
    cam_ref,
    ids_ref,
    slots_ref,
    len_ref,
    cot_ref,
    image_ref,
    grads_ref,
    held,
    held_cot,
    image,
    summed,
    ids_out,
    ids_in,
    cam_out,
    cam_in,
    table,
    low_hot,
    high_hot,
    feat_out,
    feat_in,
    wide,
    exponent,
    along,
    alpha_all,
    blend_all,
    split_a,
    split_b,
    split_c,
    split_d,
    grad_out,
    grad_in,
    dense,
    view_in,
    load_sem,
    store_sem,
    ids_s,
    ids_r,
    feat_s,
    feat_r,
    grad_s,
    grad_r,
    cam_s,
    cam_r,
    view_s,
    view_r,
):
    me = lax.axis_index("gs")
    my_view = lax.axis_index("view")
    blocks = held.shape[1]
    chunk = blocks // views
    slots_all = owners * CAP
    slot_tiles = slots_all // LANES

    def load(j):
        return pltpu.make_async_copy(
            params_ref.at[:, pl.ds(pl.multiple_of(j * LANES, LANES), LANES)],
            held.at[:, j, :],
            load_sem.at[0],
        )

    def load_body(j, carry):
        load(j).start()
        return carry

    lax.fori_loop(0, blocks, load_body, 0)

    pltpu.make_async_copy(cot_ref, held_cot, load_sem.at[1]).start()

    barrier = pltpu.get_barrier_semaphore()

    def greet(off, carry):
        peer = lax.rem(me + off, owners)
        pl.semaphore_signal(barrier, inc=1, device_id=(my_view, peer), device_id_type=MESH)
        return carry

    lax.fori_loop(1, owners, greet, 0)

    def greet_view(off, carry):
        peer = lax.rem(my_view + off, views)
        pl.semaphore_signal(barrier, inc=1, device_id=(peer, me), device_id_type=MESH)
        return carry

    lax.fori_loop(1, views, greet_view, 0)

    def gs_copy(out, into, send, recv, to, sender):
        return pltpu.make_async_remote_copy(
            src_ref=out.at[to],
            dst_ref=into.at[sender],
            send_sem=send.at[to],
            recv_sem=recv.at[sender],
            device_id=(my_view, to),
            device_id_type=MESH,
        )

    def gs_send(out, into, send, recv):
        def body(off, carry):
            peer = lax.rem(me + off, owners)
            gs_copy(out, into, send, recv, peer, me).start()
            return carry

        lax.fori_loop(1, owners, body, 0)

    def gs_wait_recv(out, into, send, recv):
        def body(off, carry):
            peer = lax.rem(me + off, owners)
            gs_copy(out, into, send, recv, peer, peer).wait_recv()
            return carry

        lax.fori_loop(1, owners, body, 0)

    def gs_wait_send(out, into, send, recv):
        def body(off, carry):
            peer = lax.rem(me + off, owners)
            gs_copy(out, into, send, recv, peer, me).wait_send()
            return carry

        lax.fori_loop(1, owners, body, 0)

    asked = ids_ref[...]
    doubled = jnp.concatenate([asked, asked], axis=1)
    my_half = (iota(doubled.shape, 1) >> 6) == lax.rem(me, 2)
    ids_out[...] = jnp.where(my_half, doubled, 0).reshape(owners, 1, LANES)
    cam_x = cam_ref[0, 0]
    cam_y = cam_ref[0, 1]
    cam_z = cam_ref[0, 2]
    cam_row = iota((8, LANES), 0)
    cam_tile = jnp.where(cam_row == 0, cam_x, jnp.where(cam_row == 1, cam_y, cam_z))
    cam_out[...] = cam_tile

    pl.semaphore_wait(barrier, owners + views - 2)

    gs_send(ids_out, ids_in, ids_s, ids_r)
    ids_in[me] = ids_out[me]

    def cam_copy(to, sender):
        return pltpu.make_async_remote_copy(
            src_ref=cam_out,
            dst_ref=cam_in.at[sender],
            send_sem=cam_s.at[to],
            recv_sem=cam_r.at[sender],
            device_id=(to, me),
            device_id_type=MESH,
        )

    def cam_send(off, carry):
        cam_copy(lax.rem(my_view + off, views), my_view).start()
        return carry

    lax.fori_loop(1, views, cam_send, 0)
    cam_in[my_view] = cam_tile

    pltpu.make_async_copy(held, held, load_sem.at[0]).wait()

    def features_body(at, carry):
        rows = pl.ds(pl.multiple_of(at * 16, 16), 16)

        def get(r):
            return held[r, rows, :]

        x = get(0) - cam_x
        y = get(1) - cam_y
        z = get(2) - cam_z
        sigma = covariance([get(3), get(4), get(5)], [get(6), get(7), get(8), get(9)])
        values = list(geometry(x, y, z, sigma))
        values.append(-jnp.log(1.0 + jnp.exp(-get(10))))
        basis = harmonic_basis(x, y, z)
        for c in range(3):
            total = sh_zero * get(11 + 16 * c) + 0.5
            for k in range(15):
                total = total + basis[k] * get(12 + 16 * c + k)
            values.append(total)
        half = lax.div(at, 2)
        inner = lax.rem(at, 2)
        lanes = pl.ds(pl.multiple_of(half * LANES, LANES), LANES)
        for c in range(9):
            for s, piece in enumerate(pieces(values[c], 3)):
                table[s, pl.ds(pl.multiple_of(c * 32 + inner * 16, 16), 16), lanes] = piece
        return carry

    lax.fori_loop(0, blocks // 16, features_body, 0)

    gs_wait_recv(ids_out, ids_in, ids_s, ids_r)

    def hot_body(at, carry):
        ids = ids_in[2 * at] + ids_in[2 * at + 1]
        low = (ids & (LANES - 1)) + ((ids >> 12) << 7)
        high = (ids >> 7) & 31
        lanes = pl.ds(pl.multiple_of(at * LANES, LANES), LANES)
        low_hot[:, lanes] = (iota((256, LANES), 0) == low).astype(F32).astype(BF16)
        high_hot[:, lanes] = (iota((32, LANES), 0) == high).astype(F32)
        return carry

    lax.fori_loop(0, slot_tiles, hot_body, 0)

    lane_half = iota((8, LANES), 1) < CAP

    def gather_body(at, carry):
        lanes = pl.ds(pl.multiple_of(at * 256, 256), 256)
        right = low_hot[:, lanes]
        picked = dot(table[0], right, ((1,), (0,)))
        picked += dot(table[1], right, ((1,), (0,)))
        picked += dot(table[2], right, ((1,), (0,)))
        mask = high_hot[:, lanes]
        rows = [
            jnp.sum(picked[c * 32 : c * 32 + 32] * mask, axis=0, keepdims=True) for c in range(9)
        ]
        blank = jnp.zeros((1, 256), F32)
        left_group = jnp.concatenate(rows[0:5] + [blank] * 3, axis=0)
        right_group = jnp.concatenate(rows[5:9] + [blank] * 4, axis=0)
        for part in range(2):
            a = left_group[:, part * LANES : (part + 1) * LANES]
            b = right_group[:, part * LANES : (part + 1) * LANES]
            even = jnp.where(lane_half, a, pltpu.roll(b, CAP, 1))
            odd = jnp.where(lane_half, pltpu.roll(a, CAP, 1), b)
            feat_out[4 * at + 2 * part] = even
            feat_out[4 * at + 2 * part + 1] = odd
        return carry

    lax.fori_loop(0, slots_all // 256, gather_body, 0)

    def feat_copy(out, into, send, recv, to, sender):
        return pltpu.make_async_remote_copy(
            src_ref=out.at[to, pl.ds(0, 5)],
            dst_ref=into.at[sender, pl.ds(0, 5)],
            send_sem=send.at[to],
            recv_sem=recv.at[sender],
            device_id=(my_view, to),
            device_id_type=MESH,
        )

    def feat_send(out, into, send, recv):
        def body(off, carry):
            feat_copy(out, into, send, recv, lax.rem(me + off, owners), me).start()
            return carry

        lax.fori_loop(1, owners, body, 0)

    def feat_wait_recv(out, into, send, recv):
        def body(off, carry):
            peer = lax.rem(me + off, owners)
            feat_copy(out, into, send, recv, peer, peer).wait_recv()
            return carry

        lax.fori_loop(1, owners, body, 0)

    def feat_wait_send(out, into, send, recv):
        def body(off, carry):
            peer = lax.rem(me + off, owners)
            feat_copy(out, into, send, recv, peer, me).wait_send()
            return carry

        lax.fori_loop(1, owners, body, 0)

    feat_send(feat_out, feat_in, feat_s, feat_r)
    feat_in[me] = feat_out[me]

    lane_row = iota((TILES, ROWS), 1)
    tile_hot = (lane_row & 15) == iota((TILES, ROWS), 0)
    tile_mask = tile_hot.astype(F32)
    entry_hot = ((iota((ENTRIES, ROWS), 1) >> 4) == iota((ENTRIES, ROWS), 0)).astype(F32).astype(BF16)
    slots = slots_ref[...]
    both = jnp.concatenate([slots >> 6, slots & (CAP - 1)], axis=0).astype(F32).astype(BF16)
    spread = dot(both, entry_hot, ((1,), (0,)))
    owner_row = jnp.sum(spread[0:TILES] * tile_mask, axis=0, keepdims=True)
    place_row = jnp.sum(spread[TILES:] * tile_mask, axis=0, keepdims=True)
    lengths = jnp.broadcast_to(len_ref[...], (TILES, TILES)).astype(F32).astype(BF16)
    len_row = dot(lengths, tile_mask.astype(BF16), ((1,), (0,)))[0:1]
    entry_row = iota((1, ROWS), 1)
    live = (entry_row >> 4).astype(F32) < len_row
    place_sub = iota((LANES, ROWS), 0)
    place_left = (place_sub.astype(F32) == place_row).astype(F32).astype(BF16)
    place_right = ((place_sub - CAP).astype(F32) == place_row).astype(F32).astype(BF16)
    center_of_x = (entry_row & 15).astype(F32) * 16.0 + (8.0 - 128.0)
    center_of_y = (me * 16 + 8 - 8 * owners).astype(F32)

    pixel = iota((8, PIXELS), 1)
    mono_x = (pixel & 15).astype(F32) - 7.5
    mono_y = (pixel >> 4).astype(F32) - 7.5
    kind = iota((8, PIXELS), 0)
    monomials = jnp.where(kind == 0, mono_x * mono_x, 0.0)
    monomials = jnp.where(kind == 1, mono_x * mono_y, monomials)
    monomials = jnp.where(kind == 2, mono_y * mono_y, monomials)
    monomials = jnp.where(kind == 3, mono_x, monomials)
    monomials = jnp.where(kind == 4, mono_y, monomials)
    monomials = jnp.where(kind == 5, 1.0, monomials)
    monomials_two = jnp.concatenate([monomials, jnp.zeros_like(monomials)], axis=0).astype(BF16)
    monomials_four = jnp.concatenate([monomials] * 3 + [jnp.zeros_like(monomials)], axis=0).astype(BF16)

    pltpu.make_async_copy(cot_ref, held_cot, load_sem.at[1]).wait()
    cot = jnp.concatenate(
        [held_cot[pl.ds(half, 3 * TILES, stride=2), :] for half in range(2)], axis=1
    )
    cot_high, cot_low = pieces(cot, 2)

    feat_wait_recv(feat_out, feat_in, feat_s, feat_r)
    arrived = feat_in[...].reshape(owners * 8, LANES)
    arrived_pieces = pieces(arrived, 3)
    left_parts = []
    right_parts = []
    for at in range(ROWS // 256):
        lanes = slice(at * 256, at * 256 + 256)
        owners_here = owner_row[:, lanes]
        totals = []
        for hot in (place_left, place_right):
            found = dot(arrived_pieces[0], hot[:, lanes], ((1,), (0,)))
            found += dot(arrived_pieces[1], hot[:, lanes], ((1,), (0,)))
            found += dot(arrived_pieces[2], hot[:, lanes], ((1,), (0,)))
            total = jnp.zeros((8, 256), F32)
            for o in range(owners):
                total = jnp.where(owners_here == float(o), found[o * 8 : o * 8 + 8], total)
            totals.append(total)
        left_parts.append(totals[0])
        right_parts.append(totals[1])
    left = jnp.concatenate(left_parts, axis=1)
    right = jnp.concatenate(right_parts, axis=1)
    center_x = left[0:1] - center_of_x
    center_y = left[1:2] - center_of_y
    conic_a = left[2:3]
    conic_b = left[3:4]
    conic_c = left[4:5]
    log_opacity = right[0:1]
    colors = [right[1 + c : 2 + c] for c in range(3)]

    lin_x = conic_a * center_x + conic_b * center_y
    lin_y = conic_b * center_x + conic_c * center_y
    blank = jnp.zeros((1, ROWS), F32)
    coefs = jnp.concatenate(
        [
            jnp.where(live, -0.5 * conic_a, 0.0),
            jnp.where(live, -conic_b, 0.0),
            jnp.where(live, -0.5 * conic_c, 0.0),
            jnp.where(live, lin_x, 0.0),
            jnp.where(live, lin_y, 0.0),
            jnp.where(live, log_opacity - 0.5 * (lin_x * center_x + lin_y * center_y), -1000.0),
            blank,
            blank,
        ],
        axis=0,
    )
    coef_pieces = jnp.concatenate(
        [piece.astype(F32) for piece in pieces(coefs, 3)] + [jnp.zeros_like(coefs)], axis=0
    )
    exponent[...] = dot(coef_pieces.T.astype(BF16), monomials_four, ((1,), (0,)))

    spread_color = jnp.concatenate([colors[c] * tile_mask for c in range(3)], axis=0)
    color_high, color_low = pieces(spread_color, 2)
    color_sides = jnp.concatenate([color_high, color_high, color_low], axis=0)
    cot_sides = jnp.concatenate([cot_high, cot_low, cot_high], axis=0)
    along[...] = dot(color_sides, cot_sides, ((0,), (0,)))

    def forward_body(k, through):
        rows = pl.ds(pl.multiple_of(k * TILES, TILES), TILES)
        alpha = jnp.exp(exponent[rows, :])
        blend = through * alpha
        alpha_all[rows, :] = alpha
        blend_all[rows, :] = blend
        high, low = pieces(blend, 2)
        split_a[rows, :] = high
        split_b[rows, :] = low
        return through - blend

    lax.fori_loop(0, ENTRIES, forward_body, jnp.ones((TILES, PIXELS), F32))

    def backward_body(step, behind):
        rows = pl.ds(pl.multiple_of((ENTRIES - 1 - step) * TILES, TILES), TILES)
        gain = along[rows, :] - behind
        high, low = pieces(blend_all[rows, :] * gain, 2)
        split_c[rows, :] = high
        split_d[rows, :] = low
        return behind + alpha_all[rows, :] * gain

    lax.fori_loop(0, ENTRIES, backward_body, jnp.zeros((TILES, PIXELS), F32))

    moments = dot(monomials_two, split_c[...], ((1,), (1,))) + dot(
        monomials_two, split_d[...], ((1,), (1,))
    )
    cot_both = jnp.concatenate([cot_high, cot_low], axis=0)
    by_color = dot(cot_both, split_a[...], ((1,), (1,)))
    by_color = (
        by_color[0 : 3 * TILES]
        + by_color[3 * TILES :]
        + dot(cot_high, split_b[...], ((1,), (1,)))
    )
    grad_colors = [
        jnp.sum(by_color[c * TILES : (c + 1) * TILES] * tile_mask, axis=0, keepdims=True)
        for c in range(3)
    ]
    m_xx, m_xy, m_yy, m_x, m_y, m_one = [moments[row : row + 1] for row in range(6)]
    off_x = m_x - center_x * m_one
    off_y = m_y - center_y * m_one
    off_xx = m_xx - center_x * (m_x + off_x)
    off_xy = m_xy - center_x * m_y - center_y * off_x
    off_yy = m_yy - center_y * (m_y + off_y)
    entry_grads = jnp.concatenate(
        [
            conic_a * off_x + conic_b * off_y,
            conic_b * off_x + conic_c * off_y,
            -0.5 * off_xx,
            -off_xy,
            -0.5 * off_yy,
            blank,
            blank,
            blank,
            m_one,
            grad_colors[0],
            grad_colors[1],
            grad_colors[2],
            blank,
            blank,
            blank,
            blank,
        ],
        axis=0,
    )
    grad_high, grad_low = pieces(entry_grads, 2)
    owner_wide = jnp.broadcast_to(owner_row, (16, ROWS)).astype(BF16)
    nothing = jnp.zeros((16, ROWS), BF16)
    for o in range(owners):
        here = owner_wide == jnp.asarray(o, BF16)
        wide[o * 16 : o * 16 + 16, 0:ROWS] = jnp.where(here, grad_high, nothing)
        wide[(owners + o) * 16 : (owners + o) * 16 + 16, 0:ROWS] = jnp.where(here, grad_low, nothing)
    place_both = place_left + place_right
    by_slot = dot(wide[0 : 32 * owners, 0:ROWS], place_both, ((1,), (1,)))
    by_slot = (by_slot[0 : 16 * owners] + by_slot[16 * owners :]).reshape(owners, 16, LANES)
    lane_half_all = iota((owners, 8, LANES), 2) < CAP
    grad_out[...] = jnp.where(lane_half_all, by_slot[:, 0:8], by_slot[:, 8:16])

    feat_send(grad_out, grad_in, grad_s, grad_r)
    grad_in[me] = grad_out[me]

    color_both = jnp.concatenate([color_high, color_low], axis=0)
    shown = dot(color_both, split_a[...], ((1,), (0,)))
    shown = (
        shown[0 : 3 * TILES]
        + shown[3 * TILES :]
        + dot(color_high, split_b[...], ((1,), (0,)))
    )
    for half in range(2):
        image[pl.ds(half, 3 * TILES, stride=2), :] = shown[:, half * LANES : half * LANES + LANES]
    pltpu.make_async_copy(image, image_ref, store_sem.at[0]).start()

    feat_wait_recv(grad_out, grad_in, grad_s, grad_r)

    def scatter_body(at, carry):
        even = grad_in[2 * at]
        odd = grad_in[2 * at + 1]
        a = jnp.where(lane_half, even, pltpu.roll(odd, CAP, 1))
        b = jnp.where(lane_half, pltpu.roll(even, CAP, 1), odd)
        lanes = pl.ds(pl.multiple_of(at * LANES, LANES), LANES)
        mask = high_hot[:, lanes].astype(BF16)
        for c in range(9):
            row = a[c : c + 1] if c < 5 else b[c - 5 : c - 4]
            for s, piece in enumerate(pieces(jnp.broadcast_to(row, (32, LANES)), 2)):
                wide[s * 288 + c * 32 : s * 288 + c * 32 + 32, lanes] = piece * mask
        return carry

    lax.fori_loop(0, slot_tiles, scatter_body, 0)
    placed = dot(wide[0:576, 0:slots_all], low_hot[...], ((1,), (1,)))
    placed = (placed[0:288] + placed[288:576]).reshape(9, 32, 256)
    dense[:, 0:32, :] = placed[:, :, 0:LANES]
    dense[:, 32:64, :] = placed[:, :, LANES:256]

    def view_copy(to, sender):
        return pltpu.make_async_remote_copy(
            src_ref=dense.at[:, pl.ds(pl.multiple_of(to * chunk, chunk), chunk), :],
            dst_ref=view_in.at[sender],
            send_sem=view_s.at[to],
            recv_sem=view_r.at[sender],
            device_id=(to, me),
            device_id_type=MESH,
        )

    def view_send(off, carry):
        view_copy(lax.rem(my_view + off, views), my_view).start()
        return carry

    lax.fori_loop(1, views, view_send, 0)
    mine = pl.ds(pl.multiple_of(my_view * chunk, chunk), chunk)
    view_in[my_view] = dense[:, mine, :]

    def cam_wait(off, carry):
        peer = lax.rem(my_view + off, views)
        cam_copy(peer, peer).wait_recv()
        cam_copy(peer, my_view).wait_send()
        return carry

    lax.fori_loop(1, views, cam_wait, 0)
    gs_wait_send(ids_out, ids_in, ids_s, ids_r)
    feat_wait_send(feat_out, feat_in, feat_s, feat_r)
    feat_wait_send(grad_out, grad_in, grad_s, grad_r)
    pltpu.make_async_copy(image, image_ref, store_sem.at[0]).wait()

    def get(r):
        return held[r, mine, :]

    scale_quat = [get(r) for r in range(3, 10)]

    def shape_of(values):
        return covariance(values[0:3], values[3:7])

    sigma, shape_back = jax.vjp(shape_of, scale_quat)
    zero = jnp.zeros((chunk, LANES), F32)
    for r in range(59):
        summed[r] = zero

    def view_wait(off, carry):
        peer = lax.rem(my_view + off, views)
        view_copy(peer, peer).wait_recv()
        view_copy(peer, my_view).wait_send()
        return carry

    lax.fori_loop(1, views, view_wait, 0)

    def view_body(v, carry):
        totals = carry
        camera = cam_in[v]
        x = get(0) - camera[0:1]
        y = get(1) - camera[1:2]
        z = get(2) - camera[2:3]
        grads = [view_in[v, c] for c in range(9)]
        _, geometry_back = jax.vjp(geometry, x, y, z, sigma)
        gx, gy, gz, g_sigma = geometry_back(tuple(grads[0:5]))
        basis, basis_back = jax.vjp(harmonic_basis, x, y, z)
        g_basis = [zero] * 15
        for c in range(3):
            color_grad = grads[6 + c]
            summed[11 + 16 * c] += sh_zero * color_grad
            for k in range(15):
                row = 12 + 16 * c + k
                summed[row] += basis[k] * color_grad
                g_basis[k] = g_basis[k] + get(row) * color_grad
        hx, hy, hz = basis_back(g_basis)
        add = [gx + hx, gy + hy, gz + hz, grads[5]] + list(g_sigma)
        return tuple(t + a for t, a in zip(totals, add))

    totals = lax.fori_loop(0, views, view_body, tuple([zero] * 10))
    for r in range(3):
        summed[r] = totals[r]
    (by_shape,) = shape_back(list(totals[4:10]))
    for r in range(7):
        summed[3 + r] = by_shape[r]
    summed[10] = totals[3] / (1.0 + jnp.exp(get(10)))

    def store_grads(j):
        return pltpu.make_async_copy(
            summed.at[:, j, :],
            grads_ref.at[:, pl.ds(pl.multiple_of(j * LANES, LANES), LANES)],
            store_sem.at[1],
        )

    def store_grads_body(j, carry):
        store_grads(j).start()
        return carry

    lax.fori_loop(0, chunk, store_grads_body, 0)
    pltpu.make_async_copy(summed, summed, store_sem.at[1]).wait()


def local(owners, views, params, cam_pos, req_ids, tile_slots, tile_len, cotangent):
    count, owned = params.shape
    blocks = owned // LANES
    chunk = blocks // views
    slots_all = owners * CAP
    vmem = pltpu.VMEM
    dma = pltpu.SemaphoreType.DMA
    whole = pl.BlockSpec(memory_space=vmem)
    image, grads = pl.pallas_call(
        functools.partial(kernel, owners, views),
        out_shape=(
            jax.ShapeDtypeStruct((6 * TILES, LANES), F32),
            jax.ShapeDtypeStruct((count, owned // views), F32),
        ),
        in_specs=[
            pl.BlockSpec(memory_space=pltpu.HBM),
            pl.BlockSpec(memory_space=pltpu.SMEM),
            whole,
            whole,
            whole,
            pl.BlockSpec(memory_space=pltpu.HBM),
        ],
        out_specs=(pl.BlockSpec(memory_space=pltpu.HBM), pl.BlockSpec(memory_space=pltpu.HBM)),
        scratch_shapes=[
            vmem((count, blocks, LANES), F32),
            vmem((6 * TILES, LANES), F32),
            vmem((6 * TILES, LANES), F32),
            vmem((count, chunk, LANES), F32),
            vmem((owners, 1, LANES), jnp.int32),
            vmem((owners, 1, LANES), jnp.int32),
            vmem((8, LANES), F32),
            vmem((views, 8, LANES), F32),
            vmem((3, 288, 256), BF16),
            vmem((256, slots_all), BF16),
            vmem((32, slots_all), F32),
            vmem((owners, 8, LANES), F32),
            vmem((owners, 8, LANES), F32),
            vmem((max(576, 32 * owners), max(ROWS, slots_all)), BF16),
            vmem((ROWS, PIXELS), F32),
            vmem((ROWS, PIXELS), F32),
            vmem((ROWS, PIXELS), F32),
            vmem((ROWS, PIXELS), F32),
            vmem((ROWS, PIXELS), BF16),
            vmem((ROWS, PIXELS), BF16),
            vmem((ROWS, PIXELS), BF16),
            vmem((ROWS, PIXELS), BF16),
            vmem((owners, 8, LANES), F32),
            vmem((owners, 8, LANES), F32),
            vmem((9, blocks, LANES), F32),
            vmem((views, 9, chunk, LANES), F32),
            dma((2,)),
            dma((2,)),
        ]
        + [dma((owners,)) for _ in range(6)]
        + [dma((views,)) for _ in range(4)],
        compiler_params=pltpu.CompilerParams(
            collective_id=0, has_side_effects=True, vmem_limit_bytes=40 * 1024 * 1024
        ),
        cost_estimate=pl.CostEstimate(
            flops=2_000_000_000, bytes_accessed=4_000_000, transcendentals=300_000
        ),
    )(
        params,
        cam_pos,
        req_ids.reshape(owners, CAP),
        tile_slots.reshape(TILES, ENTRIES),
        tile_len,
        cotangent.reshape(6 * TILES, LANES),
    )
    return image.reshape(cotangent.shape), grads


def solution(mesh):
    placed = (
        P(None, "gs"),
        P("view", None),
        P("view", "gs", None, None),
        P("view", "gs", None),
        P("view", "gs"),
        P("view", None, "gs"),
    )
    return jax.shard_map(
        functools.partial(local, mesh.shape["gs"], mesh.shape["view"]),
        mesh=mesh,
        in_specs=placed,
        out_specs=(P("view", None, "gs"), P(None, ("gs", "view"))),
        check_vma=False,
    )
```

```python
import functools

import jax
import jax.numpy as jnp
from jax import lax
from jax.experimental import pallas as pl
from jax.experimental.pallas import tpu as pltpu
from jax.sharding import PartitionSpec as P

MESH = pl.DeviceIdType.MESH
F32 = jnp.float32
BF16 = jnp.bfloat16
TILES = 16
ENTRIES = 64
ROWS = TILES * ENTRIES
PIXELS = 256
CAP = 64
LANES = 128
LINE = 4

focal = 1.2 * 128.0
dilate = 0.3
sh_zero = 0.28209479177387814
sh_one = 0.4886025119029199
sh_two = [
    1.0925484305920792,
    -1.0925484305920792,
    0.31539156525252005,
    -1.0925484305920792,
    0.5462742152960396,
]
sh_three = [
    -0.5900435899266435,
    2.890611442640554,
    -0.4570457994644658,
    0.3731763325901154,
    -0.4570457994644658,
    1.445305721320277,
    -0.5900435899266435,
]


def covariance(log_scales, quat):
    squares = [jnp.exp(2.0 * value) for value in log_scales]
    norm_sq = quat[0] * quat[0] + quat[1] * quat[1] + quat[2] * quat[2] + quat[3] * quat[3]
    inv_norm = 1.0 / jnp.sqrt(norm_sq)
    w, x, y, z = [value * inv_norm for value in quat]
    rotation = [
        [1 - 2 * (y * y + z * z), 2 * (x * y - w * z), 2 * (x * z + w * y)],
        [2 * (x * y + w * z), 1 - 2 * (x * x + z * z), 2 * (y * z - w * x)],
        [2 * (x * z - w * y), 2 * (y * z + w * x), 1 - 2 * (x * x + y * y)],
    ]
    scaled = [[rotation[i][j] * squares[j] for j in range(3)] for i in range(3)]

    def entry(i, j):
        return (
            scaled[i][0] * rotation[j][0]
            + scaled[i][1] * rotation[j][1]
            + scaled[i][2] * rotation[j][2]
        )

    return [entry(0, 0), entry(0, 1), entry(0, 2), entry(1, 1), entry(1, 2), entry(2, 2)]


def geometry(x, y, z, sigma):
    s00, s01, s02, s11, s12, s22 = sigma
    inv_z = 1.0 / z
    jac = focal * inv_z
    center_x = jac * x
    center_y = jac * y
    jac_x = -center_x * inv_z
    jac_y = -center_y * inv_z
    jac_sq = jac * jac
    cov_a = jac_sq * s00 + 2.0 * (jac * jac_x) * s02 + jac_x * jac_x * s22 + dilate
    cov_b = jac_sq * s01 + jac * (jac_y * s02 + jac_x * s12) + jac_x * jac_y * s22
    cov_c = jac_sq * s11 + 2.0 * (jac * jac_y) * s12 + jac_y * jac_y * s22 + dilate
    inv_det = 1.0 / (cov_a * cov_c - cov_b * cov_b)
    return center_x, center_y, cov_c * inv_det, -cov_b * inv_det, cov_a * inv_det


def harmonic_basis(x, y, z):
    inv_distance = 1.0 / jnp.sqrt(x * x + y * y + z * z)
    dx = x * inv_distance
    dy = y * inv_distance
    dz = z * inv_distance
    xx = dx * dx
    yy = dy * dy
    zz = dz * dz
    xy = dx * dy
    yz = dy * dz
    xz = dx * dz
    return [
        -sh_one * dy,
        sh_one * dz,
        -sh_one * dx,
        sh_two[0] * xy,
        sh_two[1] * yz,
        sh_two[2] * (2 * zz - xx - yy),
        sh_two[3] * xz,
        sh_two[4] * (xx - yy),
        sh_three[0] * dy * (3 * xx - yy),
        sh_three[1] * xy * dz,
        sh_three[2] * dy * (4 * zz - xx - yy),
        sh_three[3] * dz * (2 * zz - 3 * xx - 3 * yy),
        sh_three[4] * dx * (4 * zz - xx - yy),
        sh_three[5] * dz * (xx - yy),
        sh_three[6] * dx * (xx - 3 * yy),
    ]


def pieces(value, count):
    out = []
    for at in range(count):
        piece = value.astype(BF16)
        out.append(piece)
        if at + 1 < count:
            value = value - piece.astype(F32)
    return out


def dot(left, right, dims):
    return lax.dot_general(left, right, ((dims[0], dims[1]), ((), ())), preferred_element_type=F32)


def iota(shape, axis):
    return lax.broadcasted_iota(jnp.int32, shape, axis)


def kernel(
    owners,
    views,
    params_ref,
    cam_ref,
    ids_ref,
    slots_ref,
    len_ref,
    cot_ref,
    image_ref,
    grads_ref,
    held,
    asked,
    cam_held,
    slots_held,
    len_held,
    held_cot,
    image,
    summed,
    ids_out,
    ids_in,
    cam_out,
    cam_in,
    table,
    low_hot,
    high_hot,
    feat_out,
    feat_in,
    wide,
    gathered,
    exponent,
    along,
    alpha_all,
    blend_all,
    split_a,
    split_b,
    split_c,
    split_d,
    grad_out,
    grad_in,
    dense,
    view_in,
    load_sem,
    store_sem,
    ids_s,
    ids_r,
    feat_s,
    feat_r,
    grad_s,
    grad_r,
    cam_s,
    cam_r,
    view_s,
    view_r,
):
    me = lax.axis_index("gs")
    my_view = lax.axis_index("view")
    my_y = lax.rem(me, LINE)
    my_z = lax.div(me, LINE)
    my_x = lax.div(my_view, 2)
    my_core = lax.rem(my_view, 2)
    planes = owners // LINE
    blocks = held.shape[1]
    chunk = blocks // views

    def plane(i):
        half = (i + 1) // 2
        odd = i % 2
        return lax.rem(my_z + odd * half + (1 - odd) * (planes - half), planes)

    def peers(i, first):
        return [plane(i) * LINE + lax.rem(my_y + step, LINE) for step in range(1 if first else 0, LINE)]

    def view_peer(i):
        pair = i // 2
        step = pair + pair // 2 - 2 * (pair // 3)
        return lax.rem(my_x + step, views // 2) * 2 + lax.rem(my_core + i, 2)

    ids_load = pltpu.make_async_copy(ids_ref.at[0, 0], asked, load_sem.at[2])
    cam_load = pltpu.make_async_copy(cam_ref, cam_held, load_sem.at[3])
    slots_load = pltpu.make_async_copy(slots_ref.at[0], slots_held, load_sem.at[4])
    len_load = pltpu.make_async_copy(len_ref, len_held, load_sem.at[5])
    cot_load = pltpu.make_async_copy(cot_ref, held_cot, load_sem.at[1])
    ids_load.start()
    cam_load.start()

    barrier = pltpu.get_barrier_semaphore()

    def greet(off, carry):
        peer = lax.rem(me + off, owners)
        pl.semaphore_signal(barrier, inc=1, device_id=(my_view, peer), device_id_type=MESH)
        return carry

    lax.fori_loop(1, owners, greet, 0)

    def greet_view(off, carry):
        peer = lax.rem(my_view + off, views)
        pl.semaphore_signal(barrier, inc=1, device_id=(peer, me), device_id_type=MESH)
        return carry

    lax.fori_loop(1, views, greet_view, 0)

    def load_body(j, carry):
        pltpu.make_async_copy(
            params_ref.at[:, pl.ds(pl.multiple_of(j * LANES, LANES), LANES)],
            held.at[:, j, :],
            load_sem.at[0],
        ).start()
        return carry

    lax.fori_loop(0, blocks, load_body, 0)
    slots_load.start()
    len_load.start()
    cot_load.start()

    def ids_copy(to, sender):
        return pltpu.make_async_remote_copy(
            src_ref=ids_out.at[to],
            dst_ref=ids_in.at[sender],
            send_sem=ids_s.at[to],
            recv_sem=ids_r.at[sender],
            device_id=(my_view, to),
            device_id_type=MESH,
        )

    def feat_copy(to, sender):
        return pltpu.make_async_remote_copy(
            src_ref=feat_out.at[to, pl.ds(0, 5)],
            dst_ref=feat_in.at[sender, pl.ds(0, 5)],
            send_sem=feat_s.at[to],
            recv_sem=feat_r.at[sender],
            device_id=(my_view, to),
            device_id_type=MESH,
        )

    def grad_copy(to, sender):
        return pltpu.make_async_remote_copy(
            src_ref=grad_out.at[to, pl.ds(0, 5)],
            dst_ref=grad_in.at[sender, pl.ds(0, 5)],
            send_sem=grad_s.at[to],
            recv_sem=grad_r.at[sender],
            device_id=(my_view, to),
            device_id_type=MESH,
        )

    def cam_copy(to, sender):
        return pltpu.make_async_remote_copy(
            src_ref=cam_out,
            dst_ref=cam_in.at[sender],
            send_sem=cam_s.at[to],
            recv_sem=cam_r.at[sender],
            device_id=(to, me),
            device_id_type=MESH,
        )

    def view_copy(to, sender):
        return pltpu.make_async_remote_copy(
            src_ref=dense.at[:, pl.ds(pl.multiple_of(to * chunk, chunk), chunk), :],
            dst_ref=view_in.at[sender],
            send_sem=view_s.at[to],
            recv_sem=view_r.at[sender],
            device_id=(to, me),
            device_id_type=MESH,
        )

    def wait_sent(copy):
        def body(off, carry):
            copy(lax.rem(me + off, owners), me).wait_send()
            return carry

        lax.fori_loop(1, owners, body, 0)

    ids_load.wait()
    doubled = jnp.concatenate([asked[...], asked[...]], axis=1)
    my_half = (iota(doubled.shape, 1) >> 6) == lax.rem(me, 2)
    ids_out[...] = jnp.where(my_half, doubled, 0).reshape(owners, 1, LANES)
    ids_in[me] = ids_out[me]
    cam_load.wait()
    cam_row = iota((8, LANES), 0)
    cam_tile = jnp.where(
        cam_row == 0, cam_held[0:1, 0:1], jnp.where(cam_row == 1, cam_held[0:1, 1:2], cam_held[0:1, 2:3])
    )
    cam_out[...] = cam_tile
    cam_in[my_view] = cam_tile

    pltpu.make_async_copy(held, held, load_sem.at[0]).wait()

    def features_body(at, carry):
        rows = pl.ds(pl.multiple_of(at * 16, 16), 16)

        def get(r):
            return held[r, rows, :]

        x = get(0) - cam_out[0:1]
        y = get(1) - cam_out[1:2]
        z = get(2) - cam_out[2:3]
        sigma = covariance([get(3), get(4), get(5)], [get(6), get(7), get(8), get(9)])
        values = list(geometry(x, y, z, sigma))
        values.append(-jnp.log(1.0 + jnp.exp(-get(10))))
        basis = harmonic_basis(x, y, z)
        for c in range(3):
            total = sh_zero * get(11 + 16 * c) + 0.5
            for k in range(15):
                total = total + basis[k] * get(12 + 16 * c + k)
            values.append(total)
        half = lax.div(at, 2)
        inner = lax.rem(at, 2)
        lanes = pl.ds(pl.multiple_of(half * LANES, LANES), LANES)
        for c in range(9):
            for s, piece in enumerate(pieces(values[c], 3)):
                table[s, pl.ds(pl.multiple_of(c * 32 + inner * 16, 16), 16), lanes] = piece
        return carry

    lax.fori_loop(0, blocks // 16, features_body, 0)

    pl.semaphore_wait(barrier, owners + views - 2)

    def ids_body(step, carry):
        for peer in peers(planes - 1 - step, False):
            ids_copy(peer, me).start()
        return carry

    lax.fori_loop(0, planes - 1, ids_body, 0)
    for peer in peers(0, True):
        ids_copy(peer, me).start()

    def cam_send(off, carry):
        cam_copy(lax.rem(my_view + off, views), my_view).start()
        return carry

    lax.fori_loop(1, views, cam_send, 0)

    lane_half = iota((8, LANES), 1) < CAP

    def serve(i, first):
        for peer in peers(i, first):
            ids_copy(peer, peer).wait_recv()
        base = plane(i) * LINE
        ids = jnp.concatenate(
            [ids_in[base] + ids_in[base + 1], ids_in[base + 2] + ids_in[base + 3]], axis=1
        )
        low = (ids & (LANES - 1)) + ((ids >> 12) << 7)
        high = (ids >> 7) & 31
        lanes = pl.ds(pl.multiple_of(base * CAP, LINE * CAP), LINE * CAP)
        right = (iota((256, LINE * CAP), 0) == low).astype(F32).astype(BF16)
        low_hot[:, lanes] = right
        mask = (iota((32, LINE * CAP), 0) == high).astype(F32)
        high_hot[:, lanes] = mask.astype(BF16)
        picked = dot(table[0], right, ((1,), (0,)))
        picked += dot(table[1], right, ((1,), (0,)))
        picked += dot(table[2], right, ((1,), (0,)))
        rows = [
            jnp.sum(picked[c * 32 : c * 32 + 32] * mask, axis=0, keepdims=True) for c in range(9)
        ]
        blank = jnp.zeros((1, LINE * CAP), F32)
        left_group = jnp.concatenate(rows[0:5] + [blank] * 3, axis=0)
        right_group = jnp.concatenate(rows[5:9] + [blank] * 4, axis=0)
        for part in range(2):
            a = left_group[:, part * LANES : (part + 1) * LANES]
            b = right_group[:, part * LANES : (part + 1) * LANES]
            feat_out[base + 2 * part] = jnp.where(lane_half, a, pltpu.roll(b, CAP, 1))
            feat_out[base + 2 * part + 1] = jnp.where(lane_half, pltpu.roll(a, CAP, 1), b)
        for peer in peers(i, first):
            feat_copy(peer, me).start()

    def serve_body(i, carry):
        serve(i, False)
        return carry

    serve(0, True)
    lax.fori_loop(1, planes, serve_body, 0)
    feat_in[me] = feat_out[me]

    slots_load.wait()
    len_load.wait()
    lane_row = iota((TILES, ROWS), 1)
    tile_hot = (lane_row & 15) == iota((TILES, ROWS), 0)
    tile_mask = tile_hot.astype(F32)
    entry_hot = ((iota((ENTRIES, ROWS), 1) >> 4) == iota((ENTRIES, ROWS), 0)).astype(F32).astype(BF16)
    slots = slots_held[...]
    both = jnp.concatenate([slots >> 6, slots & (CAP - 1)], axis=0).astype(F32).astype(BF16)
    spread = dot(both, entry_hot, ((1,), (0,)))
    owner_row = jnp.sum(spread[0:TILES] * tile_mask, axis=0, keepdims=True)
    place_row = jnp.sum(spread[TILES:] * tile_mask, axis=0, keepdims=True)
    lengths = jnp.broadcast_to(len_held[...], (TILES, TILES)).astype(F32).astype(BF16)
    len_row = dot(lengths, tile_mask.astype(BF16), ((1,), (0,)))[0:1]
    entry_row = iota((1, ROWS), 1)
    live = (entry_row >> 4).astype(F32) < len_row
    place_sub = iota((LANES, ROWS), 0)
    place_left = (place_sub.astype(F32) == place_row).astype(F32).astype(BF16)
    place_right = ((place_sub - CAP).astype(F32) == place_row).astype(F32).astype(BF16)
    center_of_x = (entry_row & 15).astype(F32) * 16.0 + (8.0 - 128.0)
    center_of_y = (me * 16 + 8 - 8 * owners).astype(F32)

    pixel = iota((8, PIXELS), 1)
    mono_x = (pixel & 15).astype(F32) - 7.5
    mono_y = (pixel >> 4).astype(F32) - 7.5
    kind = iota((8, PIXELS), 0)
    monomials = jnp.where(kind == 0, mono_x * mono_x, 0.0)
    monomials = jnp.where(kind == 1, mono_x * mono_y, monomials)
    monomials = jnp.where(kind == 2, mono_y * mono_y, monomials)
    monomials = jnp.where(kind == 3, mono_x, monomials)
    monomials = jnp.where(kind == 4, mono_y, monomials)
    monomials = jnp.where(kind == 5, 1.0, monomials)
    monomials_two = jnp.concatenate([monomials, jnp.zeros_like(monomials)], axis=0).astype(BF16)
    monomials_four = jnp.concatenate([monomials] * 3 + [jnp.zeros_like(monomials)], axis=0).astype(BF16)

    cot_load.wait()
    cot = jnp.concatenate(
        [held_cot[pl.ds(half, 3 * TILES, stride=2), :] for half in range(2)], axis=1
    )
    cot_high, cot_low = pieces(cot, 2)

    halves = [[jnp.zeros((8, 256), F32)] * (ROWS // 256) for _ in range(2)]

    def collect(group):
        for i in group:
            for peer in peers(i, i == 0):
                feat_copy(peer, peer).wait_recv()
        bases = [plane(i) * LINE for i in group]
        arrived = jnp.concatenate(
            [feat_in[pl.ds(base, LINE)].reshape(LINE * 8, LANES) for base in bases], axis=0
        )
        count = arrived.shape[0]
        stack = jnp.concatenate(pieces(arrived, 3), axis=0)
        for at in range(ROWS // 256):
            lanes = slice(at * 256, at * 256 + 256)
            owners_here = owner_row[:, lanes]
            for side, hot in enumerate((place_left, place_right)):
                found = dot(stack, hot[:, lanes], ((1,), (0,)))
                found = found[0:count] + found[count : 2 * count] + found[2 * count :]
                total = halves[side][at]
                for n, base in enumerate(bases):
                    for step in range(LINE):
                        row = (n * LINE + step) * 8
                        here = owners_here == (base + step).astype(F32)
                        total = jnp.where(here, found[row : row + 8], total)
                halves[side][at] = total

    near = (planes * 5 + 7) // 8
    collect(list(range(near)))
    if near < planes:
        collect(list(range(near, planes)))
    left = jnp.concatenate(halves[0], axis=1)
    right = jnp.concatenate(halves[1], axis=1)
    center_x = left[0:1] - center_of_x
    center_y = left[1:2] - center_of_y
    conic_a = left[2:3]
    conic_b = left[3:4]
    conic_c = left[4:5]
    log_opacity = right[0:1]
    colors = [right[1 + c : 2 + c] for c in range(3)]

    lin_x = conic_a * center_x + conic_b * center_y
    lin_y = conic_b * center_x + conic_c * center_y
    blank = jnp.zeros((1, ROWS), F32)
    coefs = jnp.concatenate(
        [
            jnp.where(live, -0.5 * conic_a, 0.0),
            jnp.where(live, -conic_b, 0.0),
            jnp.where(live, -0.5 * conic_c, 0.0),
            jnp.where(live, lin_x, 0.0),
            jnp.where(live, lin_y, 0.0),
            jnp.where(live, log_opacity - 0.5 * (lin_x * center_x + lin_y * center_y), -1000.0),
            blank,
            blank,
        ],
        axis=0,
    )
    coef_pieces = jnp.concatenate(
        [piece.astype(F32) for piece in pieces(coefs, 3)] + [jnp.zeros_like(coefs)], axis=0
    )
    exponent[...] = dot(coef_pieces.T.astype(BF16), monomials_four, ((1,), (0,)))

    spread_color = jnp.concatenate([colors[c] * tile_mask for c in range(3)], axis=0)
    color_high, color_low = pieces(spread_color, 2)
    color_sides = jnp.concatenate([color_high, color_high, color_low], axis=0)
    cot_sides = jnp.concatenate([cot_high, cot_low, cot_high], axis=0)
    along[...] = dot(color_sides, cot_sides, ((0,), (0,)))

    def forward_body(k, through):
        rows = pl.ds(pl.multiple_of(k * TILES, TILES), TILES)
        alpha = jnp.exp(exponent[rows, :])
        blend = through * alpha
        alpha_all[rows, :] = alpha
        blend_all[rows, :] = blend
        high, low = pieces(blend, 2)
        split_a[rows, :] = high
        split_b[rows, :] = low
        return through - blend

    lax.fori_loop(0, ENTRIES, forward_body, jnp.ones((TILES, PIXELS), F32))

    def backward_body(step, behind):
        rows = pl.ds(pl.multiple_of((ENTRIES - 1 - step) * TILES, TILES), TILES)
        gain = along[rows, :] - behind
        high, low = pieces(blend_all[rows, :] * gain, 2)
        split_c[rows, :] = high
        split_d[rows, :] = low
        return behind + alpha_all[rows, :] * gain

    lax.fori_loop(0, ENTRIES, backward_body, jnp.zeros((TILES, PIXELS), F32))

    moments = dot(monomials_two, split_c[...], ((1,), (1,))) + dot(
        monomials_two, split_d[...], ((1,), (1,))
    )
    cot_both = jnp.concatenate([cot_high, cot_low], axis=0)
    by_color = dot(cot_both, split_a[...], ((1,), (1,)))
    by_color = (
        by_color[0 : 3 * TILES]
        + by_color[3 * TILES :]
        + dot(cot_high, split_b[...], ((1,), (1,)))
    )
    grad_colors = [
        jnp.sum(by_color[c * TILES : (c + 1) * TILES] * tile_mask, axis=0, keepdims=True)
        for c in range(3)
    ]
    m_xx, m_xy, m_yy, m_x, m_y, m_one = [moments[row : row + 1] for row in range(6)]
    off_x = m_x - center_x * m_one
    off_y = m_y - center_y * m_one
    off_xx = m_xx - center_x * (m_x + off_x)
    off_xy = m_xy - center_x * m_y - center_y * off_x
    off_yy = m_yy - center_y * (m_y + off_y)
    entry_grads = jnp.concatenate(
        [
            conic_a * off_x + conic_b * off_y,
            conic_b * off_x + conic_c * off_y,
            -0.5 * off_xx,
            -off_xy,
            -0.5 * off_yy,
            blank,
            blank,
            blank,
            m_one,
            grad_colors[0],
            grad_colors[1],
            grad_colors[2],
            blank,
            blank,
            blank,
            blank,
        ],
        axis=0,
    )
    grad_high, grad_low = pieces(entry_grads, 2)

    place_both = place_left + place_right
    owner_wide = jnp.broadcast_to(owner_row, (16, ROWS)).astype(BF16)
    nothing = jnp.zeros((16, ROWS), BF16)
    lane_half_all = iota((LINE, 8, LANES), 2) < CAP

    def give(group):
        parts = []
        for piece in (grad_high, grad_low):
            for i in group:
                for step in range(LINE):
                    here = owner_wide == (plane(i) * LINE + step).astype(F32).astype(BF16)
                    parts.append(jnp.where(here, piece, nothing))
        by_slot = dot(jnp.concatenate(parts, axis=0), place_both, ((1,), (1,)))
        half_rows = 16 * LINE * len(group)
        by_slot = by_slot[0:half_rows] + by_slot[half_rows:]
        for n, i in enumerate(group):
            mine = by_slot[n * LINE * 16 : (n + 1) * LINE * 16].reshape(LINE, 16, LANES)
            packed = jnp.where(lane_half_all, mine[:, 0:8], mine[:, 8:16])
            grad_out[pl.ds(plane(i) * LINE, LINE)] = packed
        for i in group:
            for peer in peers(i, i == 0):
                grad_copy(peer, me).start()

    order = list(range(planes))[::-1]
    for at in range(0, planes, 2):
        give(order[at : at + 2])
    grad_in[me] = grad_out[me]

    color_both = jnp.concatenate([color_high, color_low], axis=0)
    shown = dot(color_both, split_a[...], ((1,), (0,)))
    shown = (
        shown[0 : 3 * TILES]
        + shown[3 * TILES :]
        + dot(color_high, split_b[...], ((1,), (0,)))
    )
    for half in range(2):
        image[pl.ds(half, 3 * TILES, stride=2), :] = shown[:, half * LANES : half * LANES + LANES]
    pltpu.make_async_copy(image, image_ref, store_sem.at[0]).start()

    wait_sent(ids_copy)
    wait_sent(feat_copy)

    def scatter(i, first):
        for peer in peers(i, first):
            grad_copy(peer, peer).wait_recv()
        base = plane(i) * LINE
        lanes = pl.ds(pl.multiple_of(base * CAP, LINE * CAP), LINE * CAP)
        tops = []
        bottoms = []
        for part in range(2):
            even = grad_in[base + 2 * part]
            odd = grad_in[base + 2 * part + 1]
            tops.append(jnp.where(lane_half, even, pltpu.roll(odd, CAP, 1)))
            bottoms.append(jnp.where(lane_half, pltpu.roll(even, CAP, 1), odd))
        a = jnp.concatenate(tops, axis=1)
        b = jnp.concatenate(bottoms, axis=1)
        mask = high_hot[:, lanes]
        for c in range(9):
            row = a[c : c + 1] if c < 5 else b[c - 5 : c - 4]
            for s, piece in enumerate(pieces(jnp.broadcast_to(row, (32, LINE * CAP)), 2)):
                wide[s * 288 + c * 32 : s * 288 + c * 32 + 32, :] = piece * mask
        placed = dot(wide[...], low_hot[:, lanes], ((1,), (1,)))
        placed = placed[0:288] + placed[288:576]
        if first:
            gathered[...] = placed
        else:
            gathered[...] += placed

    def scatter_body(i, carry):
        scatter(i, False)
        return carry

    scatter(0, True)
    lax.fori_loop(1, planes, scatter_body, 0)
    placed = gathered[...].reshape(9, 32, 256)
    dense[:, 0:32, :] = placed[:, :, 0:LANES]
    dense[:, 32:64, :] = placed[:, :, LANES:256]

    def view_send(step, carry):
        view_copy(view_peer(views - 1 - step), my_view).start()
        return carry

    lax.fori_loop(0, views - 1, view_send, 0)
    mine = pl.ds(pl.multiple_of(my_view * chunk, chunk), chunk)
    view_in[my_view] = dense[:, mine, :]

    def cam_wait(off, carry):
        peer = lax.rem(my_view + off, views)
        cam_copy(peer, peer).wait_recv()
        cam_copy(peer, my_view).wait_send()
        return carry

    lax.fori_loop(1, views, cam_wait, 0)
    wait_sent(grad_copy)
    pltpu.make_async_copy(image, image_ref, store_sem.at[0]).wait()

    def get(r):
        return held[r, mine, :]

    scale_quat = [get(r) for r in range(3, 10)]

    def shape_of(values):
        return covariance(values[0:3], values[3:7])

    sigma, shape_back = jax.vjp(shape_of, scale_quat)
    zero = jnp.zeros((chunk, LANES), F32)
    for r in range(59):
        summed[r] = zero

    def add_view(v, totals):
        camera = cam_in[v]
        x = get(0) - camera[0:1]
        y = get(1) - camera[1:2]
        z = get(2) - camera[2:3]
        grads = [view_in[v, c] for c in range(9)]
        _, geometry_back = jax.vjp(geometry, x, y, z, sigma)
        gx, gy, gz, g_sigma = geometry_back(tuple(grads[0:5]))
        basis, basis_back = jax.vjp(harmonic_basis, x, y, z)
        g_basis = [zero] * 15
        for c in range(3):
            color_grad = grads[6 + c]
            summed[11 + 16 * c] += sh_zero * color_grad
            for k in range(15):
                row = 12 + 16 * c + k
                summed[row] += basis[k] * color_grad
                g_basis[k] = g_basis[k] + get(row) * color_grad
        hx, hy, hz = basis_back(g_basis)
        add = [gx + hx, gy + hy, gz + hz, grads[5]] + list(g_sigma)
        return tuple(t + a for t, a in zip(totals, add))

    def view_body(i, totals):
        peer = view_peer(i)
        view_copy(peer, peer).wait_recv()
        return add_view(peer, totals)

    totals = add_view(my_view, tuple([zero] * 10))
    totals = lax.fori_loop(1, views, view_body, totals)
    for r in range(3):
        summed[r] = totals[r]
    (by_shape,) = shape_back(list(totals[4:10]))
    for r in range(7):
        summed[3 + r] = by_shape[r]
    summed[10] = totals[3] / (1.0 + jnp.exp(get(10)))

    def store_grads(j):
        return pltpu.make_async_copy(
            summed.at[:, j, :],
            grads_ref.at[:, pl.ds(pl.multiple_of(j * LANES, LANES), LANES)],
            store_sem.at[1],
        )

    def store_grads_body(j, carry):
        store_grads(j).start()
        return carry

    lax.fori_loop(0, chunk, store_grads_body, 0)

    def view_wait(off, carry):
        view_copy(lax.rem(my_view + off, views), my_view).wait_send()
        return carry

    lax.fori_loop(1, views, view_wait, 0)
    pltpu.make_async_copy(summed, summed, store_sem.at[1]).wait()


def local(owners, views, params, cam_pos, req_ids, tile_slots, tile_len, cotangent):
    count, owned = params.shape
    blocks = owned // LANES
    chunk = blocks // views
    slots_all = owners * CAP
    vmem = pltpu.VMEM
    dma = pltpu.SemaphoreType.DMA
    anywhere = pl.BlockSpec(memory_space=pl.ANY)
    image, grads = pl.pallas_call(
        functools.partial(kernel, owners, views),
        out_shape=(
            jax.ShapeDtypeStruct((6 * TILES, LANES), F32),
            jax.ShapeDtypeStruct((count, owned // views), F32),
        ),
        in_specs=[anywhere] * 6,
        out_specs=(anywhere, anywhere),
        scratch_shapes=[
            vmem((count, blocks, LANES), F32),
            vmem((owners, CAP), jnp.int32),
            vmem((1, 3), F32),
            vmem((TILES, ENTRIES), jnp.int32),
            vmem((1, TILES), jnp.int32),
            vmem((6 * TILES, LANES), F32),
            vmem((6 * TILES, LANES), F32),
            vmem((count, chunk, LANES), F32),
            vmem((owners, 1, LANES), jnp.int32),
            vmem((owners, 1, LANES), jnp.int32),
            vmem((8, LANES), F32),
            vmem((views, 8, LANES), F32),
            vmem((3, 288, 256), BF16),
            vmem((256, slots_all), BF16),
            vmem((32, slots_all), BF16),
            vmem((owners, 8, LANES), F32),
            vmem((owners, 8, LANES), F32),
            vmem((576, LINE * CAP), BF16),
            vmem((288, 256), F32),
            vmem((ROWS, PIXELS), F32),
            vmem((ROWS, PIXELS), F32),
            vmem((ROWS, PIXELS), F32),
            vmem((ROWS, PIXELS), F32),
            vmem((ROWS, PIXELS), BF16),
            vmem((ROWS, PIXELS), BF16),
            vmem((ROWS, PIXELS), BF16),
            vmem((ROWS, PIXELS), BF16),
            vmem((owners, 8, LANES), F32),
            vmem((owners, 8, LANES), F32),
            vmem((9, blocks, LANES), F32),
            vmem((views, 9, chunk, LANES), F32),
            dma((6,)),
            dma((2,)),
        ]
        + [dma((owners,)) for _ in range(6)]
        + [dma((views,)) for _ in range(4)],
        compiler_params=pltpu.CompilerParams(
            collective_id=0, has_side_effects=True, vmem_limit_bytes=60 * 1024 * 1024
        ),
        cost_estimate=pl.CostEstimate(
            flops=2_000_000_000, bytes_accessed=4_000_000, transcendentals=300_000
        ),
    )(
        params,
        cam_pos,
        req_ids,
        tile_slots,
        tile_len,
        cotangent.reshape(6 * TILES, LANES),
    )
    return image.reshape(cotangent.shape), grads


def solution(mesh):
    placed = (
        P(None, "gs"),
        P("view", None),
        P("view", "gs", None, None),
        P("view", "gs", None),
        P("view", "gs"),
        P("view", None, "gs"),
    )
    return jax.shard_map(
        functools.partial(local, mesh.shape["gs"], mesh.shape["view"]),
        mesh=mesh,
        in_specs=placed,
        out_specs=(P("view", None, "gs"), P(None, ("gs", "view"))),
        check_vma=False,
    )
```

```python
import functools

import jax
import jax.numpy as jnp
from jax import lax
from jax.experimental import pallas as pl
from jax.experimental.pallas import tpu as pltpu
from jax.sharding import PartitionSpec as P

MESH = pl.DeviceIdType.MESH
F32 = jnp.float32
BF16 = jnp.bfloat16
TILES = 16
ENTRIES = 64
ROWS = TILES * ENTRIES
PIXELS = 256
CAP = 64
LANES = 128
LINE = 4

focal = 1.2 * 128.0
dilate = 0.3
sh_zero = 0.28209479177387814
sh_one = 0.4886025119029199
sh_two = [
    1.0925484305920792,
    -1.0925484305920792,
    0.31539156525252005,
    -1.0925484305920792,
    0.5462742152960396,
]
sh_three = [
    -0.5900435899266435,
    2.890611442640554,
    -0.4570457994644658,
    0.3731763325901154,
    -0.4570457994644658,
    1.445305721320277,
    -0.5900435899266435,
]


def covariance(log_scales, quat):
    squares = [jnp.exp(2.0 * value) for value in log_scales]
    norm_sq = quat[0] * quat[0] + quat[1] * quat[1] + quat[2] * quat[2] + quat[3] * quat[3]
    inv_norm = 1.0 / jnp.sqrt(norm_sq)
    w, x, y, z = [value * inv_norm for value in quat]
    rotation = [
        [1 - 2 * (y * y + z * z), 2 * (x * y - w * z), 2 * (x * z + w * y)],
        [2 * (x * y + w * z), 1 - 2 * (x * x + z * z), 2 * (y * z - w * x)],
        [2 * (x * z - w * y), 2 * (y * z + w * x), 1 - 2 * (x * x + y * y)],
    ]
    scaled = [[rotation[i][j] * squares[j] for j in range(3)] for i in range(3)]

    def entry(i, j):
        return (
            scaled[i][0] * rotation[j][0]
            + scaled[i][1] * rotation[j][1]
            + scaled[i][2] * rotation[j][2]
        )

    return [entry(0, 0), entry(0, 1), entry(0, 2), entry(1, 1), entry(1, 2), entry(2, 2)]


def geometry(x, y, z, sigma):
    s00, s01, s02, s11, s12, s22 = sigma
    inv_z = 1.0 / z
    jac = focal * inv_z
    center_x = jac * x
    center_y = jac * y
    jac_x = -center_x * inv_z
    jac_y = -center_y * inv_z
    jac_sq = jac * jac
    cov_a = jac_sq * s00 + 2.0 * (jac * jac_x) * s02 + jac_x * jac_x * s22 + dilate
    cov_b = jac_sq * s01 + jac * (jac_y * s02 + jac_x * s12) + jac_x * jac_y * s22
    cov_c = jac_sq * s11 + 2.0 * (jac * jac_y) * s12 + jac_y * jac_y * s22 + dilate
    inv_det = 1.0 / (cov_a * cov_c - cov_b * cov_b)
    return center_x, center_y, cov_c * inv_det, -cov_b * inv_det, cov_a * inv_det


def harmonic_basis(x, y, z):
    inv_distance = 1.0 / jnp.sqrt(x * x + y * y + z * z)
    dx = x * inv_distance
    dy = y * inv_distance
    dz = z * inv_distance
    xx = dx * dx
    yy = dy * dy
    zz = dz * dz
    xy = dx * dy
    yz = dy * dz
    xz = dx * dz
    return [
        -sh_one * dy,
        sh_one * dz,
        -sh_one * dx,
        sh_two[0] * xy,
        sh_two[1] * yz,
        sh_two[2] * (2 * zz - xx - yy),
        sh_two[3] * xz,
        sh_two[4] * (xx - yy),
        sh_three[0] * dy * (3 * xx - yy),
        sh_three[1] * xy * dz,
        sh_three[2] * dy * (4 * zz - xx - yy),
        sh_three[3] * dz * (2 * zz - 3 * xx - 3 * yy),
        sh_three[4] * dx * (4 * zz - xx - yy),
        sh_three[5] * dz * (xx - yy),
        sh_three[6] * dx * (xx - 3 * yy),
    ]


def pieces(value, count):
    out = []
    for at in range(count):
        piece = value.astype(BF16)
        out.append(piece)
        if at + 1 < count:
            value = value - piece.astype(F32)
    return out


def dot(left, right, dims):
    return lax.dot_general(left, right, ((dims[0], dims[1]), ((), ())), preferred_element_type=F32)


def iota(shape, axis):
    return lax.broadcasted_iota(jnp.int32, shape, axis)


def kernel(
    owners,
    views,
    params_ref,
    cam_ref,
    ids_ref,
    slots_ref,
    len_ref,
    cot_ref,
    image_ref,
    grads_ref,
    held,
    asked,
    cam_held,
    slots_held,
    len_held,
    held_cot,
    image,
    summed,
    ids_out,
    ids_in,
    cam_out,
    cam_in,
    table,
    low_hot,
    high_hot,
    feat_out,
    feat_in,
    wide,
    gathered,
    exponent,
    along,
    alpha_all,
    blend_all,
    split_a,
    split_b,
    split_c,
    split_d,
    grad_out,
    grad_in,
    dense,
    view_in,
    load_sem,
    store_sem,
    ids_s,
    ids_r,
    feat_s,
    feat_r,
    grad_s,
    grad_r,
    cam_s,
    cam_r,
    view_s,
    view_r,
):
    me = lax.axis_index("gs")
    my_view = lax.axis_index("view")
    my_y = lax.rem(me, LINE)
    my_z = lax.div(me, LINE)
    my_x = lax.div(my_view, 2)
    my_core = lax.rem(my_view, 2)
    planes = owners // LINE
    blocks = held.shape[1]
    chunk = blocks // views

    def plane(i):
        half = (i + 1) // 2
        odd = i % 2
        return lax.rem(my_z + odd * half + (1 - odd) * (planes - half), planes)

    def peers(i, first):
        return [plane(i) * LINE + lax.rem(my_y + step, LINE) for step in range(1 if first else 0, LINE)]

    def view_peer(i):
        pair = i // 2
        step = pair + pair // 2 - 2 * (pair // 3)
        return lax.rem(my_x + step, views // 2) * 2 + lax.rem(my_core + i, 2)

    ids_load = pltpu.make_async_copy(ids_ref.at[0, 0], asked, load_sem.at[2])
    cam_load = pltpu.make_async_copy(cam_ref, cam_held, load_sem.at[3])
    slots_load = pltpu.make_async_copy(slots_ref.at[0], slots_held, load_sem.at[4])
    len_load = pltpu.make_async_copy(len_ref, len_held, load_sem.at[5])
    cot_load = pltpu.make_async_copy(cot_ref, held_cot, load_sem.at[1])
    ids_load.start()
    cam_load.start()

    barrier = pltpu.get_barrier_semaphore()

    def greet(off, carry):
        peer = lax.rem(me + off, owners)
        pl.semaphore_signal(barrier, inc=1, device_id=(my_view, peer), device_id_type=MESH)
        return carry

    lax.fori_loop(1, owners, greet, 0)

    def greet_view(off, carry):
        peer = lax.rem(my_view + off, views)
        pl.semaphore_signal(barrier, inc=1, device_id=(peer, me), device_id_type=MESH)
        return carry

    lax.fori_loop(1, views, greet_view, 0)

    def load_body(j, carry):
        pltpu.make_async_copy(
            params_ref.at[:, pl.ds(pl.multiple_of(j * LANES, LANES), LANES)],
            held.at[:, j, :],
            load_sem.at[0],
        ).start()
        return carry

    lax.fori_loop(0, blocks, load_body, 0)
    slots_load.start()
    len_load.start()
    cot_load.start()

    def ids_copy(to, sender):
        return pltpu.make_async_remote_copy(
            src_ref=ids_out.at[to],
            dst_ref=ids_in.at[sender],
            send_sem=ids_s.at[to],
            recv_sem=ids_r.at[sender],
            device_id=(my_view, to),
            device_id_type=MESH,
        )

    def feat_copy(to, sender):
        return pltpu.make_async_remote_copy(
            src_ref=feat_out.at[to, pl.ds(0, 5)],
            dst_ref=feat_in.at[sender, pl.ds(0, 5)],
            send_sem=feat_s.at[to],
            recv_sem=feat_r.at[sender],
            device_id=(my_view, to),
            device_id_type=MESH,
        )

    def grad_copy(to, sender):
        return pltpu.make_async_remote_copy(
            src_ref=grad_out.at[to, pl.ds(0, 5)],
            dst_ref=grad_in.at[sender, pl.ds(0, 5)],
            send_sem=grad_s.at[to],
            recv_sem=grad_r.at[sender],
            device_id=(my_view, to),
            device_id_type=MESH,
        )

    def cam_copy(to, sender):
        return pltpu.make_async_remote_copy(
            src_ref=cam_out,
            dst_ref=cam_in.at[sender],
            send_sem=cam_s.at[to],
            recv_sem=cam_r.at[sender],
            device_id=(to, me),
            device_id_type=MESH,
        )

    def view_copy(to, sender):
        return pltpu.make_async_remote_copy(
            src_ref=dense.at[:, pl.ds(pl.multiple_of(to * chunk, chunk), chunk), :],
            dst_ref=view_in.at[sender],
            send_sem=view_s.at[to],
            recv_sem=view_r.at[sender],
            device_id=(to, me),
            device_id_type=MESH,
        )

    def wait_sent(copy):
        def body(off, carry):
            copy(lax.rem(me + off, owners), me).wait_send()
            return carry

        lax.fori_loop(1, owners, body, 0)

    ids_load.wait()
    doubled = jnp.concatenate([asked[...], asked[...]], axis=1)
    my_half = (iota(doubled.shape, 1) >> 6) == lax.rem(me, 2)
    ids_out[...] = jnp.where(my_half, doubled, 0).reshape(owners, 1, LANES)
    ids_in[me] = ids_out[me]
    cam_load.wait()
    cam_row = iota((8, LANES), 0)
    cam_tile = jnp.where(
        cam_row == 0, cam_held[0:1, 0:1], jnp.where(cam_row == 1, cam_held[0:1, 1:2], cam_held[0:1, 2:3])
    )
    cam_out[...] = cam_tile
    cam_in[my_view] = cam_tile

    pl.semaphore_wait(barrier, owners + views - 2)

    def ids_body(step, carry):
        for peer in peers(planes - 1 - step, False):
            ids_copy(peer, me).start()
        return carry

    lax.fori_loop(0, planes - 1, ids_body, 0)
    for peer in peers(0, True):
        ids_copy(peer, me).start()

    def cam_send(off, carry):
        cam_copy(lax.rem(my_view + off, views), my_view).start()
        return carry

    lax.fori_loop(1, views, cam_send, 0)

    pltpu.make_async_copy(held, held, load_sem.at[0]).wait()

    def features_body(at, carry):
        rows = pl.ds(pl.multiple_of(at * 16, 16), 16)

        def get(r):
            return held[r, rows, :]

        x = get(0) - cam_out[0:1]
        y = get(1) - cam_out[1:2]
        z = get(2) - cam_out[2:3]
        sigma = covariance([get(3), get(4), get(5)], [get(6), get(7), get(8), get(9)])
        values = list(geometry(x, y, z, sigma))
        values.append(-jnp.log(1.0 + jnp.exp(-get(10))))
        basis = harmonic_basis(x, y, z)
        for c in range(3):
            total = sh_zero * get(11 + 16 * c) + 0.5
            for k in range(15):
                total = total + basis[k] * get(12 + 16 * c + k)
            values.append(total)
        half = lax.div(at, 2)
        inner = lax.rem(at, 2)
        lanes = pl.ds(pl.multiple_of(half * LANES, LANES), LANES)
        for c in range(9):
            for s, piece in enumerate(pieces(values[c], 3)):
                table[s, pl.ds(pl.multiple_of(c * 32 + inner * 16, 16), 16), lanes] = piece
        return carry

    lax.fori_loop(0, blocks // 16, features_body, 0)

    lane_half = iota((8, LANES), 1) < CAP

    def serve(i, first):
        for peer in peers(i, first):
            ids_copy(peer, peer).wait_recv()
        base = plane(i) * LINE
        ids = jnp.concatenate(
            [ids_in[base] + ids_in[base + 1], ids_in[base + 2] + ids_in[base + 3]], axis=1
        )
        low = (ids & (LANES - 1)) + ((ids >> 12) << 7)
        high = (ids >> 7) & 31
        lanes = pl.ds(pl.multiple_of(base * CAP, LINE * CAP), LINE * CAP)
        right = (iota((256, LINE * CAP), 0) == low).astype(F32).astype(BF16)
        low_hot[:, lanes] = right
        mask = (iota((32, LINE * CAP), 0) == high).astype(F32)
        high_hot[:, lanes] = mask.astype(BF16)
        picked = dot(table[0], right, ((1,), (0,)))
        picked += dot(table[1], right, ((1,), (0,)))
        rest = dot(table[2, 0:160], right, ((1,), (0,)))
        picked = jnp.concatenate([picked[0:160] + rest, picked[160:]], axis=0)
        rows = [
            jnp.sum(picked[c * 32 : c * 32 + 32] * mask, axis=0, keepdims=True) for c in range(9)
        ]
        blank = jnp.zeros((1, LINE * CAP), F32)
        left_group = jnp.concatenate(rows[0:5] + [blank] * 3, axis=0)
        right_group = jnp.concatenate(rows[5:9] + [blank] * 4, axis=0)
        for part in range(2):
            a = left_group[:, part * LANES : (part + 1) * LANES]
            b = right_group[:, part * LANES : (part + 1) * LANES]
            feat_out[base + 2 * part] = jnp.where(lane_half, a, pltpu.roll(b, CAP, 1))
            feat_out[base + 2 * part + 1] = jnp.where(lane_half, pltpu.roll(a, CAP, 1), b)
        for peer in peers(i, first):
            feat_copy(peer, me).start()

    def serve_body(i, carry):
        serve(i, False)
        return carry

    serve(0, True)
    lax.fori_loop(1, planes, serve_body, 0)
    feat_in[me] = feat_out[me]

    slots_load.wait()
    len_load.wait()
    lane_row = iota((TILES, ROWS), 1)
    tile_hot = (lane_row & 15) == iota((TILES, ROWS), 0)
    tile_mask = tile_hot.astype(F32)
    entry_hot = ((iota((ENTRIES, ROWS), 1) >> 4) == iota((ENTRIES, ROWS), 0)).astype(F32).astype(BF16)
    slots = slots_held[...]
    both = jnp.concatenate([slots >> 6, slots & (CAP - 1)], axis=0).astype(F32).astype(BF16)
    spread = dot(both, entry_hot, ((1,), (0,)))
    owner_row = jnp.sum(spread[0:TILES] * tile_mask, axis=0, keepdims=True)
    place_row = jnp.sum(spread[TILES:] * tile_mask, axis=0, keepdims=True)
    lengths = jnp.broadcast_to(len_held[...], (TILES, TILES)).astype(F32).astype(BF16)
    len_row = dot(lengths, tile_mask.astype(BF16), ((1,), (0,)))[0:1]
    entry_row = iota((1, ROWS), 1)
    live = (entry_row >> 4).astype(F32) < len_row
    place_sub = iota((LANES, ROWS), 0)
    place_left = (place_sub.astype(F32) == place_row).astype(F32).astype(BF16)
    place_right = ((place_sub - CAP).astype(F32) == place_row).astype(F32).astype(BF16)
    center_of_x = (entry_row & 15).astype(F32) * 16.0 + (8.0 - 128.0)
    center_of_y = (me * 16 + 8 - 8 * owners).astype(F32)

    pixel = iota((8, PIXELS), 1)
    mono_x = (pixel & 15).astype(F32) - 7.5
    mono_y = (pixel >> 4).astype(F32) - 7.5
    kind = iota((8, PIXELS), 0)
    monomials = jnp.where(kind == 0, mono_x * mono_x, 0.0)
    monomials = jnp.where(kind == 1, mono_x * mono_y, monomials)
    monomials = jnp.where(kind == 2, mono_y * mono_y, monomials)
    monomials = jnp.where(kind == 3, mono_x, monomials)
    monomials = jnp.where(kind == 4, mono_y, monomials)
    monomials = jnp.where(kind == 5, 1.0, monomials)
    monomials_two = jnp.concatenate([monomials, jnp.zeros_like(monomials)], axis=0).astype(BF16)
    monomials_four = jnp.concatenate([monomials] * 3 + [jnp.zeros_like(monomials)], axis=0).astype(BF16)

    cot_load.wait()
    cot = jnp.concatenate(
        [held_cot[pl.ds(half, 3 * TILES, stride=2), :] for half in range(2)], axis=1
    )
    cot_high, cot_low = pieces(cot, 2)

    halves = [[jnp.zeros((8, 256), F32)] * (ROWS // 256) for _ in range(2)]

    def collect(group):
        for i in group:
            for peer in peers(i, i == 0):
                feat_copy(peer, peer).wait_recv()
        bases = [plane(i) * LINE for i in group]
        arrived = jnp.concatenate(
            [feat_in[pl.ds(base, LINE)].reshape(LINE * 8, LANES) for base in bases], axis=0
        )
        count = arrived.shape[0]
        three = pieces(arrived, 3)
        stacks = [jnp.concatenate(three, axis=0), jnp.concatenate(three[0:2], axis=0)]
        for at in range(ROWS // 256):
            lanes = slice(at * 256, at * 256 + 256)
            owners_here = owner_row[:, lanes]
            for side, hot in enumerate((place_left, place_right)):
                found = dot(stacks[side], hot[:, lanes], ((1,), (0,)))
                summed_pieces = found[0:count] + found[count : 2 * count]
                found = summed_pieces + found[2 * count :] if side == 0 else summed_pieces
                total = halves[side][at]
                for n, base in enumerate(bases):
                    for step in range(LINE):
                        row = (n * LINE + step) * 8
                        here = owners_here == (base + step).astype(F32)
                        total = jnp.where(here, found[row : row + 8], total)
                halves[side][at] = total

    near = (planes * 5 + 7) // 8
    collect(list(range(near)))
    if near < planes:
        collect(list(range(near, planes)))
    left = jnp.concatenate(halves[0], axis=1)
    right = jnp.concatenate(halves[1], axis=1)
    center_x = left[0:1] - center_of_x
    center_y = left[1:2] - center_of_y
    conic_a = left[2:3]
    conic_b = left[3:4]
    conic_c = left[4:5]
    log_opacity = right[0:1]
    colors = [right[1 + c : 2 + c] for c in range(3)]

    lin_x = conic_a * center_x + conic_b * center_y
    lin_y = conic_b * center_x + conic_c * center_y
    blank = jnp.zeros((1, ROWS), F32)
    coefs = jnp.concatenate(
        [
            jnp.where(live, -0.5 * conic_a, 0.0),
            jnp.where(live, -conic_b, 0.0),
            jnp.where(live, -0.5 * conic_c, 0.0),
            jnp.where(live, lin_x, 0.0),
            jnp.where(live, lin_y, 0.0),
            jnp.where(live, log_opacity - 0.5 * (lin_x * center_x + lin_y * center_y), -1000.0),
            blank,
            blank,
        ],
        axis=0,
    )
    coef_pieces = jnp.concatenate(
        [piece.astype(F32) for piece in pieces(coefs, 3)] + [jnp.zeros_like(coefs)], axis=0
    )
    exponent[...] = dot(coef_pieces.T.astype(BF16), monomials_four, ((1,), (0,)))

    spread_color = jnp.concatenate([colors[c] * tile_mask for c in range(3)], axis=0)
    color_high, color_low = pieces(spread_color, 2)
    color_sides = jnp.concatenate([color_high, color_high, color_low], axis=0)
    cot_sides = jnp.concatenate([cot_high, cot_low, cot_high], axis=0)
    along[...] = dot(color_sides, cot_sides, ((0,), (0,)))

    def forward_body(k, through):
        rows = pl.ds(pl.multiple_of(k * TILES, TILES), TILES)
        alpha = jnp.exp(exponent[rows, :])
        blend = through * alpha
        alpha_all[rows, :] = alpha
        blend_all[rows, :] = blend
        high, low = pieces(blend, 2)
        split_a[rows, :] = high
        split_b[rows, :] = low
        return through - blend

    lax.fori_loop(0, ENTRIES, forward_body, jnp.ones((TILES, PIXELS), F32))

    def backward_body(step, behind):
        rows = pl.ds(pl.multiple_of((ENTRIES - 1 - step) * TILES, TILES), TILES)
        gain = along[rows, :] - behind
        high, low = pieces(blend_all[rows, :] * gain, 2)
        split_c[rows, :] = high
        split_d[rows, :] = low
        return behind + alpha_all[rows, :] * gain

    lax.fori_loop(0, ENTRIES, backward_body, jnp.zeros((TILES, PIXELS), F32))

    moments = dot(monomials_two, split_c[...], ((1,), (1,))) + dot(
        monomials_two, split_d[...], ((1,), (1,))
    )
    cot_both = jnp.concatenate([cot_high, cot_low], axis=0)
    by_color = dot(cot_both, split_a[...], ((1,), (1,)))
    by_color = (
        by_color[0 : 3 * TILES]
        + by_color[3 * TILES :]
        + dot(cot_high, split_b[...], ((1,), (1,)))
    )
    grad_colors = [
        jnp.sum(by_color[c * TILES : (c + 1) * TILES] * tile_mask, axis=0, keepdims=True)
        for c in range(3)
    ]
    m_xx, m_xy, m_yy, m_x, m_y, m_one = [moments[row : row + 1] for row in range(6)]
    off_x = m_x - center_x * m_one
    off_y = m_y - center_y * m_one
    off_xx = m_xx - center_x * (m_x + off_x)
    off_xy = m_xy - center_x * m_y - center_y * off_x
    off_yy = m_yy - center_y * (m_y + off_y)
    entry_grads = jnp.concatenate(
        [
            conic_a * off_x + conic_b * off_y,
            conic_b * off_x + conic_c * off_y,
            -0.5 * off_xx,
            -off_xy,
            -0.5 * off_yy,
            blank,
            blank,
            blank,
            m_one,
            grad_colors[0],
            grad_colors[1],
            grad_colors[2],
            blank,
            blank,
            blank,
            blank,
        ],
        axis=0,
    )
    grad_high, grad_low = pieces(entry_grads, 2)

    place_both = place_left + place_right
    owner_wide = jnp.broadcast_to(owner_row, (16, ROWS)).astype(BF16)
    nothing = jnp.zeros((16, ROWS), BF16)
    lane_half_all = iota((LINE, 8, LANES), 2) < CAP

    def give(group):
        parts = []
        for piece in (grad_high, grad_low):
            for i in group:
                for step in range(LINE):
                    here = owner_wide == (plane(i) * LINE + step).astype(F32).astype(BF16)
                    parts.append(jnp.where(here, piece, nothing))
        by_slot = dot(jnp.concatenate(parts, axis=0), place_both, ((1,), (1,)))
        half_rows = 16 * LINE * len(group)
        by_slot = by_slot[0:half_rows] + by_slot[half_rows:]
        for n, i in enumerate(group):
            mine = by_slot[n * LINE * 16 : (n + 1) * LINE * 16].reshape(LINE, 16, LANES)
            packed = jnp.where(lane_half_all, mine[:, 0:8], mine[:, 8:16])
            grad_out[pl.ds(plane(i) * LINE, LINE)] = packed
        for i in group:
            for peer in peers(i, i == 0):
                grad_copy(peer, me).start()

    order = list(range(planes))[::-1]
    for at in range(0, planes, 2):
        give(order[at : at + 2])
    grad_in[me] = grad_out[me]

    color_both = jnp.concatenate([color_high, color_low], axis=0)
    shown = dot(color_both, split_a[...], ((1,), (0,)))
    shown = (
        shown[0 : 3 * TILES]
        + shown[3 * TILES :]
        + dot(color_high, split_b[...], ((1,), (0,)))
    )
    for half in range(2):
        image[pl.ds(half, 3 * TILES, stride=2), :] = shown[:, half * LANES : half * LANES + LANES]
    pltpu.make_async_copy(image, image_ref, store_sem.at[0]).start()

    wait_sent(ids_copy)
    wait_sent(feat_copy)

    def scatter(i, first):
        for peer in peers(i, first):
            grad_copy(peer, peer).wait_recv()
        base = plane(i) * LINE
        lanes = pl.ds(pl.multiple_of(base * CAP, LINE * CAP), LINE * CAP)
        tops = []
        bottoms = []
        for part in range(2):
            even = grad_in[base + 2 * part]
            odd = grad_in[base + 2 * part + 1]
            tops.append(jnp.where(lane_half, even, pltpu.roll(odd, CAP, 1)))
            bottoms.append(jnp.where(lane_half, pltpu.roll(even, CAP, 1), odd))
        a = jnp.concatenate(tops, axis=1)
        b = jnp.concatenate(bottoms, axis=1)
        mask = high_hot[:, lanes]
        for c in range(9):
            row = a[c : c + 1] if c < 5 else b[c - 5 : c - 4]
            for s, piece in enumerate(pieces(jnp.broadcast_to(row, (32, LINE * CAP)), 2)):
                wide[s * 288 + c * 32 : s * 288 + c * 32 + 32, :] = piece * mask
        placed = dot(wide[...], low_hot[:, lanes], ((1,), (1,)))
        placed = placed[0:288] + placed[288:576]
        if first:
            gathered[...] = placed
        else:
            gathered[...] += placed

    def scatter_body(i, carry):
        scatter(i, False)
        return carry

    scatter(0, True)
    lax.fori_loop(1, planes, scatter_body, 0)
    placed = gathered[...].reshape(9, 32, 256)
    dense[:, 0:32, :] = placed[:, :, 0:LANES]
    dense[:, 32:64, :] = placed[:, :, LANES:256]

    def view_send(step, carry):
        view_copy(view_peer(views - 1 - step), my_view).start()
        return carry

    lax.fori_loop(0, views - 1, view_send, 0)
    mine = pl.ds(pl.multiple_of(my_view * chunk, chunk), chunk)
    view_in[my_view] = dense[:, mine, :]

    def cam_wait(off, carry):
        peer = lax.rem(my_view + off, views)
        cam_copy(peer, peer).wait_recv()
        cam_copy(peer, my_view).wait_send()
        return carry

    lax.fori_loop(1, views, cam_wait, 0)
    wait_sent(grad_copy)
    pltpu.make_async_copy(image, image_ref, store_sem.at[0]).wait()

    def get(r):
        return held[r, mine, :]

    scale_quat = [get(r) for r in range(3, 10)]

    def shape_of(values):
        return covariance(values[0:3], values[3:7])

    sigma, shape_back = jax.vjp(shape_of, scale_quat)
    zero = jnp.zeros((chunk, LANES), F32)
    for r in range(59):
        summed[r] = zero

    def add_view(v, totals):
        camera = cam_in[v]
        x = get(0) - camera[0:1]
        y = get(1) - camera[1:2]
        z = get(2) - camera[2:3]
        grads = [view_in[v, c] for c in range(9)]
        _, geometry_back = jax.vjp(geometry, x, y, z, sigma)
        gx, gy, gz, g_sigma = geometry_back(tuple(grads[0:5]))
        basis, basis_back = jax.vjp(harmonic_basis, x, y, z)
        g_basis = [zero] * 15
        for c in range(3):
            color_grad = grads[6 + c]
            summed[11 + 16 * c] += sh_zero * color_grad
            for k in range(15):
                row = 12 + 16 * c + k
                summed[row] += basis[k] * color_grad
                g_basis[k] = g_basis[k] + get(row) * color_grad
        hx, hy, hz = basis_back(g_basis)
        add = [gx + hx, gy + hy, gz + hz, grads[5]] + list(g_sigma)
        return tuple(t + a for t, a in zip(totals, add))

    def view_body(i, totals):
        peer = view_peer(i)
        view_copy(peer, peer).wait_recv()
        return add_view(peer, totals)

    totals = add_view(my_view, tuple([zero] * 10))
    totals = lax.fori_loop(1, views, view_body, totals)
    for r in range(3):
        summed[r] = totals[r]
    (by_shape,) = shape_back(list(totals[4:10]))
    for r in range(7):
        summed[3 + r] = by_shape[r]
    summed[10] = totals[3] / (1.0 + jnp.exp(get(10)))

    def store_grads(j):
        return pltpu.make_async_copy(
            summed.at[:, j, :],
            grads_ref.at[:, pl.ds(pl.multiple_of(j * LANES, LANES), LANES)],
            store_sem.at[1],
        )

    def store_grads_body(j, carry):
        store_grads(j).start()
        return carry

    lax.fori_loop(0, chunk, store_grads_body, 0)

    def view_wait(off, carry):
        view_copy(lax.rem(my_view + off, views), my_view).wait_send()
        return carry

    lax.fori_loop(1, views, view_wait, 0)
    pltpu.make_async_copy(summed, summed, store_sem.at[1]).wait()


def local(owners, views, params, cam_pos, req_ids, tile_slots, tile_len, cotangent):
    count, owned = params.shape
    blocks = owned // LANES
    chunk = blocks // views
    slots_all = owners * CAP
    vmem = pltpu.VMEM
    dma = pltpu.SemaphoreType.DMA
    anywhere = pl.BlockSpec(memory_space=pl.ANY)
    image, grads = pl.pallas_call(
        functools.partial(kernel, owners, views),
        out_shape=(
            vmem((6 * TILES, LANES), F32),
            vmem((count, owned // views), F32),
        ),
        in_specs=[anywhere] * 6,
        out_specs=(anywhere, anywhere),
        scratch_shapes=[
            vmem((count, blocks, LANES), F32),
            vmem((owners, CAP), jnp.int32),
            vmem((1, 3), F32),
            vmem((TILES, ENTRIES), jnp.int32),
            vmem((1, TILES), jnp.int32),
            vmem((6 * TILES, LANES), F32),
            vmem((6 * TILES, LANES), F32),
            vmem((count, chunk, LANES), F32),
            vmem((owners, 1, LANES), jnp.int32),
            vmem((owners, 1, LANES), jnp.int32),
            vmem((8, LANES), F32),
            vmem((views, 8, LANES), F32),
            vmem((3, 288, 256), BF16),
            vmem((256, slots_all), BF16),
            vmem((32, slots_all), BF16),
            vmem((owners, 8, LANES), F32),
            vmem((owners, 8, LANES), F32),
            vmem((576, LINE * CAP), BF16),
            vmem((288, 256), F32),
            vmem((ROWS, PIXELS), F32),
            vmem((ROWS, PIXELS), F32),
            vmem((ROWS, PIXELS), F32),
            vmem((ROWS, PIXELS), F32),
            vmem((ROWS, PIXELS), BF16),
            vmem((ROWS, PIXELS), BF16),
            vmem((ROWS, PIXELS), BF16),
            vmem((ROWS, PIXELS), BF16),
            vmem((owners, 8, LANES), F32),
            vmem((owners, 8, LANES), F32),
            vmem((9, blocks, LANES), F32),
            vmem((views, 9, chunk, LANES), F32),
            dma((6,)),
            dma((2,)),
        ]
        + [dma((owners,)) for _ in range(6)]
        + [dma((views,)) for _ in range(4)],
        compiler_params=pltpu.CompilerParams(
            collective_id=0, has_side_effects=True, vmem_limit_bytes=60 * 1024 * 1024
        ),
        cost_estimate=pl.CostEstimate(
            flops=2_000_000_000, bytes_accessed=4_000_000, transcendentals=300_000
        ),
    )(
        params,
        cam_pos,
        req_ids,
        tile_slots,
        tile_len,
        cotangent.reshape(6 * TILES, LANES),
    )
    return image.reshape(cotangent.shape), grads


def solution(mesh):
    placed = (
        P(None, "gs"),
        P("view", None),
        P("view", "gs", None, None),
        P("view", "gs", None),
        P("view", "gs"),
        P("view", None, "gs"),
    )
    return jax.shard_map(
        functools.partial(local, mesh.shape["gs"], mesh.shape["view"]),
        mesh=mesh,
        in_specs=placed,
        out_specs=(P("view", None, "gs"), P(None, ("gs", "view"))),
        check_vma=False,
    )
```

```python
import functools

import jax
import jax.numpy as jnp
from jax import lax
from jax.experimental import pallas as pl
from jax.experimental.pallas import tpu as pltpu
from jax.sharding import PartitionSpec as P

MESH = pl.DeviceIdType.MESH
F32 = jnp.float32
BF16 = jnp.bfloat16
TILES = 16
ENTRIES = 64
ROWS = TILES * ENTRIES
PIXELS = 256
CAP = 64
LANES = 128
LINE = 4

focal = 1.2 * 128.0
dilate = 0.3
sh_zero = 0.28209479177387814
sh_one = 0.4886025119029199
sh_two = [
    1.0925484305920792,
    -1.0925484305920792,
    0.31539156525252005,
    -1.0925484305920792,
    0.5462742152960396,
]
sh_three = [
    -0.5900435899266435,
    2.890611442640554,
    -0.4570457994644658,
    0.3731763325901154,
    -0.4570457994644658,
    1.445305721320277,
    -0.5900435899266435,
]


def covariance(log_scales, quat):
    squares = [jnp.exp(2.0 * value) for value in log_scales]
    norm_sq = quat[0] * quat[0] + quat[1] * quat[1] + quat[2] * quat[2] + quat[3] * quat[3]
    inv_norm = 1.0 / jnp.sqrt(norm_sq)
    w, x, y, z = [value * inv_norm for value in quat]
    rotation = [
        [1 - 2 * (y * y + z * z), 2 * (x * y - w * z), 2 * (x * z + w * y)],
        [2 * (x * y + w * z), 1 - 2 * (x * x + z * z), 2 * (y * z - w * x)],
        [2 * (x * z - w * y), 2 * (y * z + w * x), 1 - 2 * (x * x + y * y)],
    ]
    scaled = [[rotation[i][j] * squares[j] for j in range(3)] for i in range(3)]

    def entry(i, j):
        return (
            scaled[i][0] * rotation[j][0]
            + scaled[i][1] * rotation[j][1]
            + scaled[i][2] * rotation[j][2]
        )

    return [entry(0, 0), entry(0, 1), entry(0, 2), entry(1, 1), entry(1, 2), entry(2, 2)]


def geometry(x, y, z, sigma):
    s00, s01, s02, s11, s12, s22 = sigma
    inv_z = 1.0 / z
    jac = focal * inv_z
    center_x = jac * x
    center_y = jac * y
    jac_x = -center_x * inv_z
    jac_y = -center_y * inv_z
    jac_sq = jac * jac
    cov_a = jac_sq * s00 + 2.0 * (jac * jac_x) * s02 + jac_x * jac_x * s22 + dilate
    cov_b = jac_sq * s01 + jac * (jac_y * s02 + jac_x * s12) + jac_x * jac_y * s22
    cov_c = jac_sq * s11 + 2.0 * (jac * jac_y) * s12 + jac_y * jac_y * s22 + dilate
    inv_det = 1.0 / (cov_a * cov_c - cov_b * cov_b)
    return center_x, center_y, cov_c * inv_det, -cov_b * inv_det, cov_a * inv_det


def harmonic_basis(x, y, z):
    inv_distance = 1.0 / jnp.sqrt(x * x + y * y + z * z)
    dx = x * inv_distance
    dy = y * inv_distance
    dz = z * inv_distance
    xx = dx * dx
    yy = dy * dy
    zz = dz * dz
    xy = dx * dy
    yz = dy * dz
    xz = dx * dz
    return [
        -sh_one * dy,
        sh_one * dz,
        -sh_one * dx,
        sh_two[0] * xy,
        sh_two[1] * yz,
        sh_two[2] * (2 * zz - xx - yy),
        sh_two[3] * xz,
        sh_two[4] * (xx - yy),
        sh_three[0] * dy * (3 * xx - yy),
        sh_three[1] * xy * dz,
        sh_three[2] * dy * (4 * zz - xx - yy),
        sh_three[3] * dz * (2 * zz - 3 * xx - 3 * yy),
        sh_three[4] * dx * (4 * zz - xx - yy),
        sh_three[5] * dz * (xx - yy),
        sh_three[6] * dx * (xx - 3 * yy),
    ]


def pieces(value, count):
    out = []
    for at in range(count):
        piece = value.astype(BF16)
        out.append(piece)
        if at + 1 < count:
            value = value - piece.astype(F32)
    return out


def dot(left, right, dims):
    return lax.dot_general(left, right, ((dims[0], dims[1]), ((), ())), preferred_element_type=F32)


def iota(shape, axis):
    return lax.broadcasted_iota(jnp.int32, shape, axis)


def kernel(
    owners,
    views,
    params_ref,
    cam_ref,
    ids_ref,
    slots_ref,
    len_ref,
    cot_ref,
    image_ref,
    grads_ref,
    held,
    asked,
    cam_held,
    slots_held,
    len_held,
    held_cot,
    image,
    summed,
    ids_out,
    ids_in,
    cam_out,
    cam_in,
    table,
    low_hot,
    high_hot,
    feat_out,
    feat_in,
    wide,
    gathered,
    exponent,
    along,
    alpha_all,
    blend_all,
    split_a,
    split_b,
    split_c,
    split_d,
    grad_out,
    grad_in,
    dense,
    view_in,
    load_sem,
    store_sem,
    ids_s,
    ids_r,
    feat_s,
    feat_r,
    grad_s,
    grad_r,
    cam_s,
    cam_r,
    view_s,
    view_r,
):
    me = lax.axis_index("gs")
    my_view = lax.axis_index("view")
    my_y = lax.rem(me, LINE)
    my_z = lax.div(me, LINE)
    my_x = lax.div(my_view, 2)
    my_core = lax.rem(my_view, 2)
    planes = owners // LINE
    blocks = held.shape[1]
    chunk = blocks // views

    def plane(i):
        half = (i + 1) // 2
        odd = i % 2
        return lax.rem(my_z + odd * half + (1 - odd) * (planes - half), planes)

    def peers(i, first):
        return [plane(i) * LINE + lax.rem(my_y + step, LINE) for step in range(1 if first else 0, LINE)]

    def view_peer(i):
        pair = i // 2
        step = pair + pair // 2 - 2 * (pair // 3)
        return lax.rem(my_x + step, views // 2) * 2 + lax.rem(my_core + i, 2)

    ids_load = pltpu.make_async_copy(ids_ref.at[0, 0], asked, load_sem.at[2])
    cam_load = pltpu.make_async_copy(cam_ref, cam_held, load_sem.at[3])
    slots_load = pltpu.make_async_copy(slots_ref.at[0], slots_held, load_sem.at[4])
    len_load = pltpu.make_async_copy(len_ref, len_held, load_sem.at[5])
    cot_load = pltpu.make_async_copy(cot_ref, held_cot, load_sem.at[1])
    ids_load.start()
    cam_load.start()

    barrier = pltpu.get_barrier_semaphore()

    def greet(off, carry):
        peer = lax.rem(me + off, owners)
        pl.semaphore_signal(barrier, inc=1, device_id=(my_view, peer), device_id_type=MESH)
        return carry

    lax.fori_loop(1, owners, greet, 0)

    def greet_view(off, carry):
        peer = lax.rem(my_view + off, views)
        pl.semaphore_signal(barrier, inc=1, device_id=(peer, me), device_id_type=MESH)
        return carry

    lax.fori_loop(1, views, greet_view, 0)

    def load_body(j, carry):
        pltpu.make_async_copy(
            params_ref.at[:, pl.ds(pl.multiple_of(j * LANES, LANES), LANES)],
            held.at[:, j, :],
            load_sem.at[0],
        ).start()
        return carry

    lax.fori_loop(0, blocks, load_body, 0)
    slots_load.start()
    len_load.start()
    cot_load.start()

    def ids_copy(to, sender):
        return pltpu.make_async_remote_copy(
            src_ref=ids_out.at[to],
            dst_ref=ids_in.at[sender],
            send_sem=ids_s.at[to],
            recv_sem=ids_r.at[sender],
            device_id=(my_view, to),
            device_id_type=MESH,
        )

    def feat_copy(to, sender):
        return pltpu.make_async_remote_copy(
            src_ref=feat_out.at[to, pl.ds(0, 5)],
            dst_ref=feat_in.at[sender, pl.ds(0, 5)],
            send_sem=feat_s.at[to],
            recv_sem=feat_r.at[sender],
            device_id=(my_view, to),
            device_id_type=MESH,
        )

    def grad_copy(to, sender):
        return pltpu.make_async_remote_copy(
            src_ref=grad_out.at[to, pl.ds(0, 5)],
            dst_ref=grad_in.at[sender, pl.ds(0, 5)],
            send_sem=grad_s.at[to],
            recv_sem=grad_r.at[sender],
            device_id=(my_view, to),
            device_id_type=MESH,
        )

    def cam_copy(to, sender):
        return pltpu.make_async_remote_copy(
            src_ref=cam_out,
            dst_ref=cam_in.at[sender],
            send_sem=cam_s.at[to],
            recv_sem=cam_r.at[sender],
            device_id=(to, me),
            device_id_type=MESH,
        )

    def view_copy(to, sender):
        return pltpu.make_async_remote_copy(
            src_ref=dense.at[:, pl.ds(pl.multiple_of(to * chunk, chunk), chunk), :],
            dst_ref=view_in.at[sender],
            send_sem=view_s.at[to],
            recv_sem=view_r.at[sender],
            device_id=(to, me),
            device_id_type=MESH,
        )

    def wait_sent(copy):
        def body(off, carry):
            copy(lax.rem(me + off, owners), me).wait_send()
            return carry

        lax.fori_loop(1, owners, body, 0)

    ids_load.wait()
    doubled = jnp.concatenate([asked[...], asked[...]], axis=1)
    my_half = (iota(doubled.shape, 1) >> 6) == lax.rem(me, 2)
    ids_out[...] = jnp.where(my_half, doubled, 0).reshape(owners, 1, LANES)
    ids_in[me] = ids_out[me]
    cam_load.wait()
    cam_row = iota((8, LANES), 0)
    cam_tile = jnp.where(
        cam_row == 0, cam_held[0:1, 0:1], jnp.where(cam_row == 1, cam_held[0:1, 1:2], cam_held[0:1, 2:3])
    )
    cam_out[...] = cam_tile
    cam_in[my_view] = cam_tile

    pl.semaphore_wait(barrier, owners + views - 2)

    def ids_body(step, carry):
        for peer in peers(planes - 1 - step, False):
            ids_copy(peer, me).start()
        return carry

    lax.fori_loop(0, planes - 1, ids_body, 0)
    for peer in peers(0, True):
        ids_copy(peer, me).start()

    def cam_send(off, carry):
        cam_copy(lax.rem(my_view + off, views), my_view).start()
        return carry

    lax.fori_loop(1, views, cam_send, 0)

    pltpu.make_async_copy(held, held, load_sem.at[0]).wait()

    def features_body(at, carry):
        rows = pl.ds(pl.multiple_of(at * 16, 16), 16)

        def get(r):
            return held[r, rows, :]

        x = get(0) - cam_out[0:1]
        y = get(1) - cam_out[1:2]
        z = get(2) - cam_out[2:3]
        sigma = covariance([get(3), get(4), get(5)], [get(6), get(7), get(8), get(9)])
        values = list(geometry(x, y, z, sigma))
        values.append(-jnp.log(1.0 + jnp.exp(-get(10))))
        basis = harmonic_basis(x, y, z)
        for c in range(3):
            total = sh_zero * get(11 + 16 * c) + 0.5
            for k in range(15):
                total = total + basis[k] * get(12 + 16 * c + k)
            values.append(total)
        half = lax.div(at, 2)
        inner = lax.rem(at, 2)
        lanes = pl.ds(pl.multiple_of(half * LANES, LANES), LANES)
        for c in range(9):
            for s, piece in enumerate(pieces(values[c], 3)):
                if s < 2 or c < 5:
                    row = s * 288 + c * 32 + inner * 16
                    table[pl.ds(pl.multiple_of(row, 16), 16), lanes] = piece
        return carry

    lax.fori_loop(0, blocks // 16, features_body, 0)

    lane_half = iota((8, LANES), 1) < CAP

    rings = [[i for i in range(planes) if (i + 1) // 2 <= 1]]
    rings += [[i for i in range(planes) if (i + 1) // 2 == far] for far in range(2, planes // 2 + 1)]

    def serve(i):
        base = plane(i) * LINE
        ids = jnp.concatenate(
            [ids_in[base] + ids_in[base + 1], ids_in[base + 2] + ids_in[base + 3]], axis=1
        )
        low = (ids & (LANES - 1)) + ((ids >> 12) << 7)
        high = (ids >> 7) & 31
        lanes = pl.ds(pl.multiple_of(base * CAP, LINE * CAP), LINE * CAP)
        right = (iota((256, LINE * CAP), 0) == low).astype(F32).astype(BF16)
        low_hot[:, lanes] = right
        mask = (iota((32, LINE * CAP), 0) == high).astype(F32)
        high_hot[:, lanes] = mask.astype(BF16)
        short = dot(table[0:288], right, ((1,), (0,))) + dot(table[288:576], right, ((1,), (0,)))
        rest = dot(table[576:736], right, ((1,), (0,)))
        picked = jnp.concatenate([short[0:160] + rest, short[160:]], axis=0)
        rows = [
            jnp.sum(picked[c * 32 : c * 32 + 32] * mask, axis=0, keepdims=True) for c in range(9)
        ]
        blank = jnp.zeros((1, LINE * CAP), F32)
        left_group = jnp.concatenate(rows[0:5] + [blank] * 3, axis=0)
        right_group = jnp.concatenate(rows[5:9] + [blank] * 4, axis=0)
        for part in range(2):
            a = left_group[:, part * LANES : (part + 1) * LANES]
            b = right_group[:, part * LANES : (part + 1) * LANES]
            feat_out[base + 2 * part] = jnp.where(lane_half, a, pltpu.roll(b, CAP, 1))
            feat_out[base + 2 * part + 1] = jnp.where(lane_half, pltpu.roll(a, CAP, 1), b)

    for ring in rings:
        for i in ring:
            for peer in peers(i, i == 0):
                ids_copy(peer, peer).wait_recv()
        for i in ring:
            serve(i)
        for i in ring[::-1]:
            for peer in peers(i, i == 0):
                feat_copy(peer, me).start()
    feat_in[me] = feat_out[me]

    slots_load.wait()
    len_load.wait()
    lane_row = iota((TILES, ROWS), 1)
    tile_hot = (lane_row & 15) == iota((TILES, ROWS), 0)
    tile_mask = tile_hot.astype(F32)
    entry_hot = ((iota((ENTRIES, ROWS), 1) >> 4) == iota((ENTRIES, ROWS), 0)).astype(F32).astype(BF16)
    slots = slots_held[...]
    both = jnp.concatenate([slots >> 6, slots & (CAP - 1)], axis=0).astype(F32).astype(BF16)
    spread = dot(both, entry_hot, ((1,), (0,)))
    owner_row = jnp.sum(spread[0:TILES] * tile_mask, axis=0, keepdims=True)
    place_row = jnp.sum(spread[TILES:] * tile_mask, axis=0, keepdims=True)
    lengths = jnp.broadcast_to(len_held[...], (TILES, TILES)).astype(F32).astype(BF16)
    len_row = dot(lengths, tile_mask.astype(BF16), ((1,), (0,)))[0:1]
    entry_row = iota((1, ROWS), 1)
    live = (entry_row >> 4).astype(F32) < len_row
    place_sub = iota((LANES, ROWS), 0)
    place_left = (place_sub.astype(F32) == place_row).astype(F32).astype(BF16)
    place_right = ((place_sub - CAP).astype(F32) == place_row).astype(F32).astype(BF16)
    center_of_x = (entry_row & 15).astype(F32) * 16.0 + (8.0 - 128.0)
    center_of_y = (me * 16 + 8 - 8 * owners).astype(F32)

    pixel = iota((8, PIXELS), 1)
    mono_x = (pixel & 15).astype(F32) - 7.5
    mono_y = (pixel >> 4).astype(F32) - 7.5
    kind = iota((8, PIXELS), 0)
    monomials = jnp.where(kind == 0, mono_x * mono_x, 0.0)
    monomials = jnp.where(kind == 1, mono_x * mono_y, monomials)
    monomials = jnp.where(kind == 2, mono_y * mono_y, monomials)
    monomials = jnp.where(kind == 3, mono_x, monomials)
    monomials = jnp.where(kind == 4, mono_y, monomials)
    monomials = jnp.where(kind == 5, 1.0, monomials)
    monomials_two = jnp.concatenate([monomials, jnp.zeros_like(monomials)], axis=0).astype(BF16)
    monomials_four = jnp.concatenate([monomials] * 3 + [jnp.zeros_like(monomials)], axis=0).astype(BF16)

    cot_load.wait()
    cot = jnp.concatenate(
        [held_cot[pl.ds(half, 3 * TILES, stride=2), :] for half in range(2)], axis=1
    )
    cot_high, cot_low = pieces(cot, 2)

    halves = [[jnp.zeros((8, 256), F32)] * (ROWS // 256) for _ in range(2)]

    def collect(group):
        for i in group:
            for peer in peers(i, i == 0):
                feat_copy(peer, peer).wait_recv()
        bases = [plane(i) * LINE for i in group]
        arrived = jnp.concatenate(
            [feat_in[pl.ds(base, LINE)].reshape(LINE * 8, LANES) for base in bases], axis=0
        )
        count = arrived.shape[0]
        three = pieces(arrived, 3)
        stacks = [jnp.concatenate(three, axis=0), jnp.concatenate(three[0:2], axis=0)]
        for at in range(ROWS // 256):
            lanes = slice(at * 256, at * 256 + 256)
            owners_here = owner_row[:, lanes]
            for side, hot in enumerate((place_left, place_right)):
                found = dot(stacks[side], hot[:, lanes], ((1,), (0,)))
                summed_pieces = found[0:count] + found[count : 2 * count]
                found = summed_pieces + found[2 * count :] if side == 0 else summed_pieces
                total = halves[side][at]
                for n, base in enumerate(bases):
                    for step in range(LINE):
                        row = (n * LINE + step) * 8
                        here = owners_here == (base + step).astype(F32)
                        total = jnp.where(here, found[row : row + 8], total)
                halves[side][at] = total

    near = (planes * 5 + 7) // 8
    collect(list(range(near)))
    if near < planes:
        collect(list(range(near, planes)))
    left = jnp.concatenate(halves[0], axis=1)
    right = jnp.concatenate(halves[1], axis=1)
    center_x = left[0:1] - center_of_x
    center_y = left[1:2] - center_of_y
    conic_a = left[2:3]
    conic_b = left[3:4]
    conic_c = left[4:5]
    log_opacity = right[0:1]
    colors = [right[1 + c : 2 + c] for c in range(3)]

    lin_x = conic_a * center_x + conic_b * center_y
    lin_y = conic_b * center_x + conic_c * center_y
    blank = jnp.zeros((1, ROWS), F32)
    coefs = jnp.concatenate(
        [
            jnp.where(live, -0.5 * conic_a, 0.0),
            jnp.where(live, -conic_b, 0.0),
            jnp.where(live, -0.5 * conic_c, 0.0),
            jnp.where(live, lin_x, 0.0),
            jnp.where(live, lin_y, 0.0),
            jnp.where(live, log_opacity - 0.5 * (lin_x * center_x + lin_y * center_y), -1000.0),
            blank,
            blank,
        ],
        axis=0,
    )
    coef_pieces = jnp.concatenate(
        [piece.astype(F32) for piece in pieces(coefs, 3)] + [jnp.zeros_like(coefs)], axis=0
    )
    exponent[...] = dot(coef_pieces.T.astype(BF16), monomials_four, ((1,), (0,)))

    spread_color = jnp.concatenate([colors[c] * tile_mask for c in range(3)], axis=0)
    color_high, color_low = pieces(spread_color, 2)
    color_sides = jnp.concatenate([color_high, color_high, color_low], axis=0)
    cot_sides = jnp.concatenate([cot_high, cot_low, cot_high], axis=0)
    along[...] = dot(color_sides, cot_sides, ((0,), (0,)))

    def forward_body(k, through):
        rows = pl.ds(pl.multiple_of(k * TILES, TILES), TILES)
        alpha = jnp.exp(exponent[rows, :])
        blend = through * alpha
        alpha_all[rows, :] = alpha
        blend_all[rows, :] = blend
        high, low = pieces(blend, 2)
        split_a[rows, :] = high
        split_b[rows, :] = low
        return through - blend

    lax.fori_loop(0, ENTRIES, forward_body, jnp.ones((TILES, PIXELS), F32), unroll=8)

    def backward_body(step, behind):
        rows = pl.ds(pl.multiple_of((ENTRIES - 1 - step) * TILES, TILES), TILES)
        gain = along[rows, :] - behind
        high, low = pieces(blend_all[rows, :] * gain, 2)
        split_c[rows, :] = high
        split_d[rows, :] = low
        return behind + alpha_all[rows, :] * gain

    lax.fori_loop(0, ENTRIES, backward_body, jnp.zeros((TILES, PIXELS), F32), unroll=8)

    moments = dot(monomials_two, split_c[...], ((1,), (1,))) + dot(
        monomials_two, split_d[...], ((1,), (1,))
    )
    cot_both = jnp.concatenate([cot_high, cot_low], axis=0)
    by_color = dot(cot_both, split_a[...], ((1,), (1,)))
    by_color = (
        by_color[0 : 3 * TILES]
        + by_color[3 * TILES :]
        + dot(cot_high, split_b[...], ((1,), (1,)))
    )
    grad_colors = [
        jnp.sum(by_color[c * TILES : (c + 1) * TILES] * tile_mask, axis=0, keepdims=True)
        for c in range(3)
    ]
    m_xx, m_xy, m_yy, m_x, m_y, m_one = [moments[row : row + 1] for row in range(6)]
    off_x = m_x - center_x * m_one
    off_y = m_y - center_y * m_one
    off_xx = m_xx - center_x * (m_x + off_x)
    off_xy = m_xy - center_x * m_y - center_y * off_x
    off_yy = m_yy - center_y * (m_y + off_y)
    entry_grads = jnp.concatenate(
        [
            conic_a * off_x + conic_b * off_y,
            conic_b * off_x + conic_c * off_y,
            -0.5 * off_xx,
            -off_xy,
            -0.5 * off_yy,
            blank,
            blank,
            blank,
            m_one,
            grad_colors[0],
            grad_colors[1],
            grad_colors[2],
            blank,
            blank,
            blank,
            blank,
        ],
        axis=0,
    )
    grad_high, grad_low = pieces(entry_grads, 2)

    place_both = place_left + place_right
    owner_wide = jnp.broadcast_to(owner_row, (16, ROWS)).astype(BF16)
    nothing = jnp.zeros((16, ROWS), BF16)
    lane_half_all = iota((LINE, 8, LANES), 2) < CAP

    def give(group):
        parts = []
        for piece in (grad_high, grad_low):
            for i in group:
                for step in range(LINE):
                    here = owner_wide == (plane(i) * LINE + step).astype(F32).astype(BF16)
                    parts.append(jnp.where(here, piece, nothing))
        by_slot = dot(jnp.concatenate(parts, axis=0), place_both, ((1,), (1,)))
        half_rows = 16 * LINE * len(group)
        by_slot = by_slot[0:half_rows] + by_slot[half_rows:]
        for n, i in enumerate(group):
            mine = by_slot[n * LINE * 16 : (n + 1) * LINE * 16].reshape(LINE, 16, LANES)
            packed = jnp.where(lane_half_all, mine[:, 0:8], mine[:, 8:16])
            grad_out[pl.ds(plane(i) * LINE, LINE)] = packed
        for i in group:
            for peer in peers(i, i == 0):
                grad_copy(peer, me).start()

    for ring in rings[::-1]:
        give(ring[::-1])
    grad_in[me] = grad_out[me]

    color_both = jnp.concatenate([color_high, color_low], axis=0)
    shown = dot(color_both, split_a[...], ((1,), (0,)))
    shown = (
        shown[0 : 3 * TILES]
        + shown[3 * TILES :]
        + dot(color_high, split_b[...], ((1,), (0,)))
    )
    for half in range(2):
        image[pl.ds(half, 3 * TILES, stride=2), :] = shown[:, half * LANES : half * LANES + LANES]
    pltpu.make_async_copy(image, image_ref, store_sem.at[0]).start()

    wait_sent(ids_copy)
    wait_sent(feat_copy)

    def scatter(ring):
        for i in ring:
            for peer in peers(i, i == 0):
                grad_copy(peer, peer).wait_recv()
        hots = []
        for n, i in enumerate(ring):
            base = plane(i) * LINE
            lanes = pl.ds(pl.multiple_of(base * CAP, LINE * CAP), LINE * CAP)
            tops = []
            bottoms = []
            for part in range(2):
                even = grad_in[base + 2 * part]
                odd = grad_in[base + 2 * part + 1]
                tops.append(jnp.where(lane_half, even, pltpu.roll(odd, CAP, 1)))
                bottoms.append(jnp.where(lane_half, pltpu.roll(even, CAP, 1), odd))
            a = jnp.concatenate(tops, axis=1)
            b = jnp.concatenate(bottoms, axis=1)
            mask = high_hot[:, lanes]
            into = slice(n * LINE * CAP, (n + 1) * LINE * CAP)
            for c in range(9):
                row = a[c : c + 1] if c < 5 else b[c - 5 : c - 4]
                for s, piece in enumerate(pieces(jnp.broadcast_to(row, (32, LINE * CAP)), 2)):
                    wide[s * 288 + c * 32 : s * 288 + c * 32 + 32, into] = piece * mask
            hots.append(low_hot[:, lanes])
        placed = dot(wide[:, 0 : len(ring) * LINE * CAP], jnp.concatenate(hots, axis=1), ((1,), (1,)))
        return placed[0:288] + placed[288:576]

    for ring in rings[:-1]:
        if ring[0] == 0:
            gathered[...] = scatter(ring)
        else:
            gathered[...] += scatter(ring)
    placed = scatter(rings[-1])
    if len(rings) > 1:
        placed = placed + gathered[...]
    placed = placed.reshape(9, 32, 256)
    dense[:, 0:32, :] = placed[:, :, 0:LANES]
    dense[:, 32:64, :] = placed[:, :, LANES:256]

    def view_send(step, carry):
        view_copy(view_peer(views - 1 - step), my_view).start()
        return carry

    lax.fori_loop(0, views - 1, view_send, 0)
    mine = pl.ds(pl.multiple_of(my_view * chunk, chunk), chunk)
    view_in[my_view] = dense[:, mine, :]

    def cam_wait(off, carry):
        peer = lax.rem(my_view + off, views)
        cam_copy(peer, peer).wait_recv()
        cam_copy(peer, my_view).wait_send()
        return carry

    lax.fori_loop(1, views, cam_wait, 0)
    wait_sent(grad_copy)
    pltpu.make_async_copy(image, image_ref, store_sem.at[0]).wait()

    def get(r):
        return held[r, mine, :]

    scale_quat = [get(r) for r in range(3, 10)]

    def shape_of(values):
        return covariance(values[0:3], values[3:7])

    sigma, shape_back = jax.vjp(shape_of, scale_quat)
    zero = jnp.zeros((chunk, LANES), F32)
    for r in range(59):
        summed[r] = zero

    def add_view(v, totals):
        camera = cam_in[v]
        x = get(0) - camera[0:1]
        y = get(1) - camera[1:2]
        z = get(2) - camera[2:3]
        grads = [view_in[v, c] for c in range(9)]
        _, geometry_back = jax.vjp(geometry, x, y, z, sigma)
        gx, gy, gz, g_sigma = geometry_back(tuple(grads[0:5]))
        basis, basis_back = jax.vjp(harmonic_basis, x, y, z)
        g_basis = [zero] * 15
        for c in range(3):
            color_grad = grads[6 + c]
            summed[11 + 16 * c] += sh_zero * color_grad
            for k in range(15):
                row = 12 + 16 * c + k
                summed[row] += basis[k] * color_grad
                g_basis[k] = g_basis[k] + get(row) * color_grad
        hx, hy, hz = basis_back(g_basis)
        add = [gx + hx, gy + hy, gz + hz, grads[5]] + list(g_sigma)
        return tuple(t + a for t, a in zip(totals, add))

    def view_body(i, totals):
        peer = view_peer(i)
        view_copy(peer, peer).wait_recv()
        return add_view(peer, totals)

    totals = add_view(my_view, tuple([zero] * 10))
    totals = lax.fori_loop(1, views, view_body, totals)
    for r in range(3):
        summed[r] = totals[r]
    (by_shape,) = shape_back(list(totals[4:10]))
    for r in range(7):
        summed[3 + r] = by_shape[r]
    summed[10] = totals[3] / (1.0 + jnp.exp(get(10)))

    def store_grads(j):
        return pltpu.make_async_copy(
            summed.at[:, j, :],
            grads_ref.at[:, pl.ds(pl.multiple_of(j * LANES, LANES), LANES)],
            store_sem.at[1],
        )

    def store_grads_body(j, carry):
        store_grads(j).start()
        return carry

    lax.fori_loop(0, chunk, store_grads_body, 0)

    def view_wait(off, carry):
        view_copy(lax.rem(my_view + off, views), my_view).wait_send()
        return carry

    lax.fori_loop(1, views, view_wait, 0)
    pltpu.make_async_copy(summed, summed, store_sem.at[1]).wait()


def local(owners, views, params, cam_pos, req_ids, tile_slots, tile_len, cotangent):
    count, owned = params.shape
    blocks = owned // LANES
    chunk = blocks // views
    slots_all = owners * CAP
    vmem = pltpu.VMEM
    dma = pltpu.SemaphoreType.DMA
    anywhere = pl.BlockSpec(memory_space=pl.ANY)
    image, grads = pl.pallas_call(
        functools.partial(kernel, owners, views),
        out_shape=(
            vmem((6 * TILES, LANES), F32),
            vmem((count, owned // views), F32),
        ),
        in_specs=[anywhere] * 6,
        out_specs=(anywhere, anywhere),
        scratch_shapes=[
            vmem((count, blocks, LANES), F32),
            vmem((owners, CAP), jnp.int32),
            vmem((1, 3), F32),
            vmem((TILES, ENTRIES), jnp.int32),
            vmem((1, TILES), jnp.int32),
            vmem((6 * TILES, LANES), F32),
            vmem((6 * TILES, LANES), F32),
            vmem((count, chunk, LANES), F32),
            vmem((owners, 1, LANES), jnp.int32),
            vmem((owners, 1, LANES), jnp.int32),
            vmem((8, LANES), F32),
            vmem((views, 8, LANES), F32),
            vmem((736, 256), BF16),
            vmem((256, slots_all), BF16),
            vmem((32, slots_all), BF16),
            vmem((owners, 8, LANES), F32),
            vmem((owners, 8, LANES), F32),
            vmem((576, 3 * LINE * CAP), BF16),
            vmem((288, 256), F32),
            vmem((ROWS, PIXELS), F32),
            vmem((ROWS, PIXELS), F32),
            vmem((ROWS, PIXELS), F32),
            vmem((ROWS, PIXELS), F32),
            vmem((ROWS, PIXELS), BF16),
            vmem((ROWS, PIXELS), BF16),
            vmem((ROWS, PIXELS), BF16),
            vmem((ROWS, PIXELS), BF16),
            vmem((owners, 8, LANES), F32),
            vmem((owners, 8, LANES), F32),
            vmem((9, blocks, LANES), F32),
            vmem((views, 9, chunk, LANES), F32),
            dma((6,)),
            dma((2,)),
        ]
        + [dma((owners,)) for _ in range(6)]
        + [dma((views,)) for _ in range(4)],
        compiler_params=pltpu.CompilerParams(
            collective_id=0, has_side_effects=True, vmem_limit_bytes=60 * 1024 * 1024
        ),
        cost_estimate=pl.CostEstimate(
            flops=2_000_000_000, bytes_accessed=4_000_000, transcendentals=300_000
        ),
    )(
        params,
        cam_pos,
        req_ids,
        tile_slots,
        tile_len,
        cotangent.reshape(6 * TILES, LANES),
    )
    return image.reshape(cotangent.shape), grads


def solution(mesh):
    placed = (
        P(None, "gs"),
        P("view", None),
        P("view", "gs", None, None),
        P("view", "gs", None),
        P("view", "gs"),
        P("view", None, "gs"),
    )
    return jax.shard_map(
        functools.partial(local, mesh.shape["gs"], mesh.shape["view"]),
        mesh=mesh,
        in_specs=placed,
        out_specs=(P("view", None, "gs"), P(None, ("gs", "view"))),
        check_vma=False,
    )
```

```python
import functools

import jax
import jax.numpy as jnp
from jax import lax
from jax.experimental import pallas as pl
from jax.experimental.pallas import tpu as pltpu
from jax.sharding import PartitionSpec as P

MESH = pl.DeviceIdType.MESH
F32 = jnp.float32
BF16 = jnp.bfloat16
TILES = 16
ENTRIES = 64
ROWS = TILES * ENTRIES
PIXELS = 256
CAP = 64
LANES = 128
LINE = 4

focal = 1.2 * 128.0
dilate = 0.3
sh_zero = 0.28209479177387814
sh_one = 0.4886025119029199
sh_two = [
    1.0925484305920792,
    -1.0925484305920792,
    0.31539156525252005,
    -1.0925484305920792,
    0.5462742152960396,
]
sh_three = [
    -0.5900435899266435,
    2.890611442640554,
    -0.4570457994644658,
    0.3731763325901154,
    -0.4570457994644658,
    1.445305721320277,
    -0.5900435899266435,
]


def covariance(log_scales, quat):
    squares = [jnp.exp(2.0 * value) for value in log_scales]
    norm_sq = quat[0] * quat[0] + quat[1] * quat[1] + quat[2] * quat[2] + quat[3] * quat[3]
    inv_norm = 1.0 / jnp.sqrt(norm_sq)
    w, x, y, z = [value * inv_norm for value in quat]
    rotation = [
        [1 - 2 * (y * y + z * z), 2 * (x * y - w * z), 2 * (x * z + w * y)],
        [2 * (x * y + w * z), 1 - 2 * (x * x + z * z), 2 * (y * z - w * x)],
        [2 * (x * z - w * y), 2 * (y * z + w * x), 1 - 2 * (x * x + y * y)],
    ]
    scaled = [[rotation[i][j] * squares[j] for j in range(3)] for i in range(3)]

    def entry(i, j):
        return (
            scaled[i][0] * rotation[j][0]
            + scaled[i][1] * rotation[j][1]
            + scaled[i][2] * rotation[j][2]
        )

    return [entry(0, 0), entry(0, 1), entry(0, 2), entry(1, 1), entry(1, 2), entry(2, 2)]


def geometry(x, y, z, sigma):
    s00, s01, s02, s11, s12, s22 = sigma
    inv_z = 1.0 / z
    jac = focal * inv_z
    center_x = jac * x
    center_y = jac * y
    jac_x = -center_x * inv_z
    jac_y = -center_y * inv_z
    jac_sq = jac * jac
    cov_a = jac_sq * s00 + 2.0 * (jac * jac_x) * s02 + jac_x * jac_x * s22 + dilate
    cov_b = jac_sq * s01 + jac * (jac_y * s02 + jac_x * s12) + jac_x * jac_y * s22
    cov_c = jac_sq * s11 + 2.0 * (jac * jac_y) * s12 + jac_y * jac_y * s22 + dilate
    inv_det = 1.0 / (cov_a * cov_c - cov_b * cov_b)
    return center_x, center_y, cov_c * inv_det, -cov_b * inv_det, cov_a * inv_det


def harmonic_basis(x, y, z):
    inv_distance = 1.0 / jnp.sqrt(x * x + y * y + z * z)
    dx = x * inv_distance
    dy = y * inv_distance
    dz = z * inv_distance
    xx = dx * dx
    yy = dy * dy
    zz = dz * dz
    xy = dx * dy
    yz = dy * dz
    xz = dx * dz
    return [
        -sh_one * dy,
        sh_one * dz,
        -sh_one * dx,
        sh_two[0] * xy,
        sh_two[1] * yz,
        sh_two[2] * (2 * zz - xx - yy),
        sh_two[3] * xz,
        sh_two[4] * (xx - yy),
        sh_three[0] * dy * (3 * xx - yy),
        sh_three[1] * xy * dz,
        sh_three[2] * dy * (4 * zz - xx - yy),
        sh_three[3] * dz * (2 * zz - 3 * xx - 3 * yy),
        sh_three[4] * dx * (4 * zz - xx - yy),
        sh_three[5] * dz * (xx - yy),
        sh_three[6] * dx * (xx - 3 * yy),
    ]


def pieces(value, count):
    out = []
    for at in range(count):
        piece = value.astype(BF16)
        out.append(piece)
        if at + 1 < count:
            value = value - piece.astype(F32)
    return out


def dot(left, right, dims):
    return lax.dot_general(left, right, ((dims[0], dims[1]), ((), ())), preferred_element_type=F32)


def iota(shape, axis):
    return lax.broadcasted_iota(jnp.int32, shape, axis)


def kernel(
    owners,
    views,
    params_ref,
    cam_ref,
    ids_ref,
    slots_ref,
    len_ref,
    cot_ref,
    image,
    summed,
    held,
    asked,
    cam_held,
    slots_held,
    len_held,
    held_cot,
    ids_out,
    ids_in,
    cam_out,
    cam_in,
    table,
    low_hot,
    high_hot,
    feat_out,
    feat_in,
    wide,
    gathered,
    exponent,
    along,
    alpha_all,
    blend_all,
    split_a,
    split_b,
    split_c,
    split_d,
    grad_out,
    grad_in,
    dense,
    view_in,
    load_sem,
    ids_s,
    ids_r,
    feat_s,
    feat_r,
    grad_s,
    grad_r,
    cam_s,
    cam_r,
    view_s,
    view_r,
):
    me = lax.axis_index("gs")
    my_view = lax.axis_index("view")
    my_y = lax.rem(me, LINE)
    my_z = lax.div(me, LINE)
    my_x = lax.div(my_view, 2)
    my_core = lax.rem(my_view, 2)
    planes = owners // LINE
    blocks = held.shape[1]
    chunk = blocks // views

    def plane(i):
        half = (i + 1) // 2
        odd = i % 2
        return lax.rem(my_z + odd * half + (1 - odd) * (planes - half), planes)

    def peers(i, first):
        return [plane(i) * LINE + lax.rem(my_y + step, LINE) for step in range(1 if first else 0, LINE)]

    def view_peer(i):
        pair = i // 2
        step = pair + pair // 2 - 2 * (pair // 3)
        return lax.rem(my_x + step, views // 2) * 2 + lax.rem(my_core + i, 2)

    ids_load = pltpu.make_async_copy(ids_ref.at[0, 0], asked, load_sem.at[2])
    cam_load = pltpu.make_async_copy(cam_ref, cam_held, load_sem.at[3])
    slots_load = pltpu.make_async_copy(slots_ref.at[0], slots_held, load_sem.at[4])
    len_load = pltpu.make_async_copy(len_ref, len_held, load_sem.at[5])
    cot_load = pltpu.make_async_copy(cot_ref, held_cot, load_sem.at[1])
    ids_load.start()
    cam_load.start()

    barrier = pltpu.get_barrier_semaphore()

    def greet(off, carry):
        peer = lax.rem(me + off, owners)
        pl.semaphore_signal(barrier, inc=1, device_id=(my_view, peer), device_id_type=MESH)
        return carry

    lax.fori_loop(1, owners, greet, 0)

    def greet_view(off, carry):
        peer = lax.rem(my_view + off, views)
        pl.semaphore_signal(barrier, inc=1, device_id=(peer, me), device_id_type=MESH)
        return carry

    lax.fori_loop(1, views, greet_view, 0)

    def load_body(j, carry):
        pltpu.make_async_copy(
            params_ref.at[:, pl.ds(pl.multiple_of(j * LANES, LANES), LANES)],
            held.at[:, j, :],
            load_sem.at[0],
        ).start()
        return carry

    lax.fori_loop(0, blocks, load_body, 0)
    slots_load.start()
    len_load.start()
    cot_load.start()

    def ids_copy(to, sender):
        return pltpu.make_async_remote_copy(
            src_ref=ids_out.at[to],
            dst_ref=ids_in.at[sender],
            send_sem=ids_s.at[to],
            recv_sem=ids_r.at[sender],
            device_id=(my_view, to),
            device_id_type=MESH,
        )

    def feat_copy(to, sender):
        return pltpu.make_async_remote_copy(
            src_ref=feat_out.at[to, pl.ds(0, 5)],
            dst_ref=feat_in.at[sender, pl.ds(0, 5)],
            send_sem=feat_s.at[to],
            recv_sem=feat_r.at[sender],
            device_id=(my_view, to),
            device_id_type=MESH,
        )

    def grad_copy(to, sender):
        return pltpu.make_async_remote_copy(
            src_ref=grad_out.at[to, pl.ds(0, 5)],
            dst_ref=grad_in.at[sender, pl.ds(0, 5)],
            send_sem=grad_s.at[to],
            recv_sem=grad_r.at[sender],
            device_id=(my_view, to),
            device_id_type=MESH,
        )

    def cam_copy(to, sender):
        return pltpu.make_async_remote_copy(
            src_ref=cam_out,
            dst_ref=cam_in.at[sender],
            send_sem=cam_s.at[to],
            recv_sem=cam_r.at[sender],
            device_id=(to, me),
            device_id_type=MESH,
        )

    def view_copy(to, sender):
        return pltpu.make_async_remote_copy(
            src_ref=dense.at[:, pl.ds(pl.multiple_of(to * chunk, chunk), chunk), :],
            dst_ref=view_in.at[sender],
            send_sem=view_s.at[to],
            recv_sem=view_r.at[sender],
            device_id=(to, me),
            device_id_type=MESH,
        )

    def wait_sent(copy):
        def body(off, carry):
            copy(lax.rem(me + off, owners), me).wait_send()
            return carry

        lax.fori_loop(1, owners, body, 0)

    ids_load.wait()
    doubled = jnp.concatenate([asked[...], asked[...]], axis=1)
    my_half = (iota(doubled.shape, 1) >> 6) == lax.rem(me, 2)
    ids_out[...] = jnp.where(my_half, doubled, 0).reshape(owners, 1, LANES)
    ids_in[me] = ids_out[me]
    cam_load.wait()
    cam_row = iota((8, LANES), 0)
    cam_tile = jnp.where(
        cam_row == 0, cam_held[0:1, 0:1], jnp.where(cam_row == 1, cam_held[0:1, 1:2], cam_held[0:1, 2:3])
    )
    cam_out[...] = cam_tile
    cam_in[my_view] = cam_tile

    pl.semaphore_wait(barrier, owners + views - 2)

    def ids_body(step, carry):
        for peer in peers(planes - 1 - step, False):
            ids_copy(peer, me).start()
        return carry

    lax.fori_loop(0, planes - 1, ids_body, 0)
    for peer in peers(0, True):
        ids_copy(peer, me).start()

    def cam_send(off, carry):
        cam_copy(lax.rem(my_view + off, views), my_view).start()
        return carry

    lax.fori_loop(1, views, cam_send, 0)

    pltpu.make_async_copy(held, held, load_sem.at[0]).wait()

    def features_body(at, carry):
        rows = pl.ds(pl.multiple_of(at * 16, 16), 16)

        def get(r):
            return held[r, rows, :]

        x = get(0) - cam_out[0:1]
        y = get(1) - cam_out[1:2]
        z = get(2) - cam_out[2:3]
        sigma = covariance([get(3), get(4), get(5)], [get(6), get(7), get(8), get(9)])
        values = list(geometry(x, y, z, sigma))
        values.append(-jnp.log(1.0 + jnp.exp(-get(10))))
        basis = harmonic_basis(x, y, z)
        for c in range(3):
            total = sh_zero * get(11 + 16 * c) + 0.5
            for k in range(15):
                total = total + basis[k] * get(12 + 16 * c + k)
            values.append(total)
        half = lax.div(at, 2)
        inner = lax.rem(at, 2)
        lanes = pl.ds(pl.multiple_of(half * LANES, LANES), LANES)
        for c in range(9):
            for s, piece in enumerate(pieces(values[c], 3)):
                if s < 2 or c < 5:
                    row = s * 288 + c * 32 + inner * 16
                    table[pl.ds(pl.multiple_of(row, 16), 16), lanes] = piece
        return carry

    lax.fori_loop(0, blocks // 16, features_body, 0)

    lane_half = iota((8, LANES), 1) < CAP

    rings = [[i for i in range(planes) if (i + 1) // 2 <= 1]]
    rings += [[i for i in range(planes) if (i + 1) // 2 == far] for far in range(2, planes // 2 + 1)]

    def serve(i):
        base = plane(i) * LINE
        ids = jnp.concatenate(
            [ids_in[base] + ids_in[base + 1], ids_in[base + 2] + ids_in[base + 3]], axis=1
        )
        low = (ids & (LANES - 1)) + ((ids >> 12) << 7)
        high = (ids >> 7) & 31
        lanes = pl.ds(pl.multiple_of(base * CAP, LINE * CAP), LINE * CAP)
        right = (iota((256, LINE * CAP), 0) == low).astype(F32).astype(BF16)
        low_hot[:, lanes] = right
        mask = (iota((32, LINE * CAP), 0) == high).astype(F32)
        high_hot[:, lanes] = mask.astype(BF16)
        short = dot(table[0:288], right, ((1,), (0,))) + dot(table[288:576], right, ((1,), (0,)))
        rest = dot(table[576:736], right, ((1,), (0,)))
        picked = jnp.concatenate([short[0:160] + rest, short[160:]], axis=0)
        rows = [
            jnp.sum(picked[c * 32 : c * 32 + 32] * mask, axis=0, keepdims=True) for c in range(9)
        ]
        blank = jnp.zeros((1, LINE * CAP), F32)
        left_group = jnp.concatenate(rows[0:5] + [blank] * 3, axis=0)
        right_group = jnp.concatenate(rows[5:9] + [blank] * 4, axis=0)
        for part in range(2):
            a = left_group[:, part * LANES : (part + 1) * LANES]
            b = right_group[:, part * LANES : (part + 1) * LANES]
            feat_out[base + 2 * part] = jnp.where(lane_half, a, pltpu.roll(b, CAP, 1))
            feat_out[base + 2 * part + 1] = jnp.where(lane_half, pltpu.roll(a, CAP, 1), b)

    for ring in rings:
        for i in ring:
            for peer in peers(i, i == 0):
                ids_copy(peer, peer).wait_recv()
        for i in ring:
            serve(i)
        for i in ring[::-1]:
            for peer in peers(i, i == 0):
                feat_copy(peer, me).start()
    feat_in[me] = feat_out[me]

    slots_load.wait()
    len_load.wait()
    lane_row = iota((TILES, ROWS), 1)
    tile_hot = (lane_row & 15) == iota((TILES, ROWS), 0)
    tile_mask = tile_hot.astype(F32)
    entry_hot = ((iota((ENTRIES, ROWS), 1) >> 4) == iota((ENTRIES, ROWS), 0)).astype(F32).astype(BF16)
    slots = slots_held[...]
    both = jnp.concatenate([slots >> 6, slots & (CAP - 1)], axis=0).astype(F32).astype(BF16)
    spread = dot(both, entry_hot, ((1,), (0,)))
    owner_row = jnp.sum(spread[0:TILES] * tile_mask, axis=0, keepdims=True)
    place_row = jnp.sum(spread[TILES:] * tile_mask, axis=0, keepdims=True)
    lengths = jnp.broadcast_to(len_held[...], (TILES, TILES)).astype(F32).astype(BF16)
    len_row = dot(lengths, tile_mask.astype(BF16), ((1,), (0,)))[0:1]
    entry_row = iota((1, ROWS), 1)
    live = (entry_row >> 4).astype(F32) < len_row
    place_sub = iota((LANES, ROWS), 0)
    place_left = (place_sub.astype(F32) == place_row).astype(F32).astype(BF16)
    place_right = ((place_sub - CAP).astype(F32) == place_row).astype(F32).astype(BF16)
    center_of_x = (entry_row & 15).astype(F32) * 16.0 + (8.0 - 128.0)
    center_of_y = (me * 16 + 8 - 8 * owners).astype(F32)

    pixel = iota((8, PIXELS), 1)
    mono_x = (pixel & 15).astype(F32) - 7.5
    mono_y = (pixel >> 4).astype(F32) - 7.5
    kind = iota((8, PIXELS), 0)
    monomials = jnp.where(kind == 0, mono_x * mono_x, 0.0)
    monomials = jnp.where(kind == 1, mono_x * mono_y, monomials)
    monomials = jnp.where(kind == 2, mono_y * mono_y, monomials)
    monomials = jnp.where(kind == 3, mono_x, monomials)
    monomials = jnp.where(kind == 4, mono_y, monomials)
    monomials = jnp.where(kind == 5, 1.0, monomials)
    monomials_two = jnp.concatenate([monomials, jnp.zeros_like(monomials)], axis=0).astype(BF16)
    monomials_four = jnp.concatenate([monomials] * 3 + [jnp.zeros_like(monomials)], axis=0).astype(BF16)

    cot_load.wait()
    cot = jnp.concatenate(
        [held_cot[pl.ds(half, 3 * TILES, stride=2), :] for half in range(2)], axis=1
    )
    cot_high, cot_low = pieces(cot, 2)

    halves = [[jnp.zeros((8, 256), F32)] * (ROWS // 256) for _ in range(2)]

    def collect(group):
        for i in group:
            for peer in peers(i, i == 0):
                feat_copy(peer, peer).wait_recv()
        bases = [plane(i) * LINE for i in group]
        arrived = jnp.concatenate(
            [feat_in[pl.ds(base, LINE)].reshape(LINE * 8, LANES) for base in bases], axis=0
        )
        count = arrived.shape[0]
        three = pieces(arrived, 3)
        stacks = [jnp.concatenate(three, axis=0), jnp.concatenate(three[0:2], axis=0)]
        for at in range(ROWS // 256):
            lanes = slice(at * 256, at * 256 + 256)
            owners_here = owner_row[:, lanes]
            for side, hot in enumerate((place_left, place_right)):
                found = dot(stacks[side], hot[:, lanes], ((1,), (0,)))
                summed_pieces = found[0:count] + found[count : 2 * count]
                found = summed_pieces + found[2 * count :] if side == 0 else summed_pieces
                total = halves[side][at]
                for n, base in enumerate(bases):
                    for step in range(LINE):
                        row = (n * LINE + step) * 8
                        here = owners_here == (base + step).astype(F32)
                        total = jnp.where(here, found[row : row + 8], total)
                halves[side][at] = total

    near = (planes * 5 + 7) // 8
    collect(list(range(near)))
    if near < planes:
        collect(list(range(near, planes)))
    left = jnp.concatenate(halves[0], axis=1)
    right = jnp.concatenate(halves[1], axis=1)
    center_x = left[0:1] - center_of_x
    center_y = left[1:2] - center_of_y
    conic_a = left[2:3]
    conic_b = left[3:4]
    conic_c = left[4:5]
    log_opacity = right[0:1]
    colors = [right[1 + c : 2 + c] for c in range(3)]

    lin_x = conic_a * center_x + conic_b * center_y
    lin_y = conic_b * center_x + conic_c * center_y
    blank = jnp.zeros((1, ROWS), F32)
    coefs = jnp.concatenate(
        [
            jnp.where(live, -0.5 * conic_a, 0.0),
            jnp.where(live, -conic_b, 0.0),
            jnp.where(live, -0.5 * conic_c, 0.0),
            jnp.where(live, lin_x, 0.0),
            jnp.where(live, lin_y, 0.0),
            jnp.where(live, log_opacity - 0.5 * (lin_x * center_x + lin_y * center_y), -1000.0),
            blank,
            blank,
        ],
        axis=0,
    )
    coef_pieces = jnp.concatenate(
        [piece.astype(F32) for piece in pieces(coefs, 3)] + [jnp.zeros_like(coefs)], axis=0
    )
    exponent[...] = dot(coef_pieces.T.astype(BF16), monomials_four, ((1,), (0,)))

    spread_color = jnp.concatenate([colors[c] * tile_mask for c in range(3)], axis=0)
    color_high, color_low = pieces(spread_color, 2)
    color_sides = jnp.concatenate([color_high, color_high, color_low], axis=0)
    cot_sides = jnp.concatenate([cot_high, cot_low, cot_high], axis=0)
    along[...] = dot(color_sides, cot_sides, ((0,), (0,)))

    def forward_body(k, through):
        rows = pl.ds(pl.multiple_of(k * TILES, TILES), TILES)
        alpha = jnp.exp(exponent[rows, :])
        blend = through * alpha
        alpha_all[rows, :] = alpha
        blend_all[rows, :] = blend
        high, low = pieces(blend, 2)
        split_a[rows, :] = high
        split_b[rows, :] = low
        return through - blend

    lax.fori_loop(0, ENTRIES, forward_body, jnp.ones((TILES, PIXELS), F32), unroll=True)

    cot_both = jnp.concatenate([cot_high, cot_low], axis=0)
    by_color = dot(cot_both, split_a[...], ((1,), (1,)))
    by_color = (
        by_color[0 : 3 * TILES]
        + by_color[3 * TILES :]
        + dot(cot_high, split_b[...], ((1,), (1,)))
    )

    def backward_body(step, behind):
        rows = pl.ds(pl.multiple_of((ENTRIES - 1 - step) * TILES, TILES), TILES)
        gain = along[rows, :] - behind
        high, low = pieces(blend_all[rows, :] * gain, 2)
        split_c[rows, :] = high
        split_d[rows, :] = low
        return behind + alpha_all[rows, :] * gain

    lax.fori_loop(0, ENTRIES, backward_body, jnp.zeros((TILES, PIXELS), F32), unroll=True)

    moments = dot(monomials_two, split_c[...], ((1,), (1,))) + dot(
        monomials_two, split_d[...], ((1,), (1,))
    )
    grad_colors = [
        jnp.sum(by_color[c * TILES : (c + 1) * TILES] * tile_mask, axis=0, keepdims=True)
        for c in range(3)
    ]
    m_xx, m_xy, m_yy, m_x, m_y, m_one = [moments[row : row + 1] for row in range(6)]
    off_x = m_x - center_x * m_one
    off_y = m_y - center_y * m_one
    off_xx = m_xx - center_x * (m_x + off_x)
    off_xy = m_xy - center_x * m_y - center_y * off_x
    off_yy = m_yy - center_y * (m_y + off_y)
    entry_grads = jnp.concatenate(
        [
            conic_a * off_x + conic_b * off_y,
            conic_b * off_x + conic_c * off_y,
            -0.5 * off_xx,
            -off_xy,
            -0.5 * off_yy,
            blank,
            blank,
            blank,
            m_one,
            grad_colors[0],
            grad_colors[1],
            grad_colors[2],
            blank,
            blank,
            blank,
            blank,
        ],
        axis=0,
    )
    grad_high, grad_low = pieces(entry_grads, 2)

    place_both = place_left + place_right
    owner_wide = jnp.broadcast_to(owner_row, (16, ROWS)).astype(BF16)
    nothing = jnp.zeros((16, ROWS), BF16)
    lane_half_all = iota((LINE, 8, LANES), 2) < CAP

    def give(group):
        parts = []
        for piece in (grad_high, grad_low):
            for i in group:
                for step in range(LINE):
                    here = owner_wide == (plane(i) * LINE + step).astype(F32).astype(BF16)
                    parts.append(jnp.where(here, piece, nothing))
        by_slot = dot(jnp.concatenate(parts, axis=0), place_both, ((1,), (1,)))
        half_rows = 16 * LINE * len(group)
        by_slot = by_slot[0:half_rows] + by_slot[half_rows:]
        for n, i in enumerate(group):
            mine = by_slot[n * LINE * 16 : (n + 1) * LINE * 16].reshape(LINE, 16, LANES)
            packed = jnp.where(lane_half_all, mine[:, 0:8], mine[:, 8:16])
            grad_out[pl.ds(plane(i) * LINE, LINE)] = packed
        for i in group:
            for peer in peers(i, i == 0):
                grad_copy(peer, me).start()

    for ring in rings[::-1]:
        give(ring[::-1])
    grad_in[me] = grad_out[me]

    color_both = jnp.concatenate([color_high, color_low], axis=0)
    shown = dot(color_both, split_a[...], ((1,), (0,)))
    shown = (
        shown[0 : 3 * TILES]
        + shown[3 * TILES :]
        + dot(color_high, split_b[...], ((1,), (0,)))
    )
    for half in range(2):
        image[pl.ds(half, 3 * TILES, stride=2), :] = shown[:, half * LANES : half * LANES + LANES]

    wait_sent(ids_copy)
    wait_sent(feat_copy)

    def scatter(ring):
        for i in ring:
            for peer in peers(i, i == 0):
                grad_copy(peer, peer).wait_recv()
        hots = []
        for n, i in enumerate(ring):
            base = plane(i) * LINE
            lanes = pl.ds(pl.multiple_of(base * CAP, LINE * CAP), LINE * CAP)
            tops = []
            bottoms = []
            for part in range(2):
                even = grad_in[base + 2 * part]
                odd = grad_in[base + 2 * part + 1]
                tops.append(jnp.where(lane_half, even, pltpu.roll(odd, CAP, 1)))
                bottoms.append(jnp.where(lane_half, pltpu.roll(even, CAP, 1), odd))
            a = jnp.concatenate(tops, axis=1)
            b = jnp.concatenate(bottoms, axis=1)
            mask = high_hot[:, lanes]
            into = slice(n * LINE * CAP, (n + 1) * LINE * CAP)
            for c in range(9):
                row = a[c : c + 1] if c < 5 else b[c - 5 : c - 4]
                for s, piece in enumerate(pieces(jnp.broadcast_to(row, (32, LINE * CAP)), 2)):
                    wide[s * 288 + c * 32 : s * 288 + c * 32 + 32, into] = piece * mask
            hots.append(low_hot[:, lanes])
        placed = dot(wide[:, 0 : len(ring) * LINE * CAP], jnp.concatenate(hots, axis=1), ((1,), (1,)))
        return placed[0:288] + placed[288:576]

    for ring in rings[:-1]:
        if ring[0] == 0:
            gathered[...] = scatter(ring)
        else:
            gathered[...] += scatter(ring)
    placed = scatter(rings[-1])
    if len(rings) > 1:
        placed = placed + gathered[...]
    placed = placed.reshape(9, 32, 256)
    dense[:, 0:32, :] = placed[:, :, 0:LANES]
    dense[:, 32:64, :] = placed[:, :, LANES:256]

    def view_send(step, carry):
        view_copy(view_peer(views - 1 - step), my_view).start()
        return carry

    lax.fori_loop(0, views - 1, view_send, 0)
    mine = pl.ds(pl.multiple_of(my_view * chunk, chunk), chunk)
    view_in[my_view] = dense[:, mine, :]

    def cam_wait(off, carry):
        peer = lax.rem(my_view + off, views)
        cam_copy(peer, peer).wait_recv()
        cam_copy(peer, my_view).wait_send()
        return carry

    lax.fori_loop(1, views, cam_wait, 0)
    wait_sent(grad_copy)

    def get(r):
        return held[r, mine, :]

    scale_quat = [get(r) for r in range(3, 10)]

    def shape_of(values):
        return covariance(values[0:3], values[3:7])

    sigma, shape_back = jax.vjp(shape_of, scale_quat)
    zero = jnp.zeros((chunk, LANES), F32)
    for r in range(59):
        summed[r] = zero

    def add_view(v, totals):
        camera = cam_in[v]
        x = get(0) - camera[0:1]
        y = get(1) - camera[1:2]
        z = get(2) - camera[2:3]
        grads = [view_in[v, c] for c in range(9)]
        _, geometry_back = jax.vjp(geometry, x, y, z, sigma)
        gx, gy, gz, g_sigma = geometry_back(tuple(grads[0:5]))
        basis, basis_back = jax.vjp(harmonic_basis, x, y, z)
        g_basis = [zero] * 15
        for c in range(3):
            color_grad = grads[6 + c]
            summed[11 + 16 * c] += sh_zero * color_grad
            for k in range(15):
                row = 12 + 16 * c + k
                summed[row] += basis[k] * color_grad
                g_basis[k] = g_basis[k] + get(row) * color_grad
        hx, hy, hz = basis_back(g_basis)
        add = [gx + hx, gy + hy, gz + hz, grads[5]] + list(g_sigma)
        return tuple(t + a for t, a in zip(totals, add))

    def view_body(i, totals):
        peer = view_peer(i)
        view_copy(peer, peer).wait_recv()
        return add_view(peer, totals)

    totals = add_view(my_view, tuple([zero] * 10))
    totals = lax.fori_loop(1, views, view_body, totals)
    for r in range(3):
        summed[r] = totals[r]
    (by_shape,) = shape_back(list(totals[4:10]))
    for r in range(7):
        summed[3 + r] = by_shape[r]
    summed[10] = totals[3] / (1.0 + jnp.exp(get(10)))

    def view_wait(off, carry):
        view_copy(lax.rem(my_view + off, views), my_view).wait_send()
        return carry

    lax.fori_loop(1, views, view_wait, 0)


def store_kernel(image, summed, image_ref, grads_ref, sems):
    image_store = pltpu.make_async_copy(image, image_ref, sems.at[0])
    image_store.start()
    for j in range(summed.shape[1]):
        pltpu.make_async_copy(
            summed.at[:, j, :], grads_ref.at[:, j * LANES : (j + 1) * LANES], sems.at[1]
        ).start()
    image_store.wait()
    pltpu.make_async_copy(summed, summed, sems.at[1]).wait()


def local(owners, views, params, cam_pos, req_ids, tile_slots, tile_len, cotangent):
    count, owned = params.shape
    blocks = owned // LANES
    chunk = blocks // views
    slots_all = owners * CAP
    vmem = pltpu.VMEM
    dma = pltpu.SemaphoreType.DMA
    anywhere = pl.BlockSpec(memory_space=pl.ANY)
    inside = pl.BlockSpec(memory_space=vmem)
    image, summed = pl.pallas_call(
        functools.partial(kernel, owners, views),
        out_shape=(
            vmem((6 * TILES, LANES), F32),
            vmem((count, chunk, LANES), F32),
        ),
        in_specs=[anywhere] * 6,
        out_specs=(inside, inside),
        scratch_shapes=[
            vmem((count, blocks, LANES), F32),
            vmem((owners, CAP), jnp.int32),
            vmem((1, 3), F32),
            vmem((TILES, ENTRIES), jnp.int32),
            vmem((1, TILES), jnp.int32),
            vmem((6 * TILES, LANES), F32),
            vmem((owners, 1, LANES), jnp.int32),
            vmem((owners, 1, LANES), jnp.int32),
            vmem((8, LANES), F32),
            vmem((views, 8, LANES), F32),
            vmem((736, 256), BF16),
            vmem((256, slots_all), BF16),
            vmem((32, slots_all), BF16),
            vmem((owners, 8, LANES), F32),
            vmem((owners, 8, LANES), F32),
            vmem((576, 3 * LINE * CAP), BF16),
            vmem((288, 256), F32),
            vmem((ROWS, PIXELS), F32),
            vmem((ROWS, PIXELS), F32),
            vmem((ROWS, PIXELS), F32),
            vmem((ROWS, PIXELS), F32),
            vmem((ROWS, PIXELS), BF16),
            vmem((ROWS, PIXELS), BF16),
            vmem((ROWS, PIXELS), BF16),
            vmem((ROWS, PIXELS), BF16),
            vmem((owners, 8, LANES), F32),
            vmem((owners, 8, LANES), F32),
            vmem((9, blocks, LANES), F32),
            vmem((views, 9, chunk, LANES), F32),
            dma((6,)),
        ]
        + [dma((owners,)) for _ in range(6)]
        + [dma((views,)) for _ in range(4)],
        compiler_params=pltpu.CompilerParams(
            collective_id=0, has_side_effects=True, vmem_limit_bytes=60 * 1024 * 1024
        ),
        cost_estimate=pl.CostEstimate(
            flops=2_000_000_000, bytes_accessed=4_000_000, transcendentals=300_000
        ),
    )(
        params,
        cam_pos,
        req_ids,
        tile_slots,
        tile_len,
        cotangent.reshape(6 * TILES, LANES),
    )
    image, grads = pl.pallas_call(
        store_kernel,
        out_shape=(
            pltpu.HBM((6 * TILES, LANES), F32),
            pltpu.HBM((count, owned // views), F32),
        ),
        in_specs=[inside] * 2,
        out_specs=(anywhere, anywhere),
        scratch_shapes=[dma((2,))],
    )(image, summed)
    return image.reshape(cotangent.shape), grads


def solution(mesh):
    placed = (
        P(None, "gs"),
        P("view", None),
        P("view", "gs", None, None),
        P("view", "gs", None),
        P("view", "gs"),
        P("view", None, "gs"),
    )
    return jax.shard_map(
        functools.partial(local, mesh.shape["gs"], mesh.shape["view"]),
        mesh=mesh,
        in_specs=placed,
        out_specs=(P("view", None, "gs"), P(None, ("gs", "view"))),
        check_vma=False,
    )
```

```python
import functools

import jax
import jax.numpy as jnp
from jax import lax
from jax.experimental import pallas as pl
from jax.experimental.pallas import tpu as pltpu
from jax.sharding import PartitionSpec as P

MESH = pl.DeviceIdType.MESH
F32 = jnp.float32
BF16 = jnp.bfloat16
TILES = 16
ENTRIES = 64
ROWS = TILES * ENTRIES
PIXELS = 256
CAP = 64
LANES = 128
LINE = 4

focal = 1.2 * 128.0
dilate = 0.3
sh_zero = 0.28209479177387814
sh_one = 0.4886025119029199
sh_two = [
    1.0925484305920792,
    -1.0925484305920792,
    0.31539156525252005,
    -1.0925484305920792,
    0.5462742152960396,
]
sh_three = [
    -0.5900435899266435,
    2.890611442640554,
    -0.4570457994644658,
    0.3731763325901154,
    -0.4570457994644658,
    1.445305721320277,
    -0.5900435899266435,
]


def covariance(log_scales, quat):
    squares = [jnp.exp(2.0 * value) for value in log_scales]
    norm_sq = quat[0] * quat[0] + quat[1] * quat[1] + quat[2] * quat[2] + quat[3] * quat[3]
    inv_norm = 1.0 / jnp.sqrt(norm_sq)
    w, x, y, z = [value * inv_norm for value in quat]
    rotation = [
        [1 - 2 * (y * y + z * z), 2 * (x * y - w * z), 2 * (x * z + w * y)],
        [2 * (x * y + w * z), 1 - 2 * (x * x + z * z), 2 * (y * z - w * x)],
        [2 * (x * z - w * y), 2 * (y * z + w * x), 1 - 2 * (x * x + y * y)],
    ]
    scaled = [[rotation[i][j] * squares[j] for j in range(3)] for i in range(3)]

    def entry(i, j):
        return (
            scaled[i][0] * rotation[j][0]
            + scaled[i][1] * rotation[j][1]
            + scaled[i][2] * rotation[j][2]
        )

    return [entry(0, 0), entry(0, 1), entry(0, 2), entry(1, 1), entry(1, 2), entry(2, 2)]


def geometry(x, y, z, sigma):
    s00, s01, s02, s11, s12, s22 = sigma
    inv_z = 1.0 / z
    jac = focal * inv_z
    center_x = jac * x
    center_y = jac * y
    jac_x = -center_x * inv_z
    jac_y = -center_y * inv_z
    jac_sq = jac * jac
    cov_a = jac_sq * s00 + 2.0 * (jac * jac_x) * s02 + jac_x * jac_x * s22 + dilate
    cov_b = jac_sq * s01 + jac * (jac_y * s02 + jac_x * s12) + jac_x * jac_y * s22
    cov_c = jac_sq * s11 + 2.0 * (jac * jac_y) * s12 + jac_y * jac_y * s22 + dilate
    inv_det = 1.0 / (cov_a * cov_c - cov_b * cov_b)
    return center_x, center_y, cov_c * inv_det, -cov_b * inv_det, cov_a * inv_det


def harmonic_basis(x, y, z):
    inv_distance = 1.0 / jnp.sqrt(x * x + y * y + z * z)
    dx = x * inv_distance
    dy = y * inv_distance
    dz = z * inv_distance
    xx = dx * dx
    yy = dy * dy
    zz = dz * dz
    xy = dx * dy
    yz = dy * dz
    xz = dx * dz
    return [
        -sh_one * dy,
        sh_one * dz,
        -sh_one * dx,
        sh_two[0] * xy,
        sh_two[1] * yz,
        sh_two[2] * (2 * zz - xx - yy),
        sh_two[3] * xz,
        sh_two[4] * (xx - yy),
        sh_three[0] * dy * (3 * xx - yy),
        sh_three[1] * xy * dz,
        sh_three[2] * dy * (4 * zz - xx - yy),
        sh_three[3] * dz * (2 * zz - 3 * xx - 3 * yy),
        sh_three[4] * dx * (4 * zz - xx - yy),
        sh_three[5] * dz * (xx - yy),
        sh_three[6] * dx * (xx - 3 * yy),
    ]


def pieces(value, count):
    out = []
    for at in range(count):
        piece = value.astype(BF16)
        out.append(piece)
        if at + 1 < count:
            value = value - piece.astype(F32)
    return out


def dot(left, right, dims):
    return lax.dot_general(left, right, ((dims[0], dims[1]), ((), ())), preferred_element_type=F32)


def iota(shape, axis):
    return lax.broadcasted_iota(jnp.int32, shape, axis)


def kernel(
    owners,
    views,
    params_ref,
    cam_ref,
    ids_ref,
    slots_ref,
    len_ref,
    cot_ref,
    image,
    summed,
    held,
    asked,
    cam_held,
    slots_held,
    len_held,
    held_cot,
    ids_out,
    ids_in,
    cam_out,
    cam_in,
    table,
    low_hot,
    high_hot,
    feat_out,
    feat_in,
    wide,
    gathered,
    exponent,
    along,
    alpha_all,
    blend_all,
    split_a,
    split_b,
    split_c,
    split_d,
    grad_out,
    grad_in,
    dense,
    view_in,
    load_sem,
    ids_s,
    ids_r,
    feat_s,
    feat_r,
    grad_s,
    grad_r,
    cam_s,
    cam_r,
    view_s,
    view_r,
):
    me = lax.axis_index("gs")
    my_view = lax.axis_index("view")
    my_y = lax.rem(me, LINE)
    my_z = lax.div(me, LINE)
    my_x = lax.div(my_view, 2)
    my_core = lax.rem(my_view, 2)
    planes = owners // LINE
    blocks = held.shape[1]
    chunk = blocks // views

    def plane(i):
        half = (i + 1) // 2
        odd = i % 2
        return lax.rem(my_z + odd * half + (1 - odd) * (planes - half), planes)

    def peers(i, first):
        return [plane(i) * LINE + lax.rem(my_y + step, LINE) for step in range(1 if first else 0, LINE)]

    def view_peer(i):
        pair = i // 2
        step = pair + pair // 2 - 2 * (pair // 3)
        return lax.rem(my_x + step, views // 2) * 2 + lax.rem(my_core + i, 2)

    ids_load = pltpu.make_async_copy(ids_ref.at[0, 0], asked, load_sem.at[2])
    cam_load = pltpu.make_async_copy(cam_ref, cam_held, load_sem.at[3])
    slots_load = pltpu.make_async_copy(slots_ref.at[0], slots_held, load_sem.at[4])
    len_load = pltpu.make_async_copy(len_ref, len_held, load_sem.at[5])
    cot_load = pltpu.make_async_copy(cot_ref, held_cot, load_sem.at[1])
    ids_load.start()
    cam_load.start()

    barrier = pltpu.get_barrier_semaphore()

    def greet(off, carry):
        peer = lax.rem(me + off, owners)
        pl.semaphore_signal(barrier, inc=1, device_id=(my_view, peer), device_id_type=MESH)
        return carry

    lax.fori_loop(1, owners, greet, 0)

    def greet_view(off, carry):
        peer = lax.rem(my_view + off, views)
        pl.semaphore_signal(barrier, inc=1, device_id=(peer, me), device_id_type=MESH)
        return carry

    lax.fori_loop(1, views, greet_view, 0)

    def load_body(j, carry):
        pltpu.make_async_copy(
            params_ref.at[:, pl.ds(pl.multiple_of(j * LANES, LANES), LANES)],
            held.at[:, j, :],
            load_sem.at[0],
        ).start()
        return carry

    lax.fori_loop(0, blocks, load_body, 0)
    slots_load.start()
    len_load.start()
    cot_load.start()

    def ids_copy(to, sender):
        return pltpu.make_async_remote_copy(
            src_ref=ids_out.at[to],
            dst_ref=ids_in.at[sender],
            send_sem=ids_s.at[to],
            recv_sem=ids_r.at[sender],
            device_id=(my_view, to),
            device_id_type=MESH,
        )

    def feat_copy(to, sender):
        return pltpu.make_async_remote_copy(
            src_ref=feat_out.at[to, pl.ds(0, 5)],
            dst_ref=feat_in.at[sender, pl.ds(0, 5)],
            send_sem=feat_s.at[to],
            recv_sem=feat_r.at[sender],
            device_id=(my_view, to),
            device_id_type=MESH,
        )

    def grad_copy(to, sender):
        return pltpu.make_async_remote_copy(
            src_ref=grad_out.at[to, pl.ds(0, 5)],
            dst_ref=grad_in.at[sender, pl.ds(0, 5)],
            send_sem=grad_s.at[to],
            recv_sem=grad_r.at[sender],
            device_id=(my_view, to),
            device_id_type=MESH,
        )

    def cam_copy(to, sender):
        return pltpu.make_async_remote_copy(
            src_ref=cam_out,
            dst_ref=cam_in.at[sender],
            send_sem=cam_s.at[to],
            recv_sem=cam_r.at[sender],
            device_id=(to, me),
            device_id_type=MESH,
        )

    def view_copy(to, sender):
        return pltpu.make_async_remote_copy(
            src_ref=dense.at[:, pl.ds(pl.multiple_of(to * chunk, chunk), chunk), :],
            dst_ref=view_in.at[sender],
            send_sem=view_s.at[to],
            recv_sem=view_r.at[sender],
            device_id=(to, me),
            device_id_type=MESH,
        )

    def wait_sent(copy):
        def body(off, carry):
            copy(lax.rem(me + off, owners), me).wait_send()
            return carry

        lax.fori_loop(1, owners, body, 0)

    ids_load.wait()
    doubled = jnp.concatenate([asked[...], asked[...]], axis=1)
    my_half = (iota(doubled.shape, 1) >> 6) == lax.rem(me, 2)
    ids_out[...] = jnp.where(my_half, doubled, 0).reshape(owners, 1, LANES)
    ids_in[me] = ids_out[me]
    cam_load.wait()
    cam_row = iota((8, LANES), 0)
    cam_tile = jnp.where(
        cam_row == 0, cam_held[0:1, 0:1], jnp.where(cam_row == 1, cam_held[0:1, 1:2], cam_held[0:1, 2:3])
    )
    cam_out[...] = cam_tile
    cam_in[my_view] = cam_tile

    pl.semaphore_wait(barrier, owners + views - 2)

    def ids_body(step, carry):
        for peer in peers(planes - 1 - step, False):
            ids_copy(peer, me).start()
        return carry

    lax.fori_loop(0, planes - 1, ids_body, 0)
    for peer in peers(0, True):
        ids_copy(peer, me).start()

    def cam_send(off, carry):
        cam_copy(lax.rem(my_view + off, views), my_view).start()
        return carry

    lax.fori_loop(1, views, cam_send, 0)

    pltpu.make_async_copy(held, held, load_sem.at[0]).wait()

    def features_body(at, carry):
        rows = pl.ds(pl.multiple_of(at * 16, 16), 16)

        def get(r):
            return held[r, rows, :]

        x = get(0) - cam_out[0:1]
        y = get(1) - cam_out[1:2]
        z = get(2) - cam_out[2:3]
        sigma = covariance([get(3), get(4), get(5)], [get(6), get(7), get(8), get(9)])
        values = list(geometry(x, y, z, sigma))
        values.append(-jnp.log(1.0 + jnp.exp(-get(10))))
        basis = harmonic_basis(x, y, z)
        for c in range(3):
            total = sh_zero * get(11 + 16 * c) + 0.5
            for k in range(15):
                total = total + basis[k] * get(12 + 16 * c + k)
            values.append(total)
        half = lax.div(at, 2)
        inner = lax.rem(at, 2)
        lanes = pl.ds(pl.multiple_of(half * LANES, LANES), LANES)
        for c in range(9):
            for s, piece in enumerate(pieces(values[c], 3)):
                if s < 2 or c < 5:
                    row = s * 288 + c * 32 + inner * 16
                    table[pl.ds(pl.multiple_of(row, 16), 16), lanes] = piece
        return carry

    lax.fori_loop(0, blocks // 16, features_body, 0)

    lane_half = iota((8, LANES), 1) < CAP

    rings = [[i for i in range(planes) if (i + 1) // 2 <= 1]]
    rings += [[i for i in range(planes) if (i + 1) // 2 == far] for far in range(2, planes // 2 + 1)]

    def serve(i):
        base = plane(i) * LINE
        ids = jnp.concatenate(
            [ids_in[base] + ids_in[base + 1], ids_in[base + 2] + ids_in[base + 3]], axis=1
        )
        low = (ids & (LANES - 1)) + ((ids >> 12) << 7)
        high = (ids >> 7) & 31
        lanes = pl.ds(pl.multiple_of(base * CAP, LINE * CAP), LINE * CAP)
        right = (iota((256, LINE * CAP), 0) == low).astype(F32).astype(BF16)
        low_hot[:, lanes] = right
        mask = (iota((32, LINE * CAP), 0) == high).astype(F32)
        high_hot[:, lanes] = mask.astype(BF16)
        short = dot(table[0:288], right, ((1,), (0,))) + dot(table[288:576], right, ((1,), (0,)))
        rest = dot(table[576:736], right, ((1,), (0,)))
        picked = jnp.concatenate([short[0:160] + rest, short[160:]], axis=0)
        rows = [
            jnp.sum(picked[c * 32 : c * 32 + 32] * mask, axis=0, keepdims=True) for c in range(9)
        ]
        blank = jnp.zeros((1, LINE * CAP), F32)
        left_group = jnp.concatenate(rows[0:5] + [blank] * 3, axis=0)
        right_group = jnp.concatenate(rows[5:9] + [blank] * 4, axis=0)
        for part in range(2):
            a = left_group[:, part * LANES : (part + 1) * LANES]
            b = right_group[:, part * LANES : (part + 1) * LANES]
            feat_out[base + 2 * part] = jnp.where(lane_half, a, pltpu.roll(b, CAP, 1))
            feat_out[base + 2 * part + 1] = jnp.where(lane_half, pltpu.roll(a, CAP, 1), b)

    for ring in rings:
        for i in ring:
            for peer in peers(i, i == 0):
                ids_copy(peer, peer).wait_recv()
        for i in ring:
            serve(i)
        for i in ring[::-1]:
            for peer in peers(i, i == 0):
                feat_copy(peer, me).start()
    feat_in[me] = feat_out[me]

    slots_load.wait()
    len_load.wait()
    lane_row = iota((TILES, ROWS), 1)
    tile_hot = (lane_row & 15) == iota((TILES, ROWS), 0)
    tile_mask = tile_hot.astype(F32)
    entry_hot = ((iota((ENTRIES, ROWS), 1) >> 4) == iota((ENTRIES, ROWS), 0)).astype(F32).astype(BF16)
    slots = slots_held[...]
    both = jnp.concatenate([slots >> 6, slots & (CAP - 1)], axis=0).astype(F32).astype(BF16)
    spread = dot(both, entry_hot, ((1,), (0,)))
    owner_row = jnp.sum(spread[0:TILES] * tile_mask, axis=0, keepdims=True)
    place_row = jnp.sum(spread[TILES:] * tile_mask, axis=0, keepdims=True)
    lengths = jnp.broadcast_to(len_held[...], (TILES, TILES)).astype(F32).astype(BF16)
    len_row = dot(lengths, tile_mask.astype(BF16), ((1,), (0,)))[0:1]
    entry_row = iota((1, ROWS), 1)
    live = (entry_row >> 4).astype(F32) < len_row
    place_sub = iota((LANES, ROWS), 0)
    place_left = (place_sub.astype(F32) == place_row).astype(F32).astype(BF16)
    place_right = ((place_sub - CAP).astype(F32) == place_row).astype(F32).astype(BF16)
    center_of_x = (entry_row & 15).astype(F32) * 16.0 + (8.0 - 128.0)
    center_of_y = (me * 16 + 8 - 8 * owners).astype(F32)

    pixel = iota((8, PIXELS), 1)
    mono_x = (pixel & 15).astype(F32) - 7.5
    mono_y = (pixel >> 4).astype(F32) - 7.5
    kind = iota((8, PIXELS), 0)
    monomials = jnp.where(kind == 0, mono_x * mono_x, 0.0)
    monomials = jnp.where(kind == 1, mono_x * mono_y, monomials)
    monomials = jnp.where(kind == 2, mono_y * mono_y, monomials)
    monomials = jnp.where(kind == 3, mono_x, monomials)
    monomials = jnp.where(kind == 4, mono_y, monomials)
    monomials = jnp.where(kind == 5, 1.0, monomials)
    monomials_two = jnp.concatenate([monomials, jnp.zeros_like(monomials)], axis=0).astype(BF16)
    monomials_four = jnp.concatenate([monomials] * 3 + [jnp.zeros_like(monomials)], axis=0).astype(BF16)

    cot_load.wait()
    cot = jnp.concatenate(
        [held_cot[pl.ds(half, 3 * TILES, stride=2), :] for half in range(2)], axis=1
    )
    cot_high, cot_low = pieces(cot, 2)

    halves = [[jnp.zeros((8, 256), F32)] * (ROWS // 256) for _ in range(2)]

    def collect(group):
        for i in group:
            for peer in peers(i, i == 0):
                feat_copy(peer, peer).wait_recv()
        bases = [plane(i) * LINE for i in group]
        arrived = jnp.concatenate(
            [feat_in[pl.ds(base, LINE)].reshape(LINE * 8, LANES) for base in bases], axis=0
        )
        count = arrived.shape[0]
        three = pieces(arrived, 3)
        stacks = [jnp.concatenate(three, axis=0), jnp.concatenate(three[0:2], axis=0)]
        for at in range(ROWS // 256):
            lanes = slice(at * 256, at * 256 + 256)
            owners_here = owner_row[:, lanes]
            for side, hot in enumerate((place_left, place_right)):
                found = dot(stacks[side], hot[:, lanes], ((1,), (0,)))
                summed_pieces = found[0:count] + found[count : 2 * count]
                found = summed_pieces + found[2 * count :] if side == 0 else summed_pieces
                total = halves[side][at]
                for n, base in enumerate(bases):
                    for step in range(LINE):
                        row = (n * LINE + step) * 8
                        here = owners_here == (base + step).astype(F32)
                        total = jnp.where(here, found[row : row + 8], total)
                halves[side][at] = total

    near = (planes * 5 + 7) // 8
    collect(list(range(near)))
    if near < planes:
        collect(list(range(near, planes)))
    left = jnp.concatenate(halves[0], axis=1)
    right = jnp.concatenate(halves[1], axis=1)
    center_x = left[0:1] - center_of_x
    center_y = left[1:2] - center_of_y
    conic_a = left[2:3]
    conic_b = left[3:4]
    conic_c = left[4:5]
    log_opacity = right[0:1]
    colors = [right[1 + c : 2 + c] for c in range(3)]

    lin_x = conic_a * center_x + conic_b * center_y
    lin_y = conic_b * center_x + conic_c * center_y
    blank = jnp.zeros((1, ROWS), F32)
    coefs = jnp.concatenate(
        [
            jnp.where(live, -0.5 * conic_a, 0.0),
            jnp.where(live, -conic_b, 0.0),
            jnp.where(live, -0.5 * conic_c, 0.0),
            jnp.where(live, lin_x, 0.0),
            jnp.where(live, lin_y, 0.0),
            jnp.where(live, log_opacity - 0.5 * (lin_x * center_x + lin_y * center_y), -1000.0),
            blank,
            blank,
        ],
        axis=0,
    )
    coef_pieces = jnp.concatenate(
        [piece.astype(F32) for piece in pieces(coefs, 3)] + [jnp.zeros_like(coefs)], axis=0
    )
    exponent[...] = dot(coef_pieces.T.astype(BF16), monomials_four, ((1,), (0,)))

    spread_color = jnp.concatenate([colors[c] * tile_mask for c in range(3)], axis=0)
    color_high, color_low = pieces(spread_color, 2)
    color_sides = jnp.concatenate([color_high, color_high, color_low], axis=0)
    cot_sides = jnp.concatenate([cot_high, cot_low, cot_high], axis=0)
    along[...] = dot(color_sides, cot_sides, ((0,), (0,)))

    def forward_body(k, through):
        rows = pl.ds(pl.multiple_of(k * TILES, TILES), TILES)
        alpha = jnp.exp(exponent[rows, :])
        blend = through * alpha
        alpha_all[rows, :] = alpha
        blend_all[rows, :] = blend
        high, low = pieces(blend, 2)
        split_a[rows, :] = high
        split_b[rows, :] = low
        return through - blend

    lax.fori_loop(0, ENTRIES, forward_body, jnp.ones((TILES, PIXELS), F32), unroll=True)

    cot_both = jnp.concatenate([cot_high, cot_low], axis=0)
    by_color = dot(cot_both, split_a[...], ((1,), (1,)))
    by_color = (
        by_color[0 : 3 * TILES]
        + by_color[3 * TILES :]
        + dot(cot_high, split_b[...], ((1,), (1,)))
    )

    def backward_body(step, behind):
        rows = pl.ds(pl.multiple_of((ENTRIES - 1 - step) * TILES, TILES), TILES)
        gain = along[rows, :] - behind
        high, low = pieces(blend_all[rows, :] * gain, 2)
        split_c[rows, :] = high
        split_d[rows, :] = low
        return behind + alpha_all[rows, :] * gain

    lax.fori_loop(0, ENTRIES, backward_body, jnp.zeros((TILES, PIXELS), F32), unroll=True)

    moments = dot(monomials_two, split_c[...], ((1,), (1,))) + dot(
        monomials_two, split_d[...], ((1,), (1,))
    )
    grad_colors = [
        jnp.sum(by_color[c * TILES : (c + 1) * TILES] * tile_mask, axis=0, keepdims=True)
        for c in range(3)
    ]
    m_xx, m_xy, m_yy, m_x, m_y, m_one = [moments[row : row + 1] for row in range(6)]
    off_x = m_x - center_x * m_one
    off_y = m_y - center_y * m_one
    off_xx = m_xx - center_x * (m_x + off_x)
    off_xy = m_xy - center_x * m_y - center_y * off_x
    off_yy = m_yy - center_y * (m_y + off_y)
    entry_grads = jnp.concatenate(
        [
            conic_a * off_x + conic_b * off_y,
            conic_b * off_x + conic_c * off_y,
            -0.5 * off_xx,
            -off_xy,
            -0.5 * off_yy,
            blank,
            blank,
            blank,
            m_one,
            grad_colors[0],
            grad_colors[1],
            grad_colors[2],
            blank,
            blank,
            blank,
            blank,
        ],
        axis=0,
    )
    grad_high, grad_low = pieces(entry_grads, 2)

    place_both = place_left + place_right
    owner_wide = jnp.broadcast_to(owner_row, (16, ROWS)).astype(BF16)
    nothing = jnp.zeros((16, ROWS), BF16)
    lane_half_all = iota((LINE, 8, LANES), 2) < CAP

    def give(group):
        parts = []
        for piece in (grad_high, grad_low):
            for i in group:
                for step in range(LINE):
                    here = owner_wide == (plane(i) * LINE + step).astype(F32).astype(BF16)
                    parts.append(jnp.where(here, piece, nothing))
        by_slot = dot(jnp.concatenate(parts, axis=0), place_both, ((1,), (1,)))
        half_rows = 16 * LINE * len(group)
        by_slot = by_slot[0:half_rows] + by_slot[half_rows:]
        for n, i in enumerate(group):
            mine = by_slot[n * LINE * 16 : (n + 1) * LINE * 16].reshape(LINE, 16, LANES)
            packed = jnp.where(lane_half_all, mine[:, 0:8], mine[:, 8:16])
            grad_out[pl.ds(plane(i) * LINE, LINE)] = packed
        for i in group:
            for peer in peers(i, i == 0):
                grad_copy(peer, me).start()

    for ring in rings[::-1]:
        give(ring[::-1])
    grad_in[me] = grad_out[me]

    color_both = jnp.concatenate([color_high, color_low], axis=0)
    shown = dot(color_both, split_a[...], ((1,), (0,)))
    shown = (
        shown[0 : 3 * TILES]
        + shown[3 * TILES :]
        + dot(color_high, split_b[...], ((1,), (0,)))
    )
    for half in range(2):
        image[pl.ds(half, 3 * TILES, stride=2), :] = shown[:, half * LANES : half * LANES + LANES]

    wait_sent(ids_copy)
    wait_sent(feat_copy)

    def scatter(ring):
        for i in ring:
            for peer in peers(i, i == 0):
                grad_copy(peer, peer).wait_recv()
        hots = []
        for n, i in enumerate(ring):
            base = plane(i) * LINE
            lanes = pl.ds(pl.multiple_of(base * CAP, LINE * CAP), LINE * CAP)
            tops = []
            bottoms = []
            for part in range(2):
                even = grad_in[base + 2 * part]
                odd = grad_in[base + 2 * part + 1]
                tops.append(jnp.where(lane_half, even, pltpu.roll(odd, CAP, 1)))
                bottoms.append(jnp.where(lane_half, pltpu.roll(even, CAP, 1), odd))
            a = jnp.concatenate(tops, axis=1)
            b = jnp.concatenate(bottoms, axis=1)
            mask = high_hot[:, lanes]
            into = slice(n * LINE * CAP, (n + 1) * LINE * CAP)
            for c in range(9):
                row = a[c : c + 1] if c < 5 else b[c - 5 : c - 4]
                for s, piece in enumerate(pieces(jnp.broadcast_to(row, (32, LINE * CAP)), 2)):
                    wide[s * 288 + c * 32 : s * 288 + c * 32 + 32, into] = piece * mask
            hots.append(low_hot[:, lanes])
        placed = dot(wide[:, 0 : len(ring) * LINE * CAP], jnp.concatenate(hots, axis=1), ((1,), (1,)))
        return placed[0:288] + placed[288:576]

    for ring in rings[:-1]:
        if ring[0] == 0:
            gathered[...] = scatter(ring)
        else:
            gathered[...] += scatter(ring)
    placed = scatter(rings[-1])
    if len(rings) > 1:
        placed = placed + gathered[...]
    placed = placed.reshape(9, 32, 256)
    dense[:, 0:32, :] = placed[:, :, 0:LANES]
    dense[:, 32:64, :] = placed[:, :, LANES:256]

    def view_send(step, carry):
        view_copy(view_peer(views - 1 - step), my_view).start()
        return carry

    lax.fori_loop(0, views - 1, view_send, 0)
    mine = pl.ds(pl.multiple_of(my_view * chunk, chunk), chunk)
    view_in[my_view] = dense[:, mine, :]

    def cam_wait(off, carry):
        peer = lax.rem(my_view + off, views)
        cam_copy(peer, peer).wait_recv()
        cam_copy(peer, my_view).wait_send()
        return carry

    lax.fori_loop(1, views, cam_wait, 0)
    wait_sent(grad_copy)

    def get(r):
        return held[r, mine, :]

    scale_quat = [get(r) for r in range(3, 10)]

    def shape_of(values):
        return covariance(values[0:3], values[3:7])

    sigma, shape_back = jax.vjp(shape_of, scale_quat)
    zero = jnp.zeros((chunk, LANES), F32)
    for r in range(59):
        summed[r] = zero

    def add_view(v, totals):
        camera = cam_in[v]
        x = get(0) - camera[0:1]
        y = get(1) - camera[1:2]
        z = get(2) - camera[2:3]
        grads = [view_in[v, c] for c in range(9)]
        _, geometry_back = jax.vjp(geometry, x, y, z, sigma)
        gx, gy, gz, g_sigma = geometry_back(tuple(grads[0:5]))
        basis, basis_back = jax.vjp(harmonic_basis, x, y, z)
        g_basis = [zero] * 15
        for c in range(3):
            color_grad = grads[6 + c]
            summed[11 + 16 * c] += sh_zero * color_grad
            for k in range(15):
                row = 12 + 16 * c + k
                summed[row] += basis[k] * color_grad
                g_basis[k] = g_basis[k] + get(row) * color_grad
        hx, hy, hz = basis_back(g_basis)
        add = [gx + hx, gy + hy, gz + hz, grads[5]] + list(g_sigma)
        return tuple(t + a for t, a in zip(totals, add))

    def view_body(i, totals):
        peer = view_peer(i)
        view_copy(peer, peer).wait_recv()
        return add_view(peer, totals)

    totals = add_view(my_view, tuple([zero] * 10))
    totals = lax.fori_loop(1, views, view_body, totals)
    for r in range(3):
        summed[r] = totals[r]
    (by_shape,) = shape_back(list(totals[4:10]))
    for r in range(7):
        summed[3 + r] = by_shape[r]
    summed[10] = totals[3] / (1.0 + jnp.exp(get(10)))

    def view_wait(off, carry):
        view_copy(lax.rem(my_view + off, views), my_view).wait_send()
        return carry

    lax.fori_loop(1, views, view_wait, 0)


def store_kernel(image, summed, image_ref, grads_ref, sems):
    image_store = pltpu.make_async_copy(image, image_ref, sems.at[0])
    image_store.start()
    for j in range(summed.shape[1]):
        pltpu.make_async_copy(
            summed.at[:, j, :], grads_ref.at[:, j * LANES : (j + 1) * LANES], sems.at[1]
        ).start()
    image_store.wait()
    pltpu.make_async_copy(summed, summed, sems.at[1]).wait()


def local(owners, views, params, cam_pos, req_ids, tile_slots, tile_len, cotangent):
    count, owned = params.shape
    blocks = owned // LANES
    chunk = blocks // views
    slots_all = owners * CAP
    vmem = pltpu.VMEM
    dma = pltpu.SemaphoreType.DMA
    anywhere = pl.BlockSpec(memory_space=pl.ANY)
    inside = pl.BlockSpec(memory_space=vmem)
    image, summed = pl.pallas_call(
        functools.partial(kernel, owners, views),
        out_shape=(
            vmem((6 * TILES, LANES), F32),
            vmem((count, chunk, LANES), F32),
        ),
        in_specs=[anywhere] * 6,
        out_specs=(inside, inside),
        scratch_shapes=[
            vmem((count, blocks, LANES), F32),
            vmem((owners, CAP), jnp.int32),
            vmem((1, 3), F32),
            vmem((TILES, ENTRIES), jnp.int32),
            vmem((1, TILES), jnp.int32),
            vmem((6 * TILES, LANES), F32),
            vmem((owners, 1, LANES), jnp.int32),
            vmem((owners, 1, LANES), jnp.int32),
            vmem((8, LANES), F32),
            vmem((views, 8, LANES), F32),
            vmem((736, 256), BF16),
            vmem((256, slots_all), BF16),
            vmem((32, slots_all), BF16),
            vmem((owners, 8, LANES), F32),
            vmem((owners, 8, LANES), F32),
            vmem((576, 3 * LINE * CAP), BF16),
            vmem((288, 256), F32),
            vmem((ROWS, PIXELS), F32),
            vmem((ROWS, PIXELS), F32),
            vmem((ROWS, PIXELS), F32),
            vmem((ROWS, PIXELS), F32),
            vmem((ROWS, PIXELS), BF16),
            vmem((ROWS, PIXELS), BF16),
            vmem((ROWS, PIXELS), BF16),
            vmem((ROWS, PIXELS), BF16),
            vmem((owners, 8, LANES), F32),
            vmem((owners, 8, LANES), F32),
            vmem((9, blocks, LANES), F32),
            vmem((views, 9, chunk, LANES), F32),
            dma((6,)),
        ]
        + [dma((owners,)) for _ in range(6)]
        + [dma((views,)) for _ in range(4)],
        compiler_params=pltpu.CompilerParams(
            collective_id=0, has_side_effects=True, vmem_limit_bytes=60 * 1024 * 1024
        ),
        cost_estimate=pl.CostEstimate(
            flops=2_000_000_000, bytes_accessed=4_000_000, transcendentals=300_000
        ),
    )(
        params,
        cam_pos,
        req_ids,
        tile_slots,
        tile_len,
        cotangent.reshape(6 * TILES, LANES),
    )
    image, grads = pl.pallas_call(
        store_kernel,
        out_shape=(
            pltpu.HBM((6 * TILES, LANES), F32),
            pltpu.HBM((count, owned // views), F32),
        ),
        in_specs=[inside] * 2,
        out_specs=(anywhere, anywhere),
        scratch_shapes=[dma((2,))],
        compiler_params=pltpu.CompilerParams(vmem_limit_bytes=4 * 1024 * 1024),
    )(image, summed)
    return image.reshape(cotangent.shape), grads


def solution(mesh):
    placed = (
        P(None, "gs"),
        P("view", None),
        P("view", "gs", None, None),
        P("view", "gs", None),
        P("view", "gs"),
        P("view", None, "gs"),
    )
    return jax.shard_map(
        functools.partial(local, mesh.shape["gs"], mesh.shape["view"]),
        mesh=mesh,
        in_specs=placed,
        out_specs=(P("view", None, "gs"), P(None, ("gs", "view"))),
        check_vma=False,
    )
```

```python
import functools

import jax
import jax.numpy as jnp
from jax import lax
from jax.experimental import pallas as pl
from jax.experimental.pallas import tpu as pltpu
from jax.sharding import PartitionSpec as P

MESH = pl.DeviceIdType.MESH
F32 = jnp.float32
BF16 = jnp.bfloat16
TILES = 16
ENTRIES = 64
ROWS = TILES * ENTRIES
PIXELS = 256
CAP = 64
LANES = 128
LINE = 4

focal = 1.2 * 128.0
dilate = 0.3
sh_zero = 0.28209479177387814
sh_one = 0.4886025119029199
sh_two = [
    1.0925484305920792,
    -1.0925484305920792,
    0.31539156525252005,
    -1.0925484305920792,
    0.5462742152960396,
]
sh_three = [
    -0.5900435899266435,
    2.890611442640554,
    -0.4570457994644658,
    0.3731763325901154,
    -0.4570457994644658,
    1.445305721320277,
    -0.5900435899266435,
]


def covariance(log_scales, quat):
    squares = [jnp.exp(2.0 * value) for value in log_scales]
    norm_sq = quat[0] * quat[0] + quat[1] * quat[1] + quat[2] * quat[2] + quat[3] * quat[3]
    inv_norm = 1.0 / jnp.sqrt(norm_sq)
    w, x, y, z = [value * inv_norm for value in quat]
    rotation = [
        [1 - 2 * (y * y + z * z), 2 * (x * y - w * z), 2 * (x * z + w * y)],
        [2 * (x * y + w * z), 1 - 2 * (x * x + z * z), 2 * (y * z - w * x)],
        [2 * (x * z - w * y), 2 * (y * z + w * x), 1 - 2 * (x * x + y * y)],
    ]
    scaled = [[rotation[i][j] * squares[j] for j in range(3)] for i in range(3)]

    def entry(i, j):
        return (
            scaled[i][0] * rotation[j][0]
            + scaled[i][1] * rotation[j][1]
            + scaled[i][2] * rotation[j][2]
        )

    return [entry(0, 0), entry(0, 1), entry(0, 2), entry(1, 1), entry(1, 2), entry(2, 2)]


def geometry(x, y, z, sigma):
    s00, s01, s02, s11, s12, s22 = sigma
    inv_z = 1.0 / z
    jac = focal * inv_z
    center_x = jac * x
    center_y = jac * y
    jac_x = -center_x * inv_z
    jac_y = -center_y * inv_z
    jac_sq = jac * jac
    cov_a = jac_sq * s00 + 2.0 * (jac * jac_x) * s02 + jac_x * jac_x * s22 + dilate
    cov_b = jac_sq * s01 + jac * (jac_y * s02 + jac_x * s12) + jac_x * jac_y * s22
    cov_c = jac_sq * s11 + 2.0 * (jac * jac_y) * s12 + jac_y * jac_y * s22 + dilate
    inv_det = 1.0 / (cov_a * cov_c - cov_b * cov_b)
    return center_x, center_y, cov_c * inv_det, -cov_b * inv_det, cov_a * inv_det


def harmonic_basis(x, y, z):
    inv_distance = 1.0 / jnp.sqrt(x * x + y * y + z * z)
    dx = x * inv_distance
    dy = y * inv_distance
    dz = z * inv_distance
    xx = dx * dx
    yy = dy * dy
    zz = dz * dz
    xy = dx * dy
    yz = dy * dz
    xz = dx * dz
    return [
        -sh_one * dy,
        sh_one * dz,
        -sh_one * dx,
        sh_two[0] * xy,
        sh_two[1] * yz,
        sh_two[2] * (2 * zz - xx - yy),
        sh_two[3] * xz,
        sh_two[4] * (xx - yy),
        sh_three[0] * dy * (3 * xx - yy),
        sh_three[1] * xy * dz,
        sh_three[2] * dy * (4 * zz - xx - yy),
        sh_three[3] * dz * (2 * zz - 3 * xx - 3 * yy),
        sh_three[4] * dx * (4 * zz - xx - yy),
        sh_three[5] * dz * (xx - yy),
        sh_three[6] * dx * (xx - 3 * yy),
    ]


def pieces(value, count):
    out = []
    for at in range(count):
        piece = value.astype(BF16)
        out.append(piece)
        if at + 1 < count:
            value = value - piece.astype(F32)
    return out


def dot(left, right, dims):
    return lax.dot_general(left, right, ((dims[0], dims[1]), ((), ())), preferred_element_type=F32)


def iota(shape, axis):
    return lax.broadcasted_iota(jnp.int32, shape, axis)


def kernel(
    owners,
    views,
    params_ref,
    cam_ref,
    ids_ref,
    slots_ref,
    len_ref,
    cot_ref,
    image,
    summed,
    held,
    asked,
    cam_held,
    slots_held,
    len_held,
    held_cot,
    ids_out,
    ids_in,
    cam_out,
    cam_in,
    table,
    low_hot,
    high_hot,
    feat_out,
    feat_in,
    wide,
    gathered,
    exponent,
    along,
    alpha_all,
    blend_all,
    split_a,
    split_b,
    split_c,
    split_d,
    grad_out,
    grad_in,
    dense,
    view_in,
    load_sem,
    ids_s,
    ids_r,
    feat_s,
    feat_r,
    grad_s,
    grad_r,
    cam_s,
    cam_r,
    view_s,
    view_r,
):
    me = lax.axis_index("gs")
    my_view = lax.axis_index("view")
    my_y = lax.rem(me, LINE)
    my_z = lax.div(me, LINE)
    my_x = lax.div(my_view, 2)
    my_core = lax.rem(my_view, 2)
    planes = owners // LINE
    blocks = held.shape[1]
    chunk = blocks // views

    def plane(i):
        half = (i + 1) // 2
        odd = i % 2
        return lax.rem(my_z + odd * half + (1 - odd) * (planes - half), planes)

    def peers(i, first):
        return [plane(i) * LINE + lax.rem(my_y + step, LINE) for step in range(1 if first else 0, LINE)]

    def view_peer(i):
        pair = i // 2
        step = pair + pair // 2 - 2 * (pair // 3)
        return lax.rem(my_x + step, views // 2) * 2 + lax.rem(my_core + i, 2)

    ids_load = pltpu.make_async_copy(ids_ref.at[0, 0], asked, load_sem.at[2])
    cam_load = pltpu.make_async_copy(cam_ref, cam_held, load_sem.at[3])
    slots_load = pltpu.make_async_copy(slots_ref.at[0], slots_held, load_sem.at[4])
    len_load = pltpu.make_async_copy(len_ref, len_held, load_sem.at[5])
    cot_load = pltpu.make_async_copy(cot_ref, held_cot, load_sem.at[1])
    ids_load.start()
    cam_load.start()

    barrier = pltpu.get_barrier_semaphore()

    def greet(off, carry):
        peer = lax.rem(me + off, owners)
        pl.semaphore_signal(barrier, inc=1, device_id=(my_view, peer), device_id_type=MESH)
        return carry

    lax.fori_loop(1, owners, greet, 0)

    def greet_view(off, carry):
        peer = lax.rem(my_view + off, views)
        pl.semaphore_signal(barrier, inc=1, device_id=(peer, me), device_id_type=MESH)
        return carry

    lax.fori_loop(1, views, greet_view, 0)

    def load_body(j, carry):
        pltpu.make_async_copy(
            params_ref.at[:, pl.ds(pl.multiple_of(j * LANES, LANES), LANES)],
            held.at[:, j, :],
            load_sem.at[0],
        ).start()
        return carry

    lax.fori_loop(0, blocks, load_body, 0)
    slots_load.start()
    len_load.start()
    cot_load.start()

    def ids_copy(to, sender):
        return pltpu.make_async_remote_copy(
            src_ref=ids_out.at[to],
            dst_ref=ids_in.at[sender],
            send_sem=ids_s.at[to],
            recv_sem=ids_r.at[sender],
            device_id=(my_view, to),
            device_id_type=MESH,
        )

    def feat_copy(to, sender):
        return pltpu.make_async_remote_copy(
            src_ref=feat_out.at[to, pl.ds(0, 5)],
            dst_ref=feat_in.at[sender, pl.ds(0, 5)],
            send_sem=feat_s.at[to],
            recv_sem=feat_r.at[sender],
            device_id=(my_view, to),
            device_id_type=MESH,
        )

    def grad_copy(to, sender):
        return pltpu.make_async_remote_copy(
            src_ref=grad_out.at[to, pl.ds(0, 5)],
            dst_ref=grad_in.at[sender, pl.ds(0, 5)],
            send_sem=grad_s.at[to],
            recv_sem=grad_r.at[sender],
            device_id=(my_view, to),
            device_id_type=MESH,
        )

    def cam_copy(to, sender):
        return pltpu.make_async_remote_copy(
            src_ref=cam_out,
            dst_ref=cam_in.at[sender],
            send_sem=cam_s.at[to],
            recv_sem=cam_r.at[sender],
            device_id=(to, me),
            device_id_type=MESH,
        )

    def view_copy(to, sender):
        return pltpu.make_async_remote_copy(
            src_ref=dense.at[:, pl.ds(pl.multiple_of(to * chunk, chunk), chunk), :],
            dst_ref=view_in.at[sender],
            send_sem=view_s.at[to],
            recv_sem=view_r.at[sender],
            device_id=(to, me),
            device_id_type=MESH,
        )

    def wait_sent(copy):
        def body(off, carry):
            copy(lax.rem(me + off, owners), me).wait_send()
            return carry

        lax.fori_loop(1, owners, body, 0)

    ids_load.wait()
    doubled = jnp.concatenate([asked[...], asked[...]], axis=1)
    my_half = (iota(doubled.shape, 1) >> 6) == lax.rem(me, 2)
    ids_out[...] = jnp.where(my_half, doubled, 0).reshape(owners, 1, LANES)
    ids_in[me] = ids_out[me]
    cam_load.wait()
    cam_row = iota((8, LANES), 0)
    cam_tile = jnp.where(
        cam_row == 0, cam_held[0:1, 0:1], jnp.where(cam_row == 1, cam_held[0:1, 1:2], cam_held[0:1, 2:3])
    )
    cam_out[...] = cam_tile
    cam_in[my_view] = cam_tile

    pl.semaphore_wait(barrier, owners + views - 2)

    def ids_body(step, carry):
        for peer in peers(planes - 1 - step, False):
            ids_copy(peer, me).start()
        return carry

    lax.fori_loop(0, planes - 1, ids_body, 0)
    for peer in peers(0, True):
        ids_copy(peer, me).start()

    def cam_send(off, carry):
        cam_copy(lax.rem(my_view + off, views), my_view).start()
        return carry

    lax.fori_loop(1, views, cam_send, 0)

    pltpu.make_async_copy(held, held, load_sem.at[0]).wait()

    def features_body(at, carry):
        rows = pl.ds(pl.multiple_of(at * 16, 16), 16)

        def get(r):
            return held[r, rows, :]

        x = get(0) - cam_out[0:1]
        y = get(1) - cam_out[1:2]
        z = get(2) - cam_out[2:3]
        sigma = covariance([get(3), get(4), get(5)], [get(6), get(7), get(8), get(9)])
        values = list(geometry(x, y, z, sigma))
        values.append(-jnp.log(1.0 + jnp.exp(-get(10))))
        basis = harmonic_basis(x, y, z)
        for c in range(3):
            total = sh_zero * get(11 + 16 * c) + 0.5
            for k in range(15):
                total = total + basis[k] * get(12 + 16 * c + k)
            values.append(total)
        half = lax.div(at, 2)
        inner = lax.rem(at, 2)
        lanes = pl.ds(pl.multiple_of(half * LANES, LANES), LANES)
        for c in range(9):
            for s, piece in enumerate(pieces(values[c], 3)):
                if s < 2 or c < 5:
                    row = s * 288 + c * 32 + inner * 16
                    table[pl.ds(pl.multiple_of(row, 16), 16), lanes] = piece
        return carry

    lax.fori_loop(0, blocks // 16, features_body, 0)

    lane_half = iota((8, LANES), 1) < CAP

    rings = [[i for i in range(planes) if (i + 1) // 2 <= 1]]
    rings += [[i for i in range(planes) if (i + 1) // 2 == far] for far in range(2, planes // 2 + 1)]

    def serve(i):
        base = plane(i) * LINE
        ids = jnp.concatenate(
            [ids_in[base] + ids_in[base + 1], ids_in[base + 2] + ids_in[base + 3]], axis=1
        )
        low = (ids & (LANES - 1)) + ((ids >> 12) << 7)
        high = (ids >> 7) & 31
        lanes = pl.ds(pl.multiple_of(base * CAP, LINE * CAP), LINE * CAP)
        right = (iota((256, LINE * CAP), 0) == low).astype(F32).astype(BF16)
        low_hot[:, lanes] = right
        mask = (iota((32, LINE * CAP), 0) == high).astype(F32)
        high_hot[:, lanes] = mask.astype(BF16)
        short = dot(table[0:288], right, ((1,), (0,))) + dot(table[288:576], right, ((1,), (0,)))
        rest = dot(table[576:736], right, ((1,), (0,)))
        picked = jnp.concatenate([short[0:160] + rest, short[160:]], axis=0)
        rows = [
            jnp.sum(picked[c * 32 : c * 32 + 32] * mask, axis=0, keepdims=True) for c in range(9)
        ]
        blank = jnp.zeros((1, LINE * CAP), F32)
        left_group = jnp.concatenate(rows[0:5] + [blank] * 3, axis=0)
        right_group = jnp.concatenate(rows[5:9] + [blank] * 4, axis=0)
        for part in range(2):
            a = left_group[:, part * LANES : (part + 1) * LANES]
            b = right_group[:, part * LANES : (part + 1) * LANES]
            feat_out[base + 2 * part] = jnp.where(lane_half, a, pltpu.roll(b, CAP, 1))
            feat_out[base + 2 * part + 1] = jnp.where(lane_half, pltpu.roll(a, CAP, 1), b)

    for ring in rings:
        for i in ring:
            for peer in peers(i, i == 0):
                ids_copy(peer, peer).wait_recv()
        for i in ring:
            serve(i)
        for i in ring[::-1]:
            for peer in peers(i, i == 0):
                feat_copy(peer, me).start()
    feat_in[me] = feat_out[me]

    slots_load.wait()
    len_load.wait()
    lane_row = iota((TILES, ROWS), 1)
    tile_hot = (lane_row & 15) == iota((TILES, ROWS), 0)
    tile_mask = tile_hot.astype(F32)
    entry_hot = ((iota((ENTRIES, ROWS), 1) >> 4) == iota((ENTRIES, ROWS), 0)).astype(F32).astype(BF16)
    slots = slots_held[...]
    both = jnp.concatenate([slots >> 6, slots & (CAP - 1)], axis=0).astype(F32).astype(BF16)
    spread = dot(both, entry_hot, ((1,), (0,)))
    owner_row = jnp.sum(spread[0:TILES] * tile_mask, axis=0, keepdims=True)
    place_row = jnp.sum(spread[TILES:] * tile_mask, axis=0, keepdims=True)
    lengths = jnp.broadcast_to(len_held[...], (TILES, TILES)).astype(F32).astype(BF16)
    len_row = dot(lengths, tile_mask.astype(BF16), ((1,), (0,)))[0:1]
    entry_row = iota((1, ROWS), 1)
    live = (entry_row >> 4).astype(F32) < len_row
    place_sub = iota((LANES, ROWS), 0)
    place_left = (place_sub.astype(F32) == place_row).astype(F32).astype(BF16)
    place_right = ((place_sub - CAP).astype(F32) == place_row).astype(F32).astype(BF16)
    center_of_x = (entry_row & 15).astype(F32) * 16.0 + (8.0 - 128.0)
    center_of_y = (me * 16 + 8 - 8 * owners).astype(F32)

    pixel = iota((8, PIXELS), 1)
    mono_x = (pixel & 15).astype(F32) - 7.5
    mono_y = (pixel >> 4).astype(F32) - 7.5
    kind = iota((8, PIXELS), 0)
    monomials = jnp.where(kind == 0, mono_x * mono_x, 0.0)
    monomials = jnp.where(kind == 1, mono_x * mono_y, monomials)
    monomials = jnp.where(kind == 2, mono_y * mono_y, monomials)
    monomials = jnp.where(kind == 3, mono_x, monomials)
    monomials = jnp.where(kind == 4, mono_y, monomials)
    monomials = jnp.where(kind == 5, 1.0, monomials)
    monomials_two = jnp.concatenate([monomials, jnp.zeros_like(monomials)], axis=0).astype(BF16)
    monomials_four = jnp.concatenate([monomials] * 3 + [jnp.zeros_like(monomials)], axis=0).astype(BF16)

    cot_load.wait()
    cot = jnp.concatenate(
        [held_cot[pl.ds(half, 3 * TILES, stride=2), :] for half in range(2)], axis=1
    )
    cot_high, cot_low = pieces(cot, 2)

    halves = [[jnp.zeros((8, 256), F32)] * (ROWS // 256) for _ in range(2)]

    def collect(group):
        for i in group:
            for peer in peers(i, i == 0):
                feat_copy(peer, peer).wait_recv()
        bases = [plane(i) * LINE for i in group]
        arrived = jnp.concatenate(
            [feat_in[pl.ds(base, LINE)].reshape(LINE * 8, LANES) for base in bases], axis=0
        )
        count = arrived.shape[0]
        three = pieces(arrived, 3)
        stacks = [jnp.concatenate(three, axis=0), jnp.concatenate(three[0:2], axis=0)]
        for at in range(ROWS // 256):
            lanes = slice(at * 256, at * 256 + 256)
            owners_here = owner_row[:, lanes]
            for side, hot in enumerate((place_left, place_right)):
                found = dot(stacks[side], hot[:, lanes], ((1,), (0,)))
                summed_pieces = found[0:count] + found[count : 2 * count]
                found = summed_pieces + found[2 * count :] if side == 0 else summed_pieces
                total = halves[side][at]
                for n, base in enumerate(bases):
                    for step in range(LINE):
                        row = (n * LINE + step) * 8
                        here = owners_here == (base + step).astype(F32)
                        total = jnp.where(here, found[row : row + 8], total)
                halves[side][at] = total

    near = (planes * 5 + 7) // 8
    collect(list(range(near)))
    if near < planes:
        collect(list(range(near, planes)))
    left = jnp.concatenate(halves[0], axis=1)
    right = jnp.concatenate(halves[1], axis=1)
    center_x = left[0:1] - center_of_x
    center_y = left[1:2] - center_of_y
    conic_a = left[2:3]
    conic_b = left[3:4]
    conic_c = left[4:5]
    log_opacity = right[0:1]
    colors = [right[1 + c : 2 + c] for c in range(3)]

    lin_x = conic_a * center_x + conic_b * center_y
    lin_y = conic_b * center_x + conic_c * center_y
    blank = jnp.zeros((1, ROWS), F32)
    coefs = jnp.concatenate(
        [
            jnp.where(live, -0.5 * conic_a, 0.0),
            jnp.where(live, -conic_b, 0.0),
            jnp.where(live, -0.5 * conic_c, 0.0),
            jnp.where(live, lin_x, 0.0),
            jnp.where(live, lin_y, 0.0),
            jnp.where(live, log_opacity - 0.5 * (lin_x * center_x + lin_y * center_y), -1000.0),
            blank,
            blank,
        ],
        axis=0,
    )
    coef_pieces = jnp.concatenate(
        [piece.astype(F32) for piece in pieces(coefs, 3)] + [jnp.zeros_like(coefs)], axis=0
    )
    exponent[...] = dot(coef_pieces.T.astype(BF16), monomials_four, ((1,), (0,)))

    spread_color = jnp.concatenate([colors[c] * tile_mask for c in range(3)], axis=0)
    color_high, color_low = pieces(spread_color, 2)
    color_sides = jnp.concatenate([color_high, color_high, color_low], axis=0)
    cot_sides = jnp.concatenate([cot_high, cot_low, cot_high], axis=0)
    along[...] = dot(color_sides, cot_sides, ((0,), (0,)))

    def forward_body(k, through):
        rows = pl.ds(pl.multiple_of(k * TILES, TILES), TILES)
        alpha = jnp.exp(exponent[rows, :])
        blend = through * alpha
        alpha_all[rows, :] = alpha
        blend_all[rows, :] = blend
        high, low = pieces(blend, 2)
        split_a[rows, :] = high
        split_b[rows, :] = low
        return through - blend

    lax.fori_loop(0, ENTRIES, forward_body, jnp.ones((TILES, PIXELS), F32), unroll=True)

    cot_both = jnp.concatenate([cot_high, cot_low], axis=0)
    by_color = dot(cot_both, split_a[...], ((1,), (1,)))
    by_color = (
        by_color[0 : 3 * TILES]
        + by_color[3 * TILES :]
        + dot(cot_high, split_b[...], ((1,), (1,)))
    )

    def backward_body(step, behind):
        rows = pl.ds(pl.multiple_of((ENTRIES - 1 - step) * TILES, TILES), TILES)
        gain = along[rows, :] - behind
        high, low = pieces(blend_all[rows, :] * gain, 2)
        split_c[rows, :] = high
        split_d[rows, :] = low
        return behind + alpha_all[rows, :] * gain

    lax.fori_loop(0, ENTRIES, backward_body, jnp.zeros((TILES, PIXELS), F32), unroll=True)

    moments = dot(monomials_two, split_c[...], ((1,), (1,))) + dot(
        monomials_two, split_d[...], ((1,), (1,))
    )
    grad_colors = [
        jnp.sum(by_color[c * TILES : (c + 1) * TILES] * tile_mask, axis=0, keepdims=True)
        for c in range(3)
    ]
    m_xx, m_xy, m_yy, m_x, m_y, m_one = [moments[row : row + 1] for row in range(6)]
    off_x = m_x - center_x * m_one
    off_y = m_y - center_y * m_one
    off_xx = m_xx - center_x * (m_x + off_x)
    off_xy = m_xy - center_x * m_y - center_y * off_x
    off_yy = m_yy - center_y * (m_y + off_y)
    entry_grads = jnp.concatenate(
        [
            conic_a * off_x + conic_b * off_y,
            conic_b * off_x + conic_c * off_y,
            -0.5 * off_xx,
            -off_xy,
            -0.5 * off_yy,
            blank,
            blank,
            blank,
            m_one,
            grad_colors[0],
            grad_colors[1],
            grad_colors[2],
            blank,
            blank,
            blank,
            blank,
        ],
        axis=0,
    )
    grad_high, grad_low = pieces(entry_grads, 2)

    place_both = place_left + place_right
    owner_wide = jnp.broadcast_to(owner_row, (16, ROWS)).astype(BF16)
    nothing = jnp.zeros((16, ROWS), BF16)
    lane_half_all = iota((LINE, 8, LANES), 2) < CAP

    def give(group):
        parts = []
        for piece in (grad_high, grad_low):
            for i in group:
                for step in range(LINE):
                    here = owner_wide == (plane(i) * LINE + step).astype(F32).astype(BF16)
                    parts.append(jnp.where(here, piece, nothing))
        by_slot = dot(jnp.concatenate(parts, axis=0), place_both, ((1,), (1,)))
        half_rows = 16 * LINE * len(group)
        by_slot = by_slot[0:half_rows] + by_slot[half_rows:]
        for n, i in enumerate(group):
            mine = by_slot[n * LINE * 16 : (n + 1) * LINE * 16].reshape(LINE, 16, LANES)
            packed = jnp.where(lane_half_all, mine[:, 0:8], mine[:, 8:16])
            grad_out[pl.ds(plane(i) * LINE, LINE)] = packed
        for i in group:
            for peer in peers(i, i == 0):
                grad_copy(peer, me).start()

    for ring in rings[::-1]:
        give(ring[::-1])
    grad_in[me] = grad_out[me]

    color_both = jnp.concatenate([color_high, color_low], axis=0)
    shown = dot(color_both, split_a[...], ((1,), (0,)))
    shown = (
        shown[0 : 3 * TILES]
        + shown[3 * TILES :]
        + dot(color_high, split_b[...], ((1,), (0,)))
    )
    for half in range(2):
        image[pl.ds(half, 3 * TILES, stride=2), :] = shown[:, half * LANES : half * LANES + LANES]

    wait_sent(ids_copy)
    wait_sent(feat_copy)

    def scatter(ring):
        for i in ring:
            for peer in peers(i, i == 0):
                grad_copy(peer, peer).wait_recv()
        hots = []
        for n, i in enumerate(ring):
            base = plane(i) * LINE
            lanes = pl.ds(pl.multiple_of(base * CAP, LINE * CAP), LINE * CAP)
            tops = []
            bottoms = []
            for part in range(2):
                even = grad_in[base + 2 * part]
                odd = grad_in[base + 2 * part + 1]
                tops.append(jnp.where(lane_half, even, pltpu.roll(odd, CAP, 1)))
                bottoms.append(jnp.where(lane_half, pltpu.roll(even, CAP, 1), odd))
            a = jnp.concatenate(tops, axis=1)
            b = jnp.concatenate(bottoms, axis=1)
            mask = high_hot[:, lanes]
            into = slice(n * LINE * CAP, (n + 1) * LINE * CAP)
            for c in range(9):
                row = a[c : c + 1] if c < 5 else b[c - 5 : c - 4]
                for s, piece in enumerate(pieces(jnp.broadcast_to(row, (32, LINE * CAP)), 2)):
                    wide[s * 288 + c * 32 : s * 288 + c * 32 + 32, into] = piece * mask
            hots.append(low_hot[:, lanes])
        placed = dot(wide[:, 0 : len(ring) * LINE * CAP], jnp.concatenate(hots, axis=1), ((1,), (1,)))
        return placed[0:288] + placed[288:576]

    for ring in rings[:-1]:
        if ring[0] == 0:
            gathered[...] = scatter(ring)
        else:
            gathered[...] += scatter(ring)
    placed = scatter(rings[-1])
    if len(rings) > 1:
        placed = placed + gathered[...]
    placed = placed.reshape(9, 32, 256)
    dense[:, 0:32, :] = placed[:, :, 0:LANES]
    dense[:, 32:64, :] = placed[:, :, LANES:256]

    order = [7, 5, 3, 6, 2, 4, 1] if views == 8 else list(range(1, views))[::-1]
    for i in order:
        view_copy(view_peer(i), my_view).start()
    mine = pl.ds(pl.multiple_of(my_view * chunk, chunk), chunk)
    view_in[my_view] = dense[:, mine, :]

    def cam_wait(off, carry):
        peer = lax.rem(my_view + off, views)
        cam_copy(peer, peer).wait_recv()
        cam_copy(peer, my_view).wait_send()
        return carry

    lax.fori_loop(1, views, cam_wait, 0)
    wait_sent(grad_copy)

    def get(r):
        return held[r, mine, :]

    scale_quat = [get(r) for r in range(3, 10)]

    def shape_of(values):
        return covariance(values[0:3], values[3:7])

    sigma, shape_back = jax.vjp(shape_of, scale_quat)
    zero = jnp.zeros((chunk, LANES), F32)

    def add_views(members, totals, first):
        held_grads = []
        bases = []
        backs = []
        for v in members:
            camera = cam_in[v]
            x = get(0) - camera[0:1]
            y = get(1) - camera[1:2]
            z = get(2) - camera[2:3]
            grads = [view_in[v, c] for c in range(9)]
            _, geometry_back = jax.vjp(geometry, x, y, z, sigma)
            gx, gy, gz, g_sigma = geometry_back(tuple(grads[0:5]))
            add = [gx, gy, gz, grads[5]] + list(g_sigma)
            totals = tuple(t + a for t, a in zip(totals, add))
            basis, basis_back = jax.vjp(harmonic_basis, x, y, z)
            held_grads.append(grads[6:9])
            bases.append(basis)
            backs.append(basis_back)
        g_bases = [[zero] * 15 for _ in members]
        for c in range(3):
            for k in range(16):
                row = 11 + 16 * c + k
                total = zero if first else summed[row]
                for n in range(len(members)):
                    color_grad = held_grads[n][c]
                    if k == 0:
                        total = total + sh_zero * color_grad
                    else:
                        total = total + bases[n][k - 1] * color_grad
                        g_bases[n][k - 1] = g_bases[n][k - 1] + get(row) * color_grad
                summed[row] = total
        for n in range(len(members)):
            by_direction = backs[n](g_bases[n])
            totals = tuple(t + a for t, a in zip(totals[0:3], by_direction)) + totals[3:]
        return totals

    totals = tuple([zero] * 10)
    for at in range(0, views, 2):
        members = []
        for i in (at, at + 1):
            peer = my_view if i == 0 else view_peer(i)
            if i > 0:
                view_copy(peer, peer).wait_recv()
            members.append(peer)
        totals = add_views(members, totals, at == 0)
    for r in range(3):
        summed[r] = totals[r]
    (by_shape,) = shape_back(list(totals[4:10]))
    for r in range(7):
        summed[3 + r] = by_shape[r]
    summed[10] = totals[3] / (1.0 + jnp.exp(get(10)))

    def view_wait(off, carry):
        view_copy(lax.rem(my_view + off, views), my_view).wait_send()
        return carry

    lax.fori_loop(1, views, view_wait, 0)


def store_kernel(image, summed, image_ref, grads_ref, sems):
    image_store = pltpu.make_async_copy(image, image_ref, sems.at[0])
    image_store.start()
    for j in range(summed.shape[1]):
        pltpu.make_async_copy(
            summed.at[:, j, :], grads_ref.at[:, j * LANES : (j + 1) * LANES], sems.at[1]
        ).start()
    image_store.wait()
    pltpu.make_async_copy(summed, summed, sems.at[1]).wait()


def local(owners, views, params, cam_pos, req_ids, tile_slots, tile_len, cotangent):
    count, owned = params.shape
    blocks = owned // LANES
    chunk = blocks // views
    slots_all = owners * CAP
    vmem = pltpu.VMEM
    dma = pltpu.SemaphoreType.DMA
    anywhere = pl.BlockSpec(memory_space=pl.ANY)
    inside = pl.BlockSpec(memory_space=vmem)
    image, summed = pl.pallas_call(
        functools.partial(kernel, owners, views),
        out_shape=(
            vmem((6 * TILES, LANES), F32),
            vmem((count, chunk, LANES), F32),
        ),
        in_specs=[anywhere] * 6,
        out_specs=(inside, inside),
        scratch_shapes=[
            vmem((count, blocks, LANES), F32),
            vmem((owners, CAP), jnp.int32),
            vmem((1, 3), F32),
            vmem((TILES, ENTRIES), jnp.int32),
            vmem((1, TILES), jnp.int32),
            vmem((6 * TILES, LANES), F32),
            vmem((owners, 1, LANES), jnp.int32),
            vmem((owners, 1, LANES), jnp.int32),
            vmem((8, LANES), F32),
            vmem((views, 8, LANES), F32),
            vmem((736, 256), BF16),
            vmem((256, slots_all), BF16),
            vmem((32, slots_all), BF16),
            vmem((owners, 8, LANES), F32),
            vmem((owners, 8, LANES), F32),
            vmem((576, 3 * LINE * CAP), BF16),
            vmem((288, 256), F32),
            vmem((ROWS, PIXELS), F32),
            vmem((ROWS, PIXELS), F32),
            vmem((ROWS, PIXELS), F32),
            vmem((ROWS, PIXELS), F32),
            vmem((ROWS, PIXELS), BF16),
            vmem((ROWS, PIXELS), BF16),
            vmem((ROWS, PIXELS), BF16),
            vmem((ROWS, PIXELS), BF16),
            vmem((owners, 8, LANES), F32),
            vmem((owners, 8, LANES), F32),
            vmem((9, blocks, LANES), F32),
            vmem((views, 9, chunk, LANES), F32),
            dma((6,)),
        ]
        + [dma((owners,)) for _ in range(6)]
        + [dma((views,)) for _ in range(4)],
        compiler_params=pltpu.CompilerParams(
            collective_id=0, has_side_effects=True, vmem_limit_bytes=60 * 1024 * 1024
        ),
        cost_estimate=pl.CostEstimate(
            flops=2_000_000_000, bytes_accessed=4_000_000, transcendentals=300_000
        ),
    )(
        params,
        cam_pos,
        req_ids,
        tile_slots,
        tile_len,
        cotangent.reshape(6 * TILES, LANES),
    )
    image, grads = pl.pallas_call(
        store_kernel,
        out_shape=(
            pltpu.HBM((6 * TILES, LANES), F32),
            pltpu.HBM((count, owned // views), F32),
        ),
        in_specs=[inside] * 2,
        out_specs=(anywhere, anywhere),
        scratch_shapes=[dma((2,))],
        compiler_params=pltpu.CompilerParams(vmem_limit_bytes=4 * 1024 * 1024),
    )(image, summed)
    return image.reshape(cotangent.shape), grads


def solution(mesh):
    placed = (
        P(None, "gs"),
        P("view", None),
        P("view", "gs", None, None),
        P("view", "gs", None),
        P("view", "gs"),
        P("view", None, "gs"),
    )
    return jax.shard_map(
        functools.partial(local, mesh.shape["gs"], mesh.shape["view"]),
        mesh=mesh,
        in_specs=placed,
        out_specs=(P("view", None, "gs"), P(None, ("gs", "view"))),
        check_vma=False,
    )
```

```python
import functools

import jax
import jax.numpy as jnp
from jax import lax
from jax.experimental import pallas as pl
from jax.experimental.pallas import tpu as pltpu
from jax.sharding import PartitionSpec as P

MESH = pl.DeviceIdType.MESH
F32 = jnp.float32
BF16 = jnp.bfloat16
TILES = 16
ENTRIES = 64
ROWS = TILES * ENTRIES
PIXELS = 256
CAP = 64
LANES = 128
LINE = 4

focal = 1.2 * 128.0
dilate = 0.3
sh_zero = 0.28209479177387814
sh_one = 0.4886025119029199
sh_two = [
    1.0925484305920792,
    -1.0925484305920792,
    0.31539156525252005,
    -1.0925484305920792,
    0.5462742152960396,
]
sh_three = [
    -0.5900435899266435,
    2.890611442640554,
    -0.4570457994644658,
    0.3731763325901154,
    -0.4570457994644658,
    1.445305721320277,
    -0.5900435899266435,
]


def covariance(log_scales, quat):
    squares = [jnp.exp(2.0 * value) for value in log_scales]
    norm_sq = quat[0] * quat[0] + quat[1] * quat[1] + quat[2] * quat[2] + quat[3] * quat[3]
    inv_norm = 1.0 / jnp.sqrt(norm_sq)
    w, x, y, z = [value * inv_norm for value in quat]
    rotation = [
        [1 - 2 * (y * y + z * z), 2 * (x * y - w * z), 2 * (x * z + w * y)],
        [2 * (x * y + w * z), 1 - 2 * (x * x + z * z), 2 * (y * z - w * x)],
        [2 * (x * z - w * y), 2 * (y * z + w * x), 1 - 2 * (x * x + y * y)],
    ]
    scaled = [[rotation[i][j] * squares[j] for j in range(3)] for i in range(3)]

    def entry(i, j):
        return (
            scaled[i][0] * rotation[j][0]
            + scaled[i][1] * rotation[j][1]
            + scaled[i][2] * rotation[j][2]
        )

    return [entry(0, 0), entry(0, 1), entry(0, 2), entry(1, 1), entry(1, 2), entry(2, 2)]


def geometry(x, y, z, sigma):
    s00, s01, s02, s11, s12, s22 = sigma
    inv_z = 1.0 / z
    jac = focal * inv_z
    center_x = jac * x
    center_y = jac * y
    jac_x = -center_x * inv_z
    jac_y = -center_y * inv_z
    jac_sq = jac * jac
    cov_a = jac_sq * s00 + 2.0 * (jac * jac_x) * s02 + jac_x * jac_x * s22 + dilate
    cov_b = jac_sq * s01 + jac * (jac_y * s02 + jac_x * s12) + jac_x * jac_y * s22
    cov_c = jac_sq * s11 + 2.0 * (jac * jac_y) * s12 + jac_y * jac_y * s22 + dilate
    inv_det = 1.0 / (cov_a * cov_c - cov_b * cov_b)
    return center_x, center_y, cov_c * inv_det, -cov_b * inv_det, cov_a * inv_det


def harmonic_basis(x, y, z):
    inv_distance = 1.0 / jnp.sqrt(x * x + y * y + z * z)
    dx = x * inv_distance
    dy = y * inv_distance
    dz = z * inv_distance
    xx = dx * dx
    yy = dy * dy
    zz = dz * dz
    xy = dx * dy
    yz = dy * dz
    xz = dx * dz
    return [
        -sh_one * dy,
        sh_one * dz,
        -sh_one * dx,
        sh_two[0] * xy,
        sh_two[1] * yz,
        sh_two[2] * (2 * zz - xx - yy),
        sh_two[3] * xz,
        sh_two[4] * (xx - yy),
        sh_three[0] * dy * (3 * xx - yy),
        sh_three[1] * xy * dz,
        sh_three[2] * dy * (4 * zz - xx - yy),
        sh_three[3] * dz * (2 * zz - 3 * xx - 3 * yy),
        sh_three[4] * dx * (4 * zz - xx - yy),
        sh_three[5] * dz * (xx - yy),
        sh_three[6] * dx * (xx - 3 * yy),
    ]


def pieces(value, count):
    out = []
    for at in range(count):
        piece = value.astype(BF16)
        out.append(piece)
        if at + 1 < count:
            value = value - piece.astype(F32)
    return out


def dot(left, right, dims):
    return lax.dot_general(left, right, ((dims[0], dims[1]), ((), ())), preferred_element_type=F32)


def iota(shape, axis):
    return lax.broadcasted_iota(jnp.int32, shape, axis)


def kernel(
    owners,
    views,
    params_ref,
    cam_ref,
    ids_ref,
    slots_ref,
    len_ref,
    cot_ref,
    image,
    summed,
    held,
    asked,
    cam_held,
    slots_held,
    len_held,
    held_cot,
    ids_out,
    ids_in,
    cam_out,
    cam_in,
    table,
    low_hot,
    high_hot,
    feat_out,
    feat_in,
    wide,
    gathered,
    exponent,
    along,
    alpha_all,
    blend_all,
    split_a,
    split_b,
    split_c,
    split_d,
    grad_out,
    grad_in,
    dense,
    view_in,
    load_sem,
    ids_s,
    ids_r,
    feat_s,
    feat_r,
    grad_s,
    grad_r,
    cam_s,
    cam_r,
    view_s,
    view_r,
):
    me = lax.axis_index("gs")
    my_view = lax.axis_index("view")
    my_y = lax.rem(me, LINE)
    my_z = lax.div(me, LINE)
    my_x = lax.div(my_view, 2)
    my_core = lax.rem(my_view, 2)
    planes = owners // LINE
    blocks = held.shape[1]
    chunk = blocks // views

    def plane(i):
        half = (i + 1) // 2
        odd = i % 2
        return lax.rem(my_z + odd * half + (1 - odd) * (planes - half), planes)

    def peers(i, first):
        return [plane(i) * LINE + lax.rem(my_y + step, LINE) for step in range(1 if first else 0, LINE)]

    def view_peer(i):
        pair = i // 2
        step = pair + pair // 2 - 2 * (pair // 3)
        return lax.rem(my_x + step, views // 2) * 2 + lax.rem(my_core + i, 2)

    ids_load = pltpu.make_async_copy(ids_ref.at[0, 0], asked, load_sem.at[2])
    cam_load = pltpu.make_async_copy(cam_ref, cam_held, load_sem.at[3])
    slots_load = pltpu.make_async_copy(slots_ref.at[0], slots_held, load_sem.at[4])
    len_load = pltpu.make_async_copy(len_ref, len_held, load_sem.at[5])
    cot_load = pltpu.make_async_copy(cot_ref, held_cot, load_sem.at[1])
    ids_load.start()
    cam_load.start()

    barrier = pltpu.get_barrier_semaphore()

    def greet(off, carry):
        peer = lax.rem(me + off, owners)
        pl.semaphore_signal(barrier, inc=1, device_id=(my_view, peer), device_id_type=MESH)
        return carry

    lax.fori_loop(1, owners, greet, 0)

    def greet_view(off, carry):
        peer = lax.rem(my_view + off, views)
        pl.semaphore_signal(barrier, inc=1, device_id=(peer, me), device_id_type=MESH)
        return carry

    lax.fori_loop(1, views, greet_view, 0)

    def load_body(j, carry):
        pltpu.make_async_copy(
            params_ref.at[:, pl.ds(pl.multiple_of(j * LANES, LANES), LANES)],
            held.at[:, j, :],
            load_sem.at[0],
        ).start()
        return carry

    lax.fori_loop(0, blocks, load_body, 0)
    slots_load.start()
    len_load.start()
    cot_load.start()

    def ids_copy(to, sender):
        return pltpu.make_async_remote_copy(
            src_ref=ids_out.at[to],
            dst_ref=ids_in.at[sender],
            send_sem=ids_s.at[to],
            recv_sem=ids_r.at[sender],
            device_id=(my_view, to),
            device_id_type=MESH,
        )

    def feat_copy(to, sender):
        return pltpu.make_async_remote_copy(
            src_ref=feat_out.at[to, pl.ds(0, 5)],
            dst_ref=feat_in.at[sender, pl.ds(0, 5)],
            send_sem=feat_s.at[to],
            recv_sem=feat_r.at[sender],
            device_id=(my_view, to),
            device_id_type=MESH,
        )

    def grad_copy(to, sender):
        return pltpu.make_async_remote_copy(
            src_ref=grad_out.at[to, pl.ds(0, 5)],
            dst_ref=grad_in.at[sender, pl.ds(0, 5)],
            send_sem=grad_s.at[to],
            recv_sem=grad_r.at[sender],
            device_id=(my_view, to),
            device_id_type=MESH,
        )

    def cam_copy(to, sender):
        return pltpu.make_async_remote_copy(
            src_ref=cam_out,
            dst_ref=cam_in.at[sender],
            send_sem=cam_s.at[to],
            recv_sem=cam_r.at[sender],
            device_id=(to, me),
            device_id_type=MESH,
        )

    def view_copy(to, sender):
        return pltpu.make_async_remote_copy(
            src_ref=dense.at[:, pl.ds(pl.multiple_of(to * chunk, chunk), chunk), :],
            dst_ref=view_in.at[sender],
            send_sem=view_s.at[to],
            recv_sem=view_r.at[sender],
            device_id=(to, me),
            device_id_type=MESH,
        )

    def wait_sent(copy):
        def body(off, carry):
            copy(lax.rem(me + off, owners), me).wait_send()
            return carry

        lax.fori_loop(1, owners, body, 0)

    ids_load.wait()
    doubled = jnp.concatenate([asked[...], asked[...]], axis=1)
    my_half = (iota(doubled.shape, 1) >> 6) == lax.rem(me, 2)
    ids_out[...] = jnp.where(my_half, doubled, 0).reshape(owners, 1, LANES)
    ids_in[me] = ids_out[me]
    cam_load.wait()
    cam_row = iota((8, LANES), 0)
    cam_tile = jnp.where(
        cam_row == 0, cam_held[0:1, 0:1], jnp.where(cam_row == 1, cam_held[0:1, 1:2], cam_held[0:1, 2:3])
    )
    cam_out[...] = cam_tile
    cam_in[my_view] = cam_tile

    pl.semaphore_wait(barrier, owners + views - 2)

    for i in [planes - 1] + list(range(planes - 1)):
        for peer in peers(i, i == 0):
            ids_copy(peer, me).start()

    def cam_send(off, carry):
        cam_copy(lax.rem(my_view + off, views), my_view).start()
        return carry

    lax.fori_loop(1, views, cam_send, 0)

    pltpu.make_async_copy(held, held, load_sem.at[0]).wait()

    def features_body(at, carry):
        rows = pl.ds(pl.multiple_of(at * 16, 16), 16)

        def get(r):
            return held[r, rows, :]

        x = get(0) - cam_out[0:1]
        y = get(1) - cam_out[1:2]
        z = get(2) - cam_out[2:3]
        sigma = covariance([get(3), get(4), get(5)], [get(6), get(7), get(8), get(9)])
        values = list(geometry(x, y, z, sigma))
        values.append(-jnp.log(1.0 + jnp.exp(-get(10))))
        basis = harmonic_basis(x, y, z)
        for c in range(3):
            total = sh_zero * get(11 + 16 * c) + 0.5
            for k in range(15):
                total = total + basis[k] * get(12 + 16 * c + k)
            values.append(total)
        half = lax.div(at, 2)
        inner = lax.rem(at, 2)
        lanes = pl.ds(pl.multiple_of(half * LANES, LANES), LANES)
        for c in range(9):
            for s, piece in enumerate(pieces(values[c], 3)):
                if s < 2 or c < 5:
                    row = s * 288 + c * 32 + inner * 16
                    table[pl.ds(pl.multiple_of(row, 16), 16), lanes] = piece
        return carry

    lax.fori_loop(0, blocks // 16, features_body, 0)

    lane_half = iota((8, LANES), 1) < CAP

    rings = [[i for i in range(planes) if (i + 1) // 2 <= 1]]
    rings += [[i for i in range(planes) if (i + 1) // 2 == far] for far in range(2, planes // 2 + 1)]

    joined = rings[:-2] + [rings[-2] + rings[-1]] if len(rings) > 2 else rings

    def serve(i):
        base = plane(i) * LINE
        ids = jnp.concatenate(
            [ids_in[base] + ids_in[base + 1], ids_in[base + 2] + ids_in[base + 3]], axis=1
        )
        low = (ids & (LANES - 1)) + ((ids >> 12) << 7)
        high = (ids >> 7) & 31
        lanes = pl.ds(pl.multiple_of(base * CAP, LINE * CAP), LINE * CAP)
        right = (iota((256, LINE * CAP), 0) == low).astype(F32).astype(BF16)
        low_hot[:, lanes] = right
        mask = (iota((32, LINE * CAP), 0) == high).astype(F32)
        high_hot[:, lanes] = mask.astype(BF16)
        short = dot(table[0:288], right, ((1,), (0,))) + dot(table[288:576], right, ((1,), (0,)))
        rest = dot(table[576:736], right, ((1,), (0,)))
        picked = jnp.concatenate([short[0:160] + rest, short[160:]], axis=0)
        rows = [
            jnp.sum(picked[c * 32 : c * 32 + 32] * mask, axis=0, keepdims=True) for c in range(9)
        ]
        blank = jnp.zeros((1, LINE * CAP), F32)
        left_group = jnp.concatenate(rows[0:5] + [blank] * 3, axis=0)
        right_group = jnp.concatenate(rows[5:9] + [blank] * 4, axis=0)
        for part in range(2):
            a = left_group[:, part * LANES : (part + 1) * LANES]
            b = right_group[:, part * LANES : (part + 1) * LANES]
            feat_out[base + 2 * part] = jnp.where(lane_half, a, pltpu.roll(b, CAP, 1))
            feat_out[base + 2 * part + 1] = jnp.where(lane_half, pltpu.roll(a, CAP, 1), b)

    for ring in joined:
        for i in ring:
            for peer in peers(i, i == 0):
                ids_copy(peer, peer).wait_recv()
        for i in ring:
            serve(i)
        for i in ring[::-1]:
            for peer in peers(i, i == 0):
                feat_copy(peer, me).start()
    feat_in[me] = feat_out[me]

    slots_load.wait()
    len_load.wait()
    lane_row = iota((TILES, ROWS), 1)
    tile_hot = (lane_row & 15) == iota((TILES, ROWS), 0)
    tile_mask = tile_hot.astype(F32)
    entry_hot = ((iota((ENTRIES, ROWS), 1) >> 4) == iota((ENTRIES, ROWS), 0)).astype(F32).astype(BF16)
    slots = slots_held[...]
    both = jnp.concatenate([slots >> 6, slots & (CAP - 1)], axis=0).astype(F32).astype(BF16)
    spread = dot(both, entry_hot, ((1,), (0,)))
    owner_row = jnp.sum(spread[0:TILES] * tile_mask, axis=0, keepdims=True)
    place_row = jnp.sum(spread[TILES:] * tile_mask, axis=0, keepdims=True)
    lengths = jnp.broadcast_to(len_held[...], (TILES, TILES)).astype(F32).astype(BF16)
    len_row = dot(lengths, tile_mask.astype(BF16), ((1,), (0,)))[0:1]
    entry_row = iota((1, ROWS), 1)
    live = (entry_row >> 4).astype(F32) < len_row
    place_sub = iota((LANES, ROWS), 0)
    place_left = (place_sub.astype(F32) == place_row).astype(F32).astype(BF16)
    place_right = ((place_sub - CAP).astype(F32) == place_row).astype(F32).astype(BF16)
    center_of_x = (entry_row & 15).astype(F32) * 16.0 + (8.0 - 128.0)
    center_of_y = (me * 16 + 8 - 8 * owners).astype(F32)

    pixel = iota((8, PIXELS), 1)
    mono_x = (pixel & 15).astype(F32) - 7.5
    mono_y = (pixel >> 4).astype(F32) - 7.5
    kind = iota((8, PIXELS), 0)
    monomials = jnp.where(kind == 0, mono_x * mono_x, 0.0)
    monomials = jnp.where(kind == 1, mono_x * mono_y, monomials)
    monomials = jnp.where(kind == 2, mono_y * mono_y, monomials)
    monomials = jnp.where(kind == 3, mono_x, monomials)
    monomials = jnp.where(kind == 4, mono_y, monomials)
    monomials = jnp.where(kind == 5, 1.0, monomials)
    monomials_two = jnp.concatenate([monomials, jnp.zeros_like(monomials)], axis=0).astype(BF16)
    monomials_four = jnp.concatenate([monomials] * 3 + [jnp.zeros_like(monomials)], axis=0).astype(BF16)

    cot_load.wait()
    cot = jnp.concatenate(
        [held_cot[pl.ds(half, 3 * TILES, stride=2), :] for half in range(2)], axis=1
    )
    cot_high, cot_low = pieces(cot, 2)

    halves = [[jnp.zeros((8, 256), F32)] * (ROWS // 256) for _ in range(2)]

    def collect(group):
        for i in group:
            for peer in peers(i, i == 0):
                feat_copy(peer, peer).wait_recv()
        bases = [plane(i) * LINE for i in group]
        arrived = jnp.concatenate(
            [feat_in[pl.ds(base, LINE)].reshape(LINE * 8, LANES) for base in bases], axis=0
        )
        count = arrived.shape[0]
        three = pieces(arrived, 3)
        stacks = [jnp.concatenate(three, axis=0), jnp.concatenate(three[0:2], axis=0)]
        for at in range(ROWS // 256):
            lanes = slice(at * 256, at * 256 + 256)
            owners_here = owner_row[:, lanes]
            for side, hot in enumerate((place_left, place_right)):
                found = dot(stacks[side], hot[:, lanes], ((1,), (0,)))
                summed_pieces = found[0:count] + found[count : 2 * count]
                found = summed_pieces + found[2 * count :] if side == 0 else summed_pieces
                total = halves[side][at]
                for n, base in enumerate(bases):
                    for step in range(LINE):
                        row = (n * LINE + step) * 8
                        here = owners_here == (base + step).astype(F32)
                        total = jnp.where(here, found[row : row + 8], total)
                halves[side][at] = total

    near = (planes * 5 + 7) // 8
    collect(list(range(near)))
    if near < planes:
        collect(list(range(near, planes)))
    left = jnp.concatenate(halves[0], axis=1)
    right = jnp.concatenate(halves[1], axis=1)
    center_x = left[0:1] - center_of_x
    center_y = left[1:2] - center_of_y
    conic_a = left[2:3]
    conic_b = left[3:4]
    conic_c = left[4:5]
    log_opacity = right[0:1]
    colors = [right[1 + c : 2 + c] for c in range(3)]

    lin_x = conic_a * center_x + conic_b * center_y
    lin_y = conic_b * center_x + conic_c * center_y
    blank = jnp.zeros((1, ROWS), F32)
    coefs = jnp.concatenate(
        [
            jnp.where(live, -0.5 * conic_a, 0.0),
            jnp.where(live, -conic_b, 0.0),
            jnp.where(live, -0.5 * conic_c, 0.0),
            jnp.where(live, lin_x, 0.0),
            jnp.where(live, lin_y, 0.0),
            jnp.where(live, log_opacity - 0.5 * (lin_x * center_x + lin_y * center_y), -1000.0),
            blank,
            blank,
        ],
        axis=0,
    )
    coef_pieces = jnp.concatenate(
        [piece.astype(F32) for piece in pieces(coefs, 3)] + [jnp.zeros_like(coefs)], axis=0
    )
    exponent[...] = dot(coef_pieces.T.astype(BF16), monomials_four, ((1,), (0,)))

    spread_color = jnp.concatenate([colors[c] * tile_mask for c in range(3)], axis=0)
    color_high, color_low = pieces(spread_color, 2)
    color_sides = jnp.concatenate([color_high, color_high, color_low], axis=0)
    cot_sides = jnp.concatenate([cot_high, cot_low, cot_high], axis=0)
    along[...] = dot(color_sides, cot_sides, ((0,), (0,)))

    def forward_body(k, through):
        rows = pl.ds(pl.multiple_of(k * TILES, TILES), TILES)
        alpha = jnp.exp(exponent[rows, :])
        blend = through * alpha
        alpha_all[rows, :] = alpha
        blend_all[rows, :] = blend
        high, low = pieces(blend, 2)
        split_a[rows, :] = high
        split_b[rows, :] = low
        return through - blend

    lax.fori_loop(0, ENTRIES, forward_body, jnp.ones((TILES, PIXELS), F32), unroll=True)

    cot_both = jnp.concatenate([cot_high, cot_low], axis=0)
    by_color = dot(cot_both, split_a[...], ((1,), (1,)))
    by_color = (
        by_color[0 : 3 * TILES]
        + by_color[3 * TILES :]
        + dot(cot_high, split_b[...], ((1,), (1,)))
    )

    def backward_body(step, behind):
        rows = pl.ds(pl.multiple_of((ENTRIES - 1 - step) * TILES, TILES), TILES)
        gain = along[rows, :] - behind
        high, low = pieces(blend_all[rows, :] * gain, 2)
        split_c[rows, :] = high
        split_d[rows, :] = low
        return behind + alpha_all[rows, :] * gain

    lax.fori_loop(0, ENTRIES, backward_body, jnp.zeros((TILES, PIXELS), F32), unroll=True)

    moments = dot(monomials_two, split_c[...], ((1,), (1,))) + dot(
        monomials_two, split_d[...], ((1,), (1,))
    )
    grad_colors = [
        jnp.sum(by_color[c * TILES : (c + 1) * TILES] * tile_mask, axis=0, keepdims=True)
        for c in range(3)
    ]
    m_xx, m_xy, m_yy, m_x, m_y, m_one = [moments[row : row + 1] for row in range(6)]
    off_x = m_x - center_x * m_one
    off_y = m_y - center_y * m_one
    off_xx = m_xx - center_x * (m_x + off_x)
    off_xy = m_xy - center_x * m_y - center_y * off_x
    off_yy = m_yy - center_y * (m_y + off_y)
    entry_grads = jnp.concatenate(
        [
            conic_a * off_x + conic_b * off_y,
            conic_b * off_x + conic_c * off_y,
            -0.5 * off_xx,
            -off_xy,
            -0.5 * off_yy,
            blank,
            blank,
            blank,
            m_one,
            grad_colors[0],
            grad_colors[1],
            grad_colors[2],
            blank,
            blank,
            blank,
            blank,
        ],
        axis=0,
    )
    grad_high, grad_low = pieces(entry_grads, 2)

    place_both = place_left + place_right
    owner_wide = jnp.broadcast_to(owner_row, (16, ROWS)).astype(BF16)
    nothing = jnp.zeros((16, ROWS), BF16)
    lane_half_all = iota((LINE, 8, LANES), 2) < CAP

    def give(group):
        parts = []
        for piece in (grad_high, grad_low):
            for i in group:
                for step in range(LINE):
                    here = owner_wide == (plane(i) * LINE + step).astype(F32).astype(BF16)
                    parts.append(jnp.where(here, piece, nothing))
        by_slot = dot(jnp.concatenate(parts, axis=0), place_both, ((1,), (1,)))
        half_rows = 16 * LINE * len(group)
        by_slot = by_slot[0:half_rows] + by_slot[half_rows:]
        for n, i in enumerate(group):
            mine = by_slot[n * LINE * 16 : (n + 1) * LINE * 16].reshape(LINE, 16, LANES)
            packed = jnp.where(lane_half_all, mine[:, 0:8], mine[:, 8:16])
            grad_out[pl.ds(plane(i) * LINE, LINE)] = packed
        for i in group:
            for peer in peers(i, i == 0):
                grad_copy(peer, me).start()

    for ring in rings[::-1]:
        give(ring[::-1])
    grad_in[me] = grad_out[me]

    color_both = jnp.concatenate([color_high, color_low], axis=0)
    shown = dot(color_both, split_a[...], ((1,), (0,)))
    shown = (
        shown[0 : 3 * TILES]
        + shown[3 * TILES :]
        + dot(color_high, split_b[...], ((1,), (0,)))
    )
    for half in range(2):
        image[pl.ds(half, 3 * TILES, stride=2), :] = shown[:, half * LANES : half * LANES + LANES]

    wait_sent(ids_copy)
    wait_sent(feat_copy)

    def scatter(ring):
        for i in ring:
            for peer in peers(i, i == 0):
                grad_copy(peer, peer).wait_recv()
        hots = []
        for n, i in enumerate(ring):
            base = plane(i) * LINE
            lanes = pl.ds(pl.multiple_of(base * CAP, LINE * CAP), LINE * CAP)
            tops = []
            bottoms = []
            for part in range(2):
                even = grad_in[base + 2 * part]
                odd = grad_in[base + 2 * part + 1]
                tops.append(jnp.where(lane_half, even, pltpu.roll(odd, CAP, 1)))
                bottoms.append(jnp.where(lane_half, pltpu.roll(even, CAP, 1), odd))
            a = jnp.concatenate(tops, axis=1)
            b = jnp.concatenate(bottoms, axis=1)
            mask = high_hot[:, lanes]
            into = slice(n * LINE * CAP, (n + 1) * LINE * CAP)
            for c in range(9):
                row = a[c : c + 1] if c < 5 else b[c - 5 : c - 4]
                for s, piece in enumerate(pieces(jnp.broadcast_to(row, (32, LINE * CAP)), 2)):
                    wide[s * 288 + c * 32 : s * 288 + c * 32 + 32, into] = piece * mask
            hots.append(low_hot[:, lanes])
        placed = dot(wide[:, 0 : len(ring) * LINE * CAP], jnp.concatenate(hots, axis=1), ((1,), (1,)))
        return placed[0:288] + placed[288:576]

    for ring in rings[:-1]:
        if ring[0] == 0:
            gathered[...] = scatter(ring)
        else:
            gathered[...] += scatter(ring)
    placed = scatter(rings[-1])
    if len(rings) > 1:
        placed = placed + gathered[...]
    placed = placed.reshape(9, 32, 256)
    dense[:, 0:32, :] = placed[:, :, 0:LANES]
    dense[:, 32:64, :] = placed[:, :, LANES:256]

    order = [7, 5, 3, 6, 2, 4, 1] if views == 8 else list(range(1, views))[::-1]
    for i in order:
        view_copy(view_peer(i), my_view).start()
    mine = pl.ds(pl.multiple_of(my_view * chunk, chunk), chunk)
    view_in[my_view] = dense[:, mine, :]

    def cam_wait(off, carry):
        peer = lax.rem(my_view + off, views)
        cam_copy(peer, peer).wait_recv()
        cam_copy(peer, my_view).wait_send()
        return carry

    lax.fori_loop(1, views, cam_wait, 0)
    wait_sent(grad_copy)

    def get(r):
        return held[r, mine, :]

    scale_quat = [get(r) for r in range(3, 10)]

    def shape_of(values):
        return covariance(values[0:3], values[3:7])

    sigma, shape_back = jax.vjp(shape_of, scale_quat)
    zero = jnp.zeros((chunk, LANES), F32)

    def add_views(members, totals, first):
        held_grads = []
        bases = []
        backs = []
        for v in members:
            camera = cam_in[v]
            x = get(0) - camera[0:1]
            y = get(1) - camera[1:2]
            z = get(2) - camera[2:3]
            grads = [view_in[v, c] for c in range(9)]
            _, geometry_back = jax.vjp(geometry, x, y, z, sigma)
            gx, gy, gz, g_sigma = geometry_back(tuple(grads[0:5]))
            add = [gx, gy, gz, grads[5]] + list(g_sigma)
            totals = tuple(t + a for t, a in zip(totals, add))
            basis, basis_back = jax.vjp(harmonic_basis, x, y, z)
            held_grads.append(grads[6:9])
            bases.append(basis)
            backs.append(basis_back)
        g_bases = [[zero] * 15 for _ in members]
        for c in range(3):
            for k in range(16):
                row = 11 + 16 * c + k
                total = zero if first else summed[row]
                for n in range(len(members)):
                    color_grad = held_grads[n][c]
                    if k == 0:
                        total = total + sh_zero * color_grad
                    else:
                        total = total + bases[n][k - 1] * color_grad
                        g_bases[n][k - 1] = g_bases[n][k - 1] + get(row) * color_grad
                summed[row] = total
        for n in range(len(members)):
            by_direction = backs[n](g_bases[n])
            totals = tuple(t + a for t, a in zip(totals[0:3], by_direction)) + totals[3:]
        return totals

    totals = tuple([zero] * 10)
    for at in range(0, views, 2):
        members = []
        for i in (at, at + 1):
            peer = my_view if i == 0 else view_peer(i)
            if i > 0:
                view_copy(peer, peer).wait_recv()
            members.append(peer)
        totals = add_views(members, totals, at == 0)
    for r in range(3):
        summed[r] = totals[r]
    (by_shape,) = shape_back(list(totals[4:10]))
    for r in range(7):
        summed[3 + r] = by_shape[r]
    summed[10] = totals[3] / (1.0 + jnp.exp(get(10)))

    def view_wait(off, carry):
        view_copy(lax.rem(my_view + off, views), my_view).wait_send()
        return carry

    lax.fori_loop(1, views, view_wait, 0)


def store_kernel(image, summed, image_ref, grads_ref, sems):
    image_store = pltpu.make_async_copy(image, image_ref, sems.at[0])
    image_store.start()
    for j in range(summed.shape[1]):
        pltpu.make_async_copy(
            summed.at[:, j, :], grads_ref.at[:, j * LANES : (j + 1) * LANES], sems.at[1]
        ).start()
    image_store.wait()
    pltpu.make_async_copy(summed, summed, sems.at[1]).wait()


def local(owners, views, params, cam_pos, req_ids, tile_slots, tile_len, cotangent):
    count, owned = params.shape
    blocks = owned // LANES
    chunk = blocks // views
    slots_all = owners * CAP
    vmem = pltpu.VMEM
    dma = pltpu.SemaphoreType.DMA
    anywhere = pl.BlockSpec(memory_space=pl.ANY)
    inside = pl.BlockSpec(memory_space=vmem)
    image, summed = pl.pallas_call(
        functools.partial(kernel, owners, views),
        out_shape=(
            vmem((6 * TILES, LANES), F32),
            vmem((count, chunk, LANES), F32),
        ),
        in_specs=[anywhere] * 6,
        out_specs=(inside, inside),
        scratch_shapes=[
            vmem((count, blocks, LANES), F32),
            vmem((owners, CAP), jnp.int32),
            vmem((1, 3), F32),
            vmem((TILES, ENTRIES), jnp.int32),
            vmem((1, TILES), jnp.int32),
            vmem((6 * TILES, LANES), F32),
            vmem((owners, 1, LANES), jnp.int32),
            vmem((owners, 1, LANES), jnp.int32),
            vmem((8, LANES), F32),
            vmem((views, 8, LANES), F32),
            vmem((736, 256), BF16),
            vmem((256, slots_all), BF16),
            vmem((32, slots_all), BF16),
            vmem((owners, 8, LANES), F32),
            vmem((owners, 8, LANES), F32),
            vmem((576, 3 * LINE * CAP), BF16),
            vmem((288, 256), F32),
            vmem((ROWS, PIXELS), F32),
            vmem((ROWS, PIXELS), F32),
            vmem((ROWS, PIXELS), F32),
            vmem((ROWS, PIXELS), F32),
            vmem((ROWS, PIXELS), BF16),
            vmem((ROWS, PIXELS), BF16),
            vmem((ROWS, PIXELS), BF16),
            vmem((ROWS, PIXELS), BF16),
            vmem((owners, 8, LANES), F32),
            vmem((owners, 8, LANES), F32),
            vmem((9, blocks, LANES), F32),
            vmem((views, 9, chunk, LANES), F32),
            dma((6,)),
        ]
        + [dma((owners,)) for _ in range(6)]
        + [dma((views,)) for _ in range(4)],
        compiler_params=pltpu.CompilerParams(
            collective_id=0, has_side_effects=True, vmem_limit_bytes=60 * 1024 * 1024
        ),
        cost_estimate=pl.CostEstimate(
            flops=2_000_000_000, bytes_accessed=4_000_000, transcendentals=300_000
        ),
    )(
        params,
        cam_pos,
        req_ids,
        tile_slots,
        tile_len,
        cotangent.reshape(6 * TILES, LANES),
    )
    image, grads = pl.pallas_call(
        store_kernel,
        out_shape=(
            pltpu.HBM((6 * TILES, LANES), F32),
            pltpu.HBM((count, owned // views), F32),
        ),
        in_specs=[inside] * 2,
        out_specs=(anywhere, anywhere),
        scratch_shapes=[dma((2,))],
        compiler_params=pltpu.CompilerParams(vmem_limit_bytes=4 * 1024 * 1024),
    )(image, summed)
    return image.reshape(cotangent.shape), grads


def solution(mesh):
    placed = (
        P(None, "gs"),
        P("view", None),
        P("view", "gs", None, None),
        P("view", "gs", None),
        P("view", "gs"),
        P("view", None, "gs"),
    )
    return jax.shard_map(
        functools.partial(local, mesh.shape["gs"], mesh.shape["view"]),
        mesh=mesh,
        in_specs=placed,
        out_specs=(P("view", None, "gs"), P(None, ("gs", "view"))),
        check_vma=False,
    )
```

```python
import functools

import jax
import jax.numpy as jnp
from jax import lax
from jax.experimental import pallas as pl
from jax.experimental.pallas import tpu as pltpu
from jax.sharding import PartitionSpec as P

MESH = pl.DeviceIdType.MESH
F32 = jnp.float32
BF16 = jnp.bfloat16
TILES = 16
ENTRIES = 64
ROWS = TILES * ENTRIES
PIXELS = 256
CAP = 64
LANES = 128
LINE = 4

focal = 1.2 * 128.0
dilate = 0.3
sh_zero = 0.28209479177387814
sh_one = 0.4886025119029199
sh_two = [
    1.0925484305920792,
    -1.0925484305920792,
    0.31539156525252005,
    -1.0925484305920792,
    0.5462742152960396,
]
sh_three = [
    -0.5900435899266435,
    2.890611442640554,
    -0.4570457994644658,
    0.3731763325901154,
    -0.4570457994644658,
    1.445305721320277,
    -0.5900435899266435,
]


def covariance(log_scales, quat):
    squares = [jnp.exp(2.0 * value) for value in log_scales]
    norm_sq = quat[0] * quat[0] + quat[1] * quat[1] + quat[2] * quat[2] + quat[3] * quat[3]
    inv_norm = 1.0 / jnp.sqrt(norm_sq)
    w, x, y, z = [value * inv_norm for value in quat]
    rotation = [
        [1 - 2 * (y * y + z * z), 2 * (x * y - w * z), 2 * (x * z + w * y)],
        [2 * (x * y + w * z), 1 - 2 * (x * x + z * z), 2 * (y * z - w * x)],
        [2 * (x * z - w * y), 2 * (y * z + w * x), 1 - 2 * (x * x + y * y)],
    ]
    scaled = [[rotation[i][j] * squares[j] for j in range(3)] for i in range(3)]

    def entry(i, j):
        return (
            scaled[i][0] * rotation[j][0]
            + scaled[i][1] * rotation[j][1]
            + scaled[i][2] * rotation[j][2]
        )

    return [entry(0, 0), entry(0, 1), entry(0, 2), entry(1, 1), entry(1, 2), entry(2, 2)]


def geometry(x, y, z, sigma):
    s00, s01, s02, s11, s12, s22 = sigma
    inv_z = 1.0 / z
    jac = focal * inv_z
    center_x = jac * x
    center_y = jac * y
    jac_x = -center_x * inv_z
    jac_y = -center_y * inv_z
    jac_sq = jac * jac
    cov_a = jac_sq * s00 + 2.0 * (jac * jac_x) * s02 + jac_x * jac_x * s22 + dilate
    cov_b = jac_sq * s01 + jac * (jac_y * s02 + jac_x * s12) + jac_x * jac_y * s22
    cov_c = jac_sq * s11 + 2.0 * (jac * jac_y) * s12 + jac_y * jac_y * s22 + dilate
    inv_det = 1.0 / (cov_a * cov_c - cov_b * cov_b)
    return center_x, center_y, cov_c * inv_det, -cov_b * inv_det, cov_a * inv_det


def harmonic_basis(x, y, z):
    inv_distance = 1.0 / jnp.sqrt(x * x + y * y + z * z)
    dx = x * inv_distance
    dy = y * inv_distance
    dz = z * inv_distance
    xx = dx * dx
    yy = dy * dy
    zz = dz * dz
    xy = dx * dy
    yz = dy * dz
    xz = dx * dz
    return [
        -sh_one * dy,
        sh_one * dz,
        -sh_one * dx,
        sh_two[0] * xy,
        sh_two[1] * yz,
        sh_two[2] * (2 * zz - xx - yy),
        sh_two[3] * xz,
        sh_two[4] * (xx - yy),
        sh_three[0] * dy * (3 * xx - yy),
        sh_three[1] * xy * dz,
        sh_three[2] * dy * (4 * zz - xx - yy),
        sh_three[3] * dz * (2 * zz - 3 * xx - 3 * yy),
        sh_three[4] * dx * (4 * zz - xx - yy),
        sh_three[5] * dz * (xx - yy),
        sh_three[6] * dx * (xx - 3 * yy),
    ]


def pieces(value, count):
    out = []
    for at in range(count):
        piece = value.astype(BF16)
        out.append(piece)
        if at + 1 < count:
            value = value - piece.astype(F32)
    return out


def dot(left, right, dims):
    return lax.dot_general(left, right, ((dims[0], dims[1]), ((), ())), preferred_element_type=F32)


def iota(shape, axis):
    return lax.broadcasted_iota(jnp.int32, shape, axis)


def kernel(
    owners,
    views,
    params_ref,
    cam_ref,
    ids_ref,
    slots_ref,
    len_ref,
    cot_ref,
    image,
    summed,
    held,
    asked,
    cam_held,
    slots_held,
    len_held,
    held_cot,
    ids_out,
    ids_in,
    cam_out,
    cam_in,
    table,
    low_hot,
    high_hot,
    feat_out,
    feat_in,
    wide,
    gathered,
    exponent,
    along,
    alpha_all,
    blend_all,
    split_a,
    split_b,
    split_c,
    split_d,
    grad_out,
    grad_in,
    dense,
    view_in,
    load_sem,
    ids_s,
    ids_r,
    feat_s,
    feat_r,
    grad_s,
    grad_r,
    cam_s,
    cam_r,
    view_s,
    view_r,
):
    me = lax.axis_index("gs")
    my_view = lax.axis_index("view")
    my_y = lax.rem(me, LINE)
    my_z = lax.div(me, LINE)
    my_x = lax.div(my_view, 2)
    my_core = lax.rem(my_view, 2)
    planes = owners // LINE
    blocks = held.shape[1]
    chunk = blocks // views

    def plane(i):
        half = (i + 1) // 2
        odd = i % 2
        return lax.rem(my_z + odd * half + (1 - odd) * (planes - half), planes)

    def peers(i, first):
        steps = (2, 1, 3) if first else (2, 1, 3, 0)
        return [plane(i) * LINE + lax.rem(my_y + step, LINE) for step in steps]

    def view_peer(i):
        pair = i // 2
        step = pair + pair // 2 - 2 * (pair // 3)
        return lax.rem(my_x + step, views // 2) * 2 + lax.rem(my_core + i, 2)

    ids_load = pltpu.make_async_copy(ids_ref.at[0, 0], asked, load_sem.at[2])
    cam_load = pltpu.make_async_copy(cam_ref, cam_held, load_sem.at[3])
    slots_load = pltpu.make_async_copy(slots_ref.at[0], slots_held, load_sem.at[4])
    len_load = pltpu.make_async_copy(len_ref, len_held, load_sem.at[5])
    cot_load = pltpu.make_async_copy(cot_ref, held_cot, load_sem.at[1])
    ids_load.start()
    cam_load.start()

    barrier = pltpu.get_barrier_semaphore()

    def greet(off, carry):
        peer = lax.rem(me + off, owners)
        pl.semaphore_signal(barrier, inc=1, device_id=(my_view, peer), device_id_type=MESH)
        return carry

    lax.fori_loop(1, owners, greet, 0)

    def greet_view(off, carry):
        peer = lax.rem(my_view + off, views)
        pl.semaphore_signal(barrier, inc=1, device_id=(peer, me), device_id_type=MESH)
        return carry

    lax.fori_loop(1, views, greet_view, 0)

    def load_body(j, carry):
        pltpu.make_async_copy(
            params_ref.at[:, pl.ds(pl.multiple_of(j * LANES, LANES), LANES)],
            held.at[:, j, :],
            load_sem.at[0],
        ).start()
        return carry

    lax.fori_loop(0, blocks, load_body, 0)
    slots_load.start()
    len_load.start()
    cot_load.start()

    def ids_copy(to, sender):
        return pltpu.make_async_remote_copy(
            src_ref=ids_out.at[to],
            dst_ref=ids_in.at[sender],
            send_sem=ids_s.at[to],
            recv_sem=ids_r.at[sender],
            device_id=(my_view, to),
            device_id_type=MESH,
        )

    def feat_copy(to, sender):
        return pltpu.make_async_remote_copy(
            src_ref=feat_out.at[to, pl.ds(0, 5)],
            dst_ref=feat_in.at[sender, pl.ds(0, 5)],
            send_sem=feat_s.at[to],
            recv_sem=feat_r.at[sender],
            device_id=(my_view, to),
            device_id_type=MESH,
        )

    def grad_copy(to, sender):
        return pltpu.make_async_remote_copy(
            src_ref=grad_out.at[to, pl.ds(0, 5)],
            dst_ref=grad_in.at[sender, pl.ds(0, 5)],
            send_sem=grad_s.at[to],
            recv_sem=grad_r.at[sender],
            device_id=(my_view, to),
            device_id_type=MESH,
        )

    def cam_copy(to, sender):
        return pltpu.make_async_remote_copy(
            src_ref=cam_out,
            dst_ref=cam_in.at[sender],
            send_sem=cam_s.at[to],
            recv_sem=cam_r.at[sender],
            device_id=(to, me),
            device_id_type=MESH,
        )

    def view_copy(to, sender):
        return pltpu.make_async_remote_copy(
            src_ref=dense.at[:, pl.ds(pl.multiple_of(to * chunk, chunk), chunk), :],
            dst_ref=view_in.at[sender],
            send_sem=view_s.at[to],
            recv_sem=view_r.at[sender],
            device_id=(to, me),
            device_id_type=MESH,
        )

    def wait_sent(copy):
        def body(off, carry):
            copy(lax.rem(me + off, owners), me).wait_send()
            return carry

        lax.fori_loop(1, owners, body, 0)

    ids_load.wait()
    doubled = jnp.concatenate([asked[...], asked[...]], axis=1)
    my_half = (iota(doubled.shape, 1) >> 6) == lax.rem(me, 2)
    ids_out[...] = jnp.where(my_half, doubled, 0).reshape(owners, 1, LANES)
    ids_in[me] = ids_out[me]
    cam_load.wait()
    cam_row = iota((8, LANES), 0)
    cam_tile = jnp.where(
        cam_row == 0, cam_held[0:1, 0:1], jnp.where(cam_row == 1, cam_held[0:1, 1:2], cam_held[0:1, 2:3])
    )
    cam_out[...] = cam_tile
    cam_in[my_view] = cam_tile

    pl.semaphore_wait(barrier, owners + views - 2)

    for i in [planes - 1] + list(range(planes - 1)):
        for peer in peers(i, i == 0):
            ids_copy(peer, me).start()

    def cam_send(off, carry):
        cam_copy(lax.rem(my_view + off, views), my_view).start()
        return carry

    lax.fori_loop(1, views, cam_send, 0)

    pltpu.make_async_copy(held, held, load_sem.at[0]).wait()

    def features_body(at, carry):
        rows = pl.ds(pl.multiple_of(at * 16, 16), 16)

        def get(r):
            return held[r, rows, :]

        x = get(0) - cam_out[0:1]
        y = get(1) - cam_out[1:2]
        z = get(2) - cam_out[2:3]
        sigma = covariance([get(3), get(4), get(5)], [get(6), get(7), get(8), get(9)])
        values = list(geometry(x, y, z, sigma))
        values.append(-jnp.log(1.0 + jnp.exp(-get(10))))
        basis = harmonic_basis(x, y, z)
        for c in range(3):
            total = sh_zero * get(11 + 16 * c) + 0.5
            for k in range(15):
                total = total + basis[k] * get(12 + 16 * c + k)
            values.append(total)
        half = lax.div(at, 2)
        inner = lax.rem(at, 2)
        lanes = pl.ds(pl.multiple_of(half * LANES, LANES), LANES)
        for c in range(9):
            for s, piece in enumerate(pieces(values[c], 3)):
                if s < 2 or c < 5:
                    row = s * 288 + c * 32 + inner * 16
                    table[pl.ds(pl.multiple_of(row, 16), 16), lanes] = piece
        return carry

    lax.fori_loop(0, blocks // 16, features_body, 0)

    lane_half = iota((8, LANES), 1) < CAP

    rings = [[i for i in range(planes) if (i + 1) // 2 <= 1]]
    rings += [[i for i in range(planes) if (i + 1) // 2 == far] for far in range(2, planes // 2 + 1)]

    joined = rings[:-2] + [rings[-2] + rings[-1]] if len(rings) > 2 else rings

    def serve(i):
        base = plane(i) * LINE
        ids = jnp.concatenate(
            [ids_in[base] + ids_in[base + 1], ids_in[base + 2] + ids_in[base + 3]], axis=1
        )
        low = (ids & (LANES - 1)) + ((ids >> 12) << 7)
        high = (ids >> 7) & 31
        lanes = pl.ds(pl.multiple_of(base * CAP, LINE * CAP), LINE * CAP)
        right = (iota((256, LINE * CAP), 0) == low).astype(F32).astype(BF16)
        low_hot[:, lanes] = right
        mask = (iota((32, LINE * CAP), 0) == high).astype(F32)
        high_hot[:, lanes] = mask.astype(BF16)
        short = dot(table[0:288], right, ((1,), (0,))) + dot(table[288:576], right, ((1,), (0,)))
        rest = dot(table[576:736], right, ((1,), (0,)))
        picked = jnp.concatenate([short[0:160] + rest, short[160:]], axis=0)
        rows = [
            jnp.sum(picked[c * 32 : c * 32 + 32] * mask, axis=0, keepdims=True) for c in range(9)
        ]
        blank = jnp.zeros((1, LINE * CAP), F32)
        left_group = jnp.concatenate(rows[0:5] + [blank] * 3, axis=0)
        right_group = jnp.concatenate(rows[5:9] + [blank] * 4, axis=0)
        for part in range(2):
            a = left_group[:, part * LANES : (part + 1) * LANES]
            b = right_group[:, part * LANES : (part + 1) * LANES]
            feat_out[base + 2 * part] = jnp.where(lane_half, a, pltpu.roll(b, CAP, 1))
            feat_out[base + 2 * part + 1] = jnp.where(lane_half, pltpu.roll(a, CAP, 1), b)

    for ring in joined:
        for i in ring:
            for peer in peers(i, i == 0):
                ids_copy(peer, peer).wait_recv()
        for i in ring:
            serve(i)
        for i in ring[::-1]:
            for peer in peers(i, i == 0):
                feat_copy(peer, me).start()
    feat_in[me] = feat_out[me]

    slots_load.wait()
    len_load.wait()
    lane_row = iota((TILES, ROWS), 1)
    tile_hot = (lane_row & 15) == iota((TILES, ROWS), 0)
    tile_mask = tile_hot.astype(F32)
    entry_hot = ((iota((ENTRIES, ROWS), 1) >> 4) == iota((ENTRIES, ROWS), 0)).astype(F32).astype(BF16)
    slots = slots_held[...]
    both = jnp.concatenate([slots >> 6, slots & (CAP - 1)], axis=0).astype(F32).astype(BF16)
    spread = dot(both, entry_hot, ((1,), (0,)))
    owner_row = jnp.sum(spread[0:TILES] * tile_mask, axis=0, keepdims=True)
    place_row = jnp.sum(spread[TILES:] * tile_mask, axis=0, keepdims=True)
    lengths = jnp.broadcast_to(len_held[...], (TILES, TILES)).astype(F32).astype(BF16)
    len_row = dot(lengths, tile_mask.astype(BF16), ((1,), (0,)))[0:1]
    entry_row = iota((1, ROWS), 1)
    live = (entry_row >> 4).astype(F32) < len_row
    place_sub = iota((LANES, ROWS), 0)
    place_left = (place_sub.astype(F32) == place_row).astype(F32).astype(BF16)
    place_right = ((place_sub - CAP).astype(F32) == place_row).astype(F32).astype(BF16)
    center_of_x = (entry_row & 15).astype(F32) * 16.0 + (8.0 - 128.0)
    center_of_y = (me * 16 + 8 - 8 * owners).astype(F32)

    pixel = iota((8, PIXELS), 1)
    mono_x = (pixel & 15).astype(F32) - 7.5
    mono_y = (pixel >> 4).astype(F32) - 7.5
    kind = iota((8, PIXELS), 0)
    monomials = jnp.where(kind == 0, mono_x * mono_x, 0.0)
    monomials = jnp.where(kind == 1, mono_x * mono_y, monomials)
    monomials = jnp.where(kind == 2, mono_y * mono_y, monomials)
    monomials = jnp.where(kind == 3, mono_x, monomials)
    monomials = jnp.where(kind == 4, mono_y, monomials)
    monomials = jnp.where(kind == 5, 1.0, monomials)
    monomials_two = jnp.concatenate([monomials, jnp.zeros_like(monomials)], axis=0).astype(BF16)
    monomials_four = jnp.concatenate([monomials] * 3 + [jnp.zeros_like(monomials)], axis=0).astype(BF16)

    cot_load.wait()
    cot = jnp.concatenate(
        [held_cot[pl.ds(half, 3 * TILES, stride=2), :] for half in range(2)], axis=1
    )
    cot_high, cot_low = pieces(cot, 2)

    halves = [[jnp.zeros((8, 256), F32)] * (ROWS // 256) for _ in range(2)]

    def collect(group):
        for i in group:
            for peer in peers(i, i == 0):
                feat_copy(peer, peer).wait_recv()
        bases = [plane(i) * LINE for i in group]
        arrived = jnp.concatenate(
            [feat_in[pl.ds(base, LINE)].reshape(LINE * 8, LANES) for base in bases], axis=0
        )
        count = arrived.shape[0]
        three = pieces(arrived, 3)
        stacks = [jnp.concatenate(three, axis=0), jnp.concatenate(three[0:2], axis=0)]
        for at in range(ROWS // 256):
            lanes = slice(at * 256, at * 256 + 256)
            owners_here = owner_row[:, lanes]
            for side, hot in enumerate((place_left, place_right)):
                found = dot(stacks[side], hot[:, lanes], ((1,), (0,)))
                summed_pieces = found[0:count] + found[count : 2 * count]
                found = summed_pieces + found[2 * count :] if side == 0 else summed_pieces
                total = halves[side][at]
                for n, base in enumerate(bases):
                    for step in range(LINE):
                        row = (n * LINE + step) * 8
                        here = owners_here == (base + step).astype(F32)
                        total = jnp.where(here, found[row : row + 8], total)
                halves[side][at] = total

    near = (planes * 5 + 7) // 8
    collect(list(range(near)))
    if near < planes:
        collect(list(range(near, planes)))
    left = jnp.concatenate(halves[0], axis=1)
    right = jnp.concatenate(halves[1], axis=1)
    center_x = left[0:1] - center_of_x
    center_y = left[1:2] - center_of_y
    conic_a = left[2:3]
    conic_b = left[3:4]
    conic_c = left[4:5]
    log_opacity = right[0:1]
    colors = [right[1 + c : 2 + c] for c in range(3)]

    lin_x = conic_a * center_x + conic_b * center_y
    lin_y = conic_b * center_x + conic_c * center_y
    blank = jnp.zeros((1, ROWS), F32)
    coefs = jnp.concatenate(
        [
            jnp.where(live, -0.5 * conic_a, 0.0),
            jnp.where(live, -conic_b, 0.0),
            jnp.where(live, -0.5 * conic_c, 0.0),
            jnp.where(live, lin_x, 0.0),
            jnp.where(live, lin_y, 0.0),
            jnp.where(live, log_opacity - 0.5 * (lin_x * center_x + lin_y * center_y), -1000.0),
            blank,
            blank,
        ],
        axis=0,
    )
    coef_pieces = jnp.concatenate(
        [piece.astype(F32) for piece in pieces(coefs, 3)] + [jnp.zeros_like(coefs)], axis=0
    )
    exponent[...] = dot(coef_pieces.T.astype(BF16), monomials_four, ((1,), (0,)))

    spread_color = jnp.concatenate([colors[c] * tile_mask for c in range(3)], axis=0)
    color_high, color_low = pieces(spread_color, 2)
    color_sides = jnp.concatenate([color_high, color_high, color_low], axis=0)
    cot_sides = jnp.concatenate([cot_high, cot_low, cot_high], axis=0)
    along[...] = dot(color_sides, cot_sides, ((0,), (0,)))

    def forward_body(k, through):
        rows = pl.ds(pl.multiple_of(k * TILES, TILES), TILES)
        alpha = jnp.exp(exponent[rows, :])
        blend = through * alpha
        alpha_all[rows, :] = alpha
        blend_all[rows, :] = blend
        high, low = pieces(blend, 2)
        split_a[rows, :] = high
        split_b[rows, :] = low
        return through - blend

    lax.fori_loop(0, ENTRIES, forward_body, jnp.ones((TILES, PIXELS), F32), unroll=True)

    cot_both = jnp.concatenate([cot_high, cot_low], axis=0)
    by_color = dot(cot_both, split_a[...], ((1,), (1,)))
    by_color = (
        by_color[0 : 3 * TILES]
        + by_color[3 * TILES :]
        + dot(cot_high, split_b[...], ((1,), (1,)))
    )

    def backward_body(step, behind):
        rows = pl.ds(pl.multiple_of((ENTRIES - 1 - step) * TILES, TILES), TILES)
        gain = along[rows, :] - behind
        high, low = pieces(blend_all[rows, :] * gain, 2)
        split_c[rows, :] = high
        split_d[rows, :] = low
        return behind + alpha_all[rows, :] * gain

    lax.fori_loop(0, ENTRIES, backward_body, jnp.zeros((TILES, PIXELS), F32), unroll=True)

    moments = dot(monomials_two, split_c[...], ((1,), (1,))) + dot(
        monomials_two, split_d[...], ((1,), (1,))
    )
    grad_colors = [
        jnp.sum(by_color[c * TILES : (c + 1) * TILES] * tile_mask, axis=0, keepdims=True)
        for c in range(3)
    ]
    m_xx, m_xy, m_yy, m_x, m_y, m_one = [moments[row : row + 1] for row in range(6)]
    off_x = m_x - center_x * m_one
    off_y = m_y - center_y * m_one
    off_xx = m_xx - center_x * (m_x + off_x)
    off_xy = m_xy - center_x * m_y - center_y * off_x
    off_yy = m_yy - center_y * (m_y + off_y)
    entry_grads = jnp.concatenate(
        [
            conic_a * off_x + conic_b * off_y,
            conic_b * off_x + conic_c * off_y,
            -0.5 * off_xx,
            -off_xy,
            -0.5 * off_yy,
            blank,
            blank,
            blank,
            m_one,
            grad_colors[0],
            grad_colors[1],
            grad_colors[2],
            blank,
            blank,
            blank,
            blank,
        ],
        axis=0,
    )
    grad_high, grad_low = pieces(entry_grads, 2)

    place_both = place_left + place_right
    owner_wide = jnp.broadcast_to(owner_row, (16, ROWS)).astype(BF16)
    nothing = jnp.zeros((16, ROWS), BF16)
    lane_half_all = iota((LINE, 8, LANES), 2) < CAP

    def give(group):
        parts = []
        for piece in (grad_high, grad_low):
            for i in group:
                for step in range(LINE):
                    here = owner_wide == (plane(i) * LINE + step).astype(F32).astype(BF16)
                    parts.append(jnp.where(here, piece, nothing))
        by_slot = dot(jnp.concatenate(parts, axis=0), place_both, ((1,), (1,)))
        half_rows = 16 * LINE * len(group)
        by_slot = by_slot[0:half_rows] + by_slot[half_rows:]
        for n, i in enumerate(group):
            mine = by_slot[n * LINE * 16 : (n + 1) * LINE * 16].reshape(LINE, 16, LANES)
            packed = jnp.where(lane_half_all, mine[:, 0:8], mine[:, 8:16])
            grad_out[pl.ds(plane(i) * LINE, LINE)] = packed
        for i in group:
            for peer in peers(i, i == 0):
                grad_copy(peer, me).start()

    for ring in rings[::-1]:
        give(ring[::-1])
    grad_in[me] = grad_out[me]

    color_both = jnp.concatenate([color_high, color_low], axis=0)
    shown = dot(color_both, split_a[...], ((1,), (0,)))
    shown = (
        shown[0 : 3 * TILES]
        + shown[3 * TILES :]
        + dot(color_high, split_b[...], ((1,), (0,)))
    )
    for half in range(2):
        image[pl.ds(half, 3 * TILES, stride=2), :] = shown[:, half * LANES : half * LANES + LANES]

    wait_sent(ids_copy)
    wait_sent(feat_copy)

    def scatter(ring):
        for i in ring:
            for peer in peers(i, i == 0):
                grad_copy(peer, peer).wait_recv()
        hots = []
        for n, i in enumerate(ring):
            base = plane(i) * LINE
            lanes = pl.ds(pl.multiple_of(base * CAP, LINE * CAP), LINE * CAP)
            tops = []
            bottoms = []
            for part in range(2):
                even = grad_in[base + 2 * part]
                odd = grad_in[base + 2 * part + 1]
                tops.append(jnp.where(lane_half, even, pltpu.roll(odd, CAP, 1)))
                bottoms.append(jnp.where(lane_half, pltpu.roll(even, CAP, 1), odd))
            a = jnp.concatenate(tops, axis=1)
            b = jnp.concatenate(bottoms, axis=1)
            mask = high_hot[:, lanes]
            into = slice(n * LINE * CAP, (n + 1) * LINE * CAP)
            for c in range(9):
                row = a[c : c + 1] if c < 5 else b[c - 5 : c - 4]
                for s, piece in enumerate(pieces(jnp.broadcast_to(row, (32, LINE * CAP)), 2)):
                    wide[s * 288 + c * 32 : s * 288 + c * 32 + 32, into] = piece * mask
            hots.append(low_hot[:, lanes])
        placed = dot(wide[:, 0 : len(ring) * LINE * CAP], jnp.concatenate(hots, axis=1), ((1,), (1,)))
        return placed[0:288] + placed[288:576]

    for ring in rings[:-1]:
        if ring[0] == 0:
            gathered[...] = scatter(ring)
        else:
            gathered[...] += scatter(ring)
    placed = scatter(rings[-1])
    if len(rings) > 1:
        placed = placed + gathered[...]
    placed = placed.reshape(9, 32, 256)
    dense[:, 0:32, :] = placed[:, :, 0:LANES]
    dense[:, 32:64, :] = placed[:, :, LANES:256]

    order = [7, 5, 3, 6, 2, 4, 1] if views == 8 else list(range(1, views))[::-1]
    for i in order:
        view_copy(view_peer(i), my_view).start()
    mine = pl.ds(pl.multiple_of(my_view * chunk, chunk), chunk)
    view_in[my_view] = dense[:, mine, :]

    def cam_wait(off, carry):
        peer = lax.rem(my_view + off, views)
        cam_copy(peer, peer).wait_recv()
        cam_copy(peer, my_view).wait_send()
        return carry

    lax.fori_loop(1, views, cam_wait, 0)
    wait_sent(grad_copy)

    def get(r):
        return held[r, mine, :]

    scale_quat = [get(r) for r in range(3, 10)]

    def shape_of(values):
        return covariance(values[0:3], values[3:7])

    sigma, shape_back = jax.vjp(shape_of, scale_quat)
    zero = jnp.zeros((chunk, LANES), F32)

    def add_views(members, totals, first):
        held_grads = []
        bases = []
        backs = []
        for v in members:
            camera = cam_in[v]
            x = get(0) - camera[0:1]
            y = get(1) - camera[1:2]
            z = get(2) - camera[2:3]
            grads = [view_in[v, c] for c in range(9)]
            _, geometry_back = jax.vjp(geometry, x, y, z, sigma)
            gx, gy, gz, g_sigma = geometry_back(tuple(grads[0:5]))
            add = [gx, gy, gz, grads[5]] + list(g_sigma)
            totals = tuple(t + a for t, a in zip(totals, add))
            basis, basis_back = jax.vjp(harmonic_basis, x, y, z)
            held_grads.append(grads[6:9])
            bases.append(basis)
            backs.append(basis_back)
        g_bases = [[zero] * 15 for _ in members]
        for c in range(3):
            for k in range(16):
                row = 11 + 16 * c + k
                total = zero if first else summed[row]
                for n in range(len(members)):
                    color_grad = held_grads[n][c]
                    if k == 0:
                        total = total + sh_zero * color_grad
                    else:
                        total = total + bases[n][k - 1] * color_grad
                        g_bases[n][k - 1] = g_bases[n][k - 1] + get(row) * color_grad
                summed[row] = total
        for n in range(len(members)):
            by_direction = backs[n](g_bases[n])
            totals = tuple(t + a for t, a in zip(totals[0:3], by_direction)) + totals[3:]
        return totals

    totals = tuple([zero] * 10)
    for at in range(0, views, 2):
        members = []
        for i in (at, at + 1):
            peer = my_view if i == 0 else view_peer(i)
            if i > 0:
                view_copy(peer, peer).wait_recv()
            members.append(peer)
        totals = add_views(members, totals, at == 0)
    for r in range(3):
        summed[r] = totals[r]
    (by_shape,) = shape_back(list(totals[4:10]))
    for r in range(7):
        summed[3 + r] = by_shape[r]
    summed[10] = totals[3] / (1.0 + jnp.exp(get(10)))

    def view_wait(off, carry):
        view_copy(lax.rem(my_view + off, views), my_view).wait_send()
        return carry

    lax.fori_loop(1, views, view_wait, 0)


def store_kernel(image, summed, image_ref, grads_ref, sems):
    image_store = pltpu.make_async_copy(image, image_ref, sems.at[0])
    image_store.start()
    for j in range(summed.shape[1]):
        pltpu.make_async_copy(
            summed.at[:, j, :], grads_ref.at[:, j * LANES : (j + 1) * LANES], sems.at[1]
        ).start()
    image_store.wait()
    pltpu.make_async_copy(summed, summed, sems.at[1]).wait()


def local(owners, views, params, cam_pos, req_ids, tile_slots, tile_len, cotangent):
    count, owned = params.shape
    blocks = owned // LANES
    chunk = blocks // views
    slots_all = owners * CAP
    vmem = pltpu.VMEM
    dma = pltpu.SemaphoreType.DMA
    anywhere = pl.BlockSpec(memory_space=pl.ANY)
    inside = pl.BlockSpec(memory_space=vmem)
    image, summed = pl.pallas_call(
        functools.partial(kernel, owners, views),
        out_shape=(
            vmem((6 * TILES, LANES), F32),
            vmem((count, chunk, LANES), F32),
        ),
        in_specs=[anywhere] * 6,
        out_specs=(inside, inside),
        scratch_shapes=[
            vmem((count, blocks, LANES), F32),
            vmem((owners, CAP), jnp.int32),
            vmem((1, 3), F32),
            vmem((TILES, ENTRIES), jnp.int32),
            vmem((1, TILES), jnp.int32),
            vmem((6 * TILES, LANES), F32),
            vmem((owners, 1, LANES), jnp.int32),
            vmem((owners, 1, LANES), jnp.int32),
            vmem((8, LANES), F32),
            vmem((views, 8, LANES), F32),
            vmem((736, 256), BF16),
            vmem((256, slots_all), BF16),
            vmem((32, slots_all), BF16),
            vmem((owners, 8, LANES), F32),
            vmem((owners, 8, LANES), F32),
            vmem((576, 3 * LINE * CAP), BF16),
            vmem((288, 256), F32),
            vmem((ROWS, PIXELS), F32),
            vmem((ROWS, PIXELS), F32),
            vmem((ROWS, PIXELS), F32),
            vmem((ROWS, PIXELS), F32),
            vmem((ROWS, PIXELS), BF16),
            vmem((ROWS, PIXELS), BF16),
            vmem((ROWS, PIXELS), BF16),
            vmem((ROWS, PIXELS), BF16),
            vmem((owners, 8, LANES), F32),
            vmem((owners, 8, LANES), F32),
            vmem((9, blocks, LANES), F32),
            vmem((views, 9, chunk, LANES), F32),
            dma((6,)),
        ]
        + [dma((owners,)) for _ in range(6)]
        + [dma((views,)) for _ in range(4)],
        compiler_params=pltpu.CompilerParams(
            collective_id=0, has_side_effects=True, vmem_limit_bytes=60 * 1024 * 1024
        ),
        cost_estimate=pl.CostEstimate(
            flops=2_000_000_000, bytes_accessed=4_000_000, transcendentals=300_000
        ),
    )(
        params,
        cam_pos,
        req_ids,
        tile_slots,
        tile_len,
        cotangent.reshape(6 * TILES, LANES),
    )
    image, grads = pl.pallas_call(
        store_kernel,
        out_shape=(
            pltpu.HBM((6 * TILES, LANES), F32),
            pltpu.HBM((count, owned // views), F32),
        ),
        in_specs=[inside] * 2,
        out_specs=(anywhere, anywhere),
        scratch_shapes=[dma((2,))],
        compiler_params=pltpu.CompilerParams(vmem_limit_bytes=4 * 1024 * 1024),
    )(image, summed)
    return image.reshape(cotangent.shape), grads


def solution(mesh):
    placed = (
        P(None, "gs"),
        P("view", None),
        P("view", "gs", None, None),
        P("view", "gs", None),
        P("view", "gs"),
        P("view", None, "gs"),
    )
    return jax.shard_map(
        functools.partial(local, mesh.shape["gs"], mesh.shape["view"]),
        mesh=mesh,
        in_specs=placed,
        out_specs=(P("view", None, "gs"), P(None, ("gs", "view"))),
        check_vma=False,
    )
```

```python
import functools

import jax
import jax.numpy as jnp
from jax import lax
from jax.experimental import pallas as pl
from jax.experimental.pallas import tpu as pltpu
from jax.sharding import PartitionSpec as P

MESH = pl.DeviceIdType.MESH
F32 = jnp.float32
BF16 = jnp.bfloat16
TILES = 16
ENTRIES = 64
ROWS = TILES * ENTRIES
PIXELS = 256
CAP = 64
LANES = 128
LINE = 4

focal = 1.2 * 128.0
dilate = 0.3
sh_zero = 0.28209479177387814
sh_one = 0.4886025119029199
sh_two = [
    1.0925484305920792,
    -1.0925484305920792,
    0.31539156525252005,
    -1.0925484305920792,
    0.5462742152960396,
]
sh_three = [
    -0.5900435899266435,
    2.890611442640554,
    -0.4570457994644658,
    0.3731763325901154,
    -0.4570457994644658,
    1.445305721320277,
    -0.5900435899266435,
]


def covariance(log_scales, quat):
    squares = [jnp.exp(2.0 * value) for value in log_scales]
    norm_sq = quat[0] * quat[0] + quat[1] * quat[1] + quat[2] * quat[2] + quat[3] * quat[3]
    inv_norm = 1.0 / jnp.sqrt(norm_sq)
    w, x, y, z = [value * inv_norm for value in quat]
    rotation = [
        [1 - 2 * (y * y + z * z), 2 * (x * y - w * z), 2 * (x * z + w * y)],
        [2 * (x * y + w * z), 1 - 2 * (x * x + z * z), 2 * (y * z - w * x)],
        [2 * (x * z - w * y), 2 * (y * z + w * x), 1 - 2 * (x * x + y * y)],
    ]
    scaled = [[rotation[i][j] * squares[j] for j in range(3)] for i in range(3)]

    def entry(i, j):
        return (
            scaled[i][0] * rotation[j][0]
            + scaled[i][1] * rotation[j][1]
            + scaled[i][2] * rotation[j][2]
        )

    return [entry(0, 0), entry(0, 1), entry(0, 2), entry(1, 1), entry(1, 2), entry(2, 2)]


def geometry(x, y, z, sigma):
    s00, s01, s02, s11, s12, s22 = sigma
    inv_z = 1.0 / z
    jac = focal * inv_z
    center_x = jac * x
    center_y = jac * y
    jac_x = -center_x * inv_z
    jac_y = -center_y * inv_z
    jac_sq = jac * jac
    cov_a = jac_sq * s00 + 2.0 * (jac * jac_x) * s02 + jac_x * jac_x * s22 + dilate
    cov_b = jac_sq * s01 + jac * (jac_y * s02 + jac_x * s12) + jac_x * jac_y * s22
    cov_c = jac_sq * s11 + 2.0 * (jac * jac_y) * s12 + jac_y * jac_y * s22 + dilate
    inv_det = 1.0 / (cov_a * cov_c - cov_b * cov_b)
    return center_x, center_y, cov_c * inv_det, -cov_b * inv_det, cov_a * inv_det


def harmonic_basis(x, y, z):
    inv_distance = 1.0 / jnp.sqrt(x * x + y * y + z * z)
    dx = x * inv_distance
    dy = y * inv_distance
    dz = z * inv_distance
    xx = dx * dx
    yy = dy * dy
    zz = dz * dz
    xy = dx * dy
    yz = dy * dz
    xz = dx * dz
    return [
        -sh_one * dy,
        sh_one * dz,
        -sh_one * dx,
        sh_two[0] * xy,
        sh_two[1] * yz,
        sh_two[2] * (2 * zz - xx - yy),
        sh_two[3] * xz,
        sh_two[4] * (xx - yy),
        sh_three[0] * dy * (3 * xx - yy),
        sh_three[1] * xy * dz,
        sh_three[2] * dy * (4 * zz - xx - yy),
        sh_three[3] * dz * (2 * zz - 3 * xx - 3 * yy),
        sh_three[4] * dx * (4 * zz - xx - yy),
        sh_three[5] * dz * (xx - yy),
        sh_three[6] * dx * (xx - 3 * yy),
    ]


def pieces(value, count):
    out = []
    for at in range(count):
        piece = value.astype(BF16)
        out.append(piece)
        if at + 1 < count:
            value = value - piece.astype(F32)
    return out


def dot(left, right, dims):
    return lax.dot_general(left, right, ((dims[0], dims[1]), ((), ())), preferred_element_type=F32)


def iota(shape, axis):
    return lax.broadcasted_iota(jnp.int32, shape, axis)


def kernel(
    owners,
    views,
    params_ref,
    cam_ref,
    ids_ref,
    slots_ref,
    len_ref,
    cot_ref,
    image,
    summed,
    held,
    asked,
    cam_held,
    slots_held,
    len_held,
    held_cot,
    ids_out,
    ids_in,
    cam_out,
    cam_in,
    table,
    low_hot,
    high_hot,
    feat_out,
    feat_in,
    wide,
    gathered,
    exponent,
    along,
    alpha_all,
    blend_all,
    split_a,
    split_b,
    split_c,
    split_d,
    grad_out,
    grad_in,
    dense,
    view_in,
    load_sem,
    ids_s,
    ids_r,
    feat_s,
    feat_r,
    grad_s,
    grad_r,
    cam_s,
    cam_r,
    view_s,
    view_r,
):
    me = lax.axis_index("gs")
    my_view = lax.axis_index("view")
    my_y = lax.rem(me, LINE)
    my_z = lax.div(me, LINE)
    my_x = lax.div(my_view, 2)
    my_core = lax.rem(my_view, 2)
    planes = owners // LINE
    blocks = held.shape[1]
    chunk = blocks // views

    def plane(i):
        half = (i + 1) // 2
        odd = i % 2
        return lax.rem(my_z + odd * half + (1 - odd) * (planes - half), planes)

    def peers(i, first):
        steps = (2, 1, 3) if first else (2, 1, 3, 0)
        return [plane(i) * LINE + lax.rem(my_y + step, LINE) for step in steps]

    def view_peer(i):
        pair = i // 2
        step = pair + pair // 2 - 2 * (pair // 3)
        return lax.rem(my_x + step, views // 2) * 2 + lax.rem(my_core + i, 2)

    ids_load = pltpu.make_async_copy(ids_ref.at[0, 0], asked, load_sem.at[2])
    cam_load = pltpu.make_async_copy(cam_ref, cam_held, load_sem.at[3])
    slots_load = pltpu.make_async_copy(slots_ref.at[0], slots_held, load_sem.at[4])
    len_load = pltpu.make_async_copy(len_ref, len_held, load_sem.at[5])
    cot_load = pltpu.make_async_copy(cot_ref, held_cot, load_sem.at[1])
    ids_load.start()
    cam_load.start()

    barrier = pltpu.get_barrier_semaphore()

    def greet(off, carry):
        peer = lax.rem(me + off, owners)
        pl.semaphore_signal(barrier, inc=1, device_id=(my_view, peer), device_id_type=MESH)
        return carry

    lax.fori_loop(1, owners, greet, 0)

    def greet_view(off, carry):
        peer = lax.rem(my_view + off, views)
        pl.semaphore_signal(barrier, inc=1, device_id=(peer, me), device_id_type=MESH)
        return carry

    lax.fori_loop(1, views, greet_view, 0)

    def load_body(j, carry):
        pltpu.make_async_copy(
            params_ref.at[:, pl.ds(pl.multiple_of(j * LANES, LANES), LANES)],
            held.at[:, j, :],
            load_sem.at[0],
        ).start()
        return carry

    lax.fori_loop(0, blocks, load_body, 0)
    slots_load.start()
    len_load.start()
    cot_load.start()

    def ids_copy(to, sender):
        return pltpu.make_async_remote_copy(
            src_ref=ids_out.at[to],
            dst_ref=ids_in.at[sender],
            send_sem=ids_s.at[to],
            recv_sem=ids_r.at[sender],
            device_id=(my_view, to),
            device_id_type=MESH,
        )

    def feat_copy(to, sender):
        return pltpu.make_async_remote_copy(
            src_ref=feat_out.at[to, pl.ds(0, 5)],
            dst_ref=feat_in.at[sender, pl.ds(0, 5)],
            send_sem=feat_s.at[to],
            recv_sem=feat_r.at[sender],
            device_id=(my_view, to),
            device_id_type=MESH,
        )

    def grad_copy(to, sender):
        return pltpu.make_async_remote_copy(
            src_ref=grad_out.at[to, pl.ds(0, 5)],
            dst_ref=grad_in.at[sender, pl.ds(0, 5)],
            send_sem=grad_s.at[to],
            recv_sem=grad_r.at[sender],
            device_id=(my_view, to),
            device_id_type=MESH,
        )

    def cam_copy(to, sender):
        return pltpu.make_async_remote_copy(
            src_ref=cam_out,
            dst_ref=cam_in.at[sender],
            send_sem=cam_s.at[to],
            recv_sem=cam_r.at[sender],
            device_id=(to, me),
            device_id_type=MESH,
        )

    def view_copy(to, sender):
        return pltpu.make_async_remote_copy(
            src_ref=dense.at[:, pl.ds(pl.multiple_of(to * chunk, chunk), chunk), :],
            dst_ref=view_in.at[sender],
            send_sem=view_s.at[to],
            recv_sem=view_r.at[sender],
            device_id=(to, me),
            device_id_type=MESH,
        )

    def wait_sent(copy):
        def body(off, carry):
            copy(lax.rem(me + off, owners), me).wait_send()
            return carry

        lax.fori_loop(1, owners, body, 0)

    ids_load.wait()
    doubled = jnp.concatenate([asked[...], asked[...]], axis=1)
    my_half = (iota(doubled.shape, 1) >> 6) == lax.rem(me, 2)
    ids_out[...] = jnp.where(my_half, doubled, 0).reshape(owners, 1, LANES)
    ids_in[me] = ids_out[me]
    cam_load.wait()
    cam_row = iota((8, LANES), 0)
    cam_tile = jnp.where(
        cam_row == 0, cam_held[0:1, 0:1], jnp.where(cam_row == 1, cam_held[0:1, 1:2], cam_held[0:1, 2:3])
    )
    cam_out[...] = cam_tile
    cam_in[my_view] = cam_tile

    pl.semaphore_wait(barrier, owners + views - 2)

    for i in [planes - 1] + list(range(planes - 1)):
        for peer in peers(i, i == 0):
            ids_copy(peer, me).start()

    def cam_send(off, carry):
        cam_copy(lax.rem(my_view + off, views), my_view).start()
        return carry

    lax.fori_loop(1, views, cam_send, 0)

    pltpu.make_async_copy(held, held, load_sem.at[0]).wait()

    def features_body(at, carry):
        rows = pl.ds(pl.multiple_of(at * 16, 16), 16)

        def get(r):
            return held[r, rows, :]

        x = get(0) - cam_out[0:1]
        y = get(1) - cam_out[1:2]
        z = get(2) - cam_out[2:3]
        sigma = covariance([get(3), get(4), get(5)], [get(6), get(7), get(8), get(9)])
        values = list(geometry(x, y, z, sigma))
        values.append(-jnp.log(1.0 + jnp.exp(-get(10))))
        basis = harmonic_basis(x, y, z)
        for c in range(3):
            total = sh_zero * get(11 + 16 * c) + 0.5
            for k in range(15):
                total = total + basis[k] * get(12 + 16 * c + k)
            values.append(total)
        half = lax.div(at, 2)
        inner = lax.rem(at, 2)
        lanes = pl.ds(pl.multiple_of(half * LANES, LANES), LANES)
        for c in range(9):
            for s, piece in enumerate(pieces(values[c], 3)):
                if s < 2 or c < 5:
                    row = s * 288 + c * 32 + inner * 16
                    table[pl.ds(pl.multiple_of(row, 16), 16), lanes] = piece
        return carry

    lax.fori_loop(0, blocks // 16, features_body, 0)

    lane_half = iota((8, LANES), 1) < CAP

    rings = [[i for i in range(planes) if (i + 1) // 2 <= 1]]
    rings += [[i for i in range(planes) if (i + 1) // 2 == far] for far in range(2, planes // 2 + 1)]

    joined = rings[:-2] + [rings[-2] + rings[-1]] if len(rings) > 2 else rings

    def serve(i):
        base = plane(i) * LINE
        ids = jnp.concatenate(
            [ids_in[base] + ids_in[base + 1], ids_in[base + 2] + ids_in[base + 3]], axis=1
        )
        low = (ids & (LANES - 1)) + ((ids >> 12) << 7)
        high = (ids >> 7) & 31
        lanes = pl.ds(pl.multiple_of(base * CAP, LINE * CAP), LINE * CAP)
        right = (iota((256, LINE * CAP), 0) == low).astype(F32).astype(BF16)
        low_hot[:, lanes] = right
        mask = (iota((32, LINE * CAP), 0) == high).astype(F32)
        high_hot[:, lanes] = mask.astype(BF16)
        short = dot(table[0:288], right, ((1,), (0,))) + dot(table[288:576], right, ((1,), (0,)))
        rest = dot(table[576:736], right, ((1,), (0,)))
        picked = jnp.concatenate([short[0:160] + rest, short[160:]], axis=0)
        rows = [
            jnp.sum(picked[c * 32 : c * 32 + 32] * mask, axis=0, keepdims=True) for c in range(9)
        ]
        blank = jnp.zeros((1, LINE * CAP), F32)
        left_group = jnp.concatenate(rows[0:5] + [blank] * 3, axis=0)
        right_group = jnp.concatenate(rows[5:9] + [blank] * 4, axis=0)
        for part in range(2):
            a = left_group[:, part * LANES : (part + 1) * LANES]
            b = right_group[:, part * LANES : (part + 1) * LANES]
            feat_out[base + 2 * part] = jnp.where(lane_half, a, pltpu.roll(b, CAP, 1))
            feat_out[base + 2 * part + 1] = jnp.where(lane_half, pltpu.roll(a, CAP, 1), b)

    for ring in joined:
        for i in ring:
            for peer in peers(i, i == 0):
                ids_copy(peer, peer).wait_recv()
        for i in ring:
            serve(i)
        for i in ring[::-1]:
            for peer in peers(i, i == 0):
                feat_copy(peer, me).start()
    feat_in[me] = feat_out[me]

    slots_load.wait()
    len_load.wait()
    lane_row = iota((TILES, ROWS), 1)
    tile_hot = (lane_row & 15) == iota((TILES, ROWS), 0)
    tile_mask = tile_hot.astype(F32)
    entry_hot = ((iota((ENTRIES, ROWS), 1) >> 4) == iota((ENTRIES, ROWS), 0)).astype(F32).astype(BF16)
    slots = slots_held[...]
    both = jnp.concatenate([slots >> 6, slots & (CAP - 1)], axis=0).astype(F32).astype(BF16)
    spread = dot(both, entry_hot, ((1,), (0,)))
    owner_row = jnp.sum(spread[0:TILES] * tile_mask, axis=0, keepdims=True)
    place_row = jnp.sum(spread[TILES:] * tile_mask, axis=0, keepdims=True)
    lengths = jnp.broadcast_to(len_held[...], (TILES, TILES)).astype(F32).astype(BF16)
    len_row = dot(lengths, tile_mask.astype(BF16), ((1,), (0,)))[0:1]
    entry_row = iota((1, ROWS), 1)
    live = (entry_row >> 4).astype(F32) < len_row
    place_sub = iota((LANES, ROWS), 0)
    place_left = (place_sub.astype(F32) == place_row).astype(F32).astype(BF16)
    place_right = ((place_sub - CAP).astype(F32) == place_row).astype(F32).astype(BF16)
    center_of_x = (entry_row & 15).astype(F32) * 16.0 + (8.0 - 128.0)
    center_of_y = (me * 16 + 8 - 8 * owners).astype(F32)

    pixel = iota((8, PIXELS), 1)
    mono_x = (pixel & 15).astype(F32) - 7.5
    mono_y = (pixel >> 4).astype(F32) - 7.5
    kind = iota((8, PIXELS), 0)
    monomials = jnp.where(kind == 0, mono_x * mono_x, 0.0)
    monomials = jnp.where(kind == 1, mono_x * mono_y, monomials)
    monomials = jnp.where(kind == 2, mono_y * mono_y, monomials)
    monomials = jnp.where(kind == 3, mono_x, monomials)
    monomials = jnp.where(kind == 4, mono_y, monomials)
    monomials = jnp.where(kind == 5, 1.0, monomials)
    monomials_two = jnp.concatenate([monomials, jnp.zeros_like(monomials)], axis=0).astype(BF16)
    monomials_four = jnp.concatenate([monomials] * 3 + [jnp.zeros_like(monomials)], axis=0).astype(BF16)

    cot_load.wait()
    cot = jnp.concatenate(
        [held_cot[pl.ds(half, 3 * TILES, stride=2), :] for half in range(2)], axis=1
    )
    cot_high, cot_low = pieces(cot, 2)

    halves = [[jnp.zeros((8, 256), F32)] * (ROWS // 256) for _ in range(2)]

    def collect(group):
        for i in group:
            for peer in peers(i, i == 0):
                feat_copy(peer, peer).wait_recv()
        bases = [plane(i) * LINE for i in group]
        arrived = jnp.concatenate(
            [feat_in[pl.ds(base, LINE)].reshape(LINE * 8, LANES) for base in bases], axis=0
        )
        count = arrived.shape[0]
        three = pieces(arrived, 3)
        stacks = [jnp.concatenate(three, axis=0), jnp.concatenate(three[0:2], axis=0)]
        for at in range(ROWS // 256):
            lanes = slice(at * 256, at * 256 + 256)
            owners_here = owner_row[:, lanes]
            for side, hot in enumerate((place_left, place_right)):
                found = dot(stacks[side], hot[:, lanes], ((1,), (0,)))
                summed_pieces = found[0:count] + found[count : 2 * count]
                found = summed_pieces + found[2 * count :] if side == 0 else summed_pieces
                total = halves[side][at]
                for n, base in enumerate(bases):
                    for step in range(LINE):
                        row = (n * LINE + step) * 8
                        here = owners_here == (base + step).astype(F32)
                        total = jnp.where(here, found[row : row + 8], total)
                halves[side][at] = total

    near = (planes * 5 + 7) // 8
    collect(list(range(near)))
    if near < planes:
        collect(list(range(near, planes)))
    left = jnp.concatenate(halves[0], axis=1)
    right = jnp.concatenate(halves[1], axis=1)
    center_x = left[0:1] - center_of_x
    center_y = left[1:2] - center_of_y
    conic_a = left[2:3]
    conic_b = left[3:4]
    conic_c = left[4:5]
    log_opacity = right[0:1]
    colors = [right[1 + c : 2 + c] for c in range(3)]

    lin_x = conic_a * center_x + conic_b * center_y
    lin_y = conic_b * center_x + conic_c * center_y
    blank = jnp.zeros((1, ROWS), F32)
    coefs = jnp.concatenate(
        [
            jnp.where(live, -0.5 * conic_a, 0.0),
            jnp.where(live, -conic_b, 0.0),
            jnp.where(live, -0.5 * conic_c, 0.0),
            jnp.where(live, lin_x, 0.0),
            jnp.where(live, lin_y, 0.0),
            jnp.where(live, log_opacity - 0.5 * (lin_x * center_x + lin_y * center_y), -1000.0),
            blank,
            blank,
        ],
        axis=0,
    )
    coef_pieces = jnp.concatenate(
        [piece.astype(F32) for piece in pieces(coefs, 3)] + [jnp.zeros_like(coefs)], axis=0
    )
    exponent[...] = dot(coef_pieces.T.astype(BF16), monomials_four, ((1,), (0,)))

    spread_color = jnp.concatenate([colors[c] * tile_mask for c in range(3)], axis=0)
    color_high, color_low = pieces(spread_color, 2)
    color_sides = jnp.concatenate([color_high, color_high, color_low], axis=0)
    cot_sides = jnp.concatenate([cot_high, cot_low, cot_high], axis=0)
    along[...] = dot(color_sides, cot_sides, ((0,), (0,)))

    def forward_body(k, through):
        rows = pl.ds(pl.multiple_of(k * TILES, TILES), TILES)
        alpha = jnp.exp(exponent[rows, :])
        blend = through * alpha
        alpha_all[rows, :] = alpha
        blend_all[rows, :] = blend
        high, low = pieces(blend, 2)
        split_a[rows, :] = high
        split_b[rows, :] = low
        return through - blend

    lax.fori_loop(0, ENTRIES, forward_body, jnp.ones((TILES, PIXELS), F32), unroll=True)

    cot_both = jnp.concatenate([cot_high, cot_low], axis=0)
    by_color = dot(cot_both, split_a[...], ((1,), (1,)))
    by_color = (
        by_color[0 : 3 * TILES]
        + by_color[3 * TILES :]
        + dot(cot_high, split_b[...], ((1,), (1,)))
    )

    def backward_body(step, behind):
        rows = pl.ds(pl.multiple_of((ENTRIES - 1 - step) * TILES, TILES), TILES)
        gain = along[rows, :] - behind
        high, low = pieces(blend_all[rows, :] * gain, 2)
        split_c[rows, :] = high
        split_d[rows, :] = low
        return behind + alpha_all[rows, :] * gain

    lax.fori_loop(0, ENTRIES, backward_body, jnp.zeros((TILES, PIXELS), F32), unroll=True)

    moments = dot(monomials_two, split_c[...], ((1,), (1,))) + dot(
        monomials_two, split_d[...], ((1,), (1,))
    )
    grad_colors = [
        jnp.sum(by_color[c * TILES : (c + 1) * TILES] * tile_mask, axis=0, keepdims=True)
        for c in range(3)
    ]
    m_xx, m_xy, m_yy, m_x, m_y, m_one = [moments[row : row + 1] for row in range(6)]
    off_x = m_x - center_x * m_one
    off_y = m_y - center_y * m_one
    off_xx = m_xx - center_x * (m_x + off_x)
    off_xy = m_xy - center_x * m_y - center_y * off_x
    off_yy = m_yy - center_y * (m_y + off_y)
    entry_grads = jnp.concatenate(
        [
            conic_a * off_x + conic_b * off_y,
            conic_b * off_x + conic_c * off_y,
            -0.5 * off_xx,
            -off_xy,
            -0.5 * off_yy,
            blank,
            blank,
            blank,
            m_one,
            grad_colors[0],
            grad_colors[1],
            grad_colors[2],
            blank,
            blank,
            blank,
            blank,
        ],
        axis=0,
    )
    grad_high, grad_low = pieces(entry_grads, 2)

    place_both = place_left + place_right
    owner_wide = jnp.broadcast_to(owner_row, (16, ROWS)).astype(BF16)
    nothing = jnp.zeros((16, ROWS), BF16)
    lane_half_all = iota((LINE, 8, LANES), 2) < CAP

    def give(group):
        parts = []
        for piece in (grad_high, grad_low):
            for i in group:
                for step in range(LINE):
                    here = owner_wide == (plane(i) * LINE + step).astype(F32).astype(BF16)
                    parts.append(jnp.where(here, piece, nothing))
        by_slot = dot(jnp.concatenate(parts, axis=0), place_both, ((1,), (1,)))
        half_rows = 16 * LINE * len(group)
        by_slot = by_slot[0:half_rows] + by_slot[half_rows:]
        for n, i in enumerate(group):
            mine = by_slot[n * LINE * 16 : (n + 1) * LINE * 16].reshape(LINE, 16, LANES)
            packed = jnp.where(lane_half_all, mine[:, 0:8], mine[:, 8:16])
            grad_out[pl.ds(plane(i) * LINE, LINE)] = packed
        for i in group:
            for peer in peers(i, i == 0):
                grad_copy(peer, me).start()

    middle = [i for ring in rings[1:-1] for i in ring]
    for ring in [rings[0], middle, rings[-1]][::-1] if middle else rings[::-1]:
        give(ring[::-1])
    grad_in[me] = grad_out[me]

    wait_sent(ids_copy)
    wait_sent(feat_copy)

    def scatter(ring):
        for i in ring:
            for peer in peers(i, i == 0):
                grad_copy(peer, peer).wait_recv()
        hots = []
        for n, i in enumerate(ring):
            base = plane(i) * LINE
            lanes = pl.ds(pl.multiple_of(base * CAP, LINE * CAP), LINE * CAP)
            tops = []
            bottoms = []
            for part in range(2):
                even = grad_in[base + 2 * part]
                odd = grad_in[base + 2 * part + 1]
                tops.append(jnp.where(lane_half, even, pltpu.roll(odd, CAP, 1)))
                bottoms.append(jnp.where(lane_half, pltpu.roll(even, CAP, 1), odd))
            a = jnp.concatenate(tops, axis=1)
            b = jnp.concatenate(bottoms, axis=1)
            mask = high_hot[:, lanes]
            into = slice(n * LINE * CAP, (n + 1) * LINE * CAP)
            for c in range(9):
                row = a[c : c + 1] if c < 5 else b[c - 5 : c - 4]
                for s, piece in enumerate(pieces(jnp.broadcast_to(row, (32, LINE * CAP)), 2)):
                    wide[s * 288 + c * 32 : s * 288 + c * 32 + 32, into] = piece * mask
            hots.append(low_hot[:, lanes])
        placed = dot(wide[:, 0 : len(ring) * LINE * CAP], jnp.concatenate(hots, axis=1), ((1,), (1,)))
        return placed[0:288] + placed[288:576]

    for ring in rings[:-1]:
        if ring[0] == 0:
            gathered[...] = scatter(ring)
        else:
            gathered[...] += scatter(ring)
    placed = scatter(rings[-1])
    if len(rings) > 1:
        placed = placed + gathered[...]
    placed = placed.reshape(9, 32, 256)
    dense[:, 0:32, :] = placed[:, :, 0:LANES]
    dense[:, 32:64, :] = placed[:, :, LANES:256]

    order = [7, 5, 3, 6, 2, 4, 1] if views == 8 else list(range(1, views))[::-1]
    for i in order:
        view_copy(view_peer(i), my_view).start()
    mine = pl.ds(pl.multiple_of(my_view * chunk, chunk), chunk)
    view_in[my_view] = dense[:, mine, :]

    def cam_wait(off, carry):
        peer = lax.rem(my_view + off, views)
        cam_copy(peer, peer).wait_recv()
        cam_copy(peer, my_view).wait_send()
        return carry

    lax.fori_loop(1, views, cam_wait, 0)
    wait_sent(grad_copy)

    color_both = jnp.concatenate([color_high, color_low], axis=0)
    shown = dot(color_both, split_a[...], ((1,), (0,)))
    shown = (
        shown[0 : 3 * TILES]
        + shown[3 * TILES :]
        + dot(color_high, split_b[...], ((1,), (0,)))
    )
    for half in range(2):
        image[pl.ds(half, 3 * TILES, stride=2), :] = shown[:, half * LANES : half * LANES + LANES]

    def get(r):
        return held[r, mine, :]

    scale_quat = [get(r) for r in range(3, 10)]

    def shape_of(values):
        return covariance(values[0:3], values[3:7])

    sigma, shape_back = jax.vjp(shape_of, scale_quat)
    zero = jnp.zeros((chunk, LANES), F32)

    def add_views(members, totals, first):
        held_grads = []
        bases = []
        backs = []
        for v in members:
            camera = cam_in[v]
            x = get(0) - camera[0:1]
            y = get(1) - camera[1:2]
            z = get(2) - camera[2:3]
            grads = [view_in[v, c] for c in range(9)]
            _, geometry_back = jax.vjp(geometry, x, y, z, sigma)
            gx, gy, gz, g_sigma = geometry_back(tuple(grads[0:5]))
            add = [gx, gy, gz, grads[5]] + list(g_sigma)
            totals = tuple(t + a for t, a in zip(totals, add))
            basis, basis_back = jax.vjp(harmonic_basis, x, y, z)
            held_grads.append(grads[6:9])
            bases.append(basis)
            backs.append(basis_back)
        g_bases = [[zero] * 15 for _ in members]
        for c in range(3):
            for k in range(16):
                row = 11 + 16 * c + k
                total = zero if first else summed[row]
                for n in range(len(members)):
                    color_grad = held_grads[n][c]
                    if k == 0:
                        total = total + sh_zero * color_grad
                    else:
                        total = total + bases[n][k - 1] * color_grad
                        g_bases[n][k - 1] = g_bases[n][k - 1] + get(row) * color_grad
                summed[row] = total
        for n in range(len(members)):
            by_direction = backs[n](g_bases[n])
            totals = tuple(t + a for t, a in zip(totals[0:3], by_direction)) + totals[3:]
        return totals

    totals = tuple([zero] * 10)
    for at in range(0, views, 2):
        members = []
        for i in (at, at + 1):
            peer = my_view if i == 0 else view_peer(i)
            if i > 0:
                view_copy(peer, peer).wait_recv()
            members.append(peer)
        totals = add_views(members, totals, at == 0)
    for r in range(3):
        summed[r] = totals[r]
    (by_shape,) = shape_back(list(totals[4:10]))
    for r in range(7):
        summed[3 + r] = by_shape[r]
    summed[10] = totals[3] / (1.0 + jnp.exp(get(10)))

    def view_wait(off, carry):
        view_copy(lax.rem(my_view + off, views), my_view).wait_send()
        return carry

    lax.fori_loop(1, views, view_wait, 0)


def store_kernel(image, summed, image_ref, grads_ref, sems):
    image_store = pltpu.make_async_copy(image, image_ref, sems.at[0])
    image_store.start()
    for j in range(summed.shape[1]):
        pltpu.make_async_copy(
            summed.at[:, j, :], grads_ref.at[:, j * LANES : (j + 1) * LANES], sems.at[1]
        ).start()
    image_store.wait()
    pltpu.make_async_copy(summed, summed, sems.at[1]).wait()


def local(owners, views, params, cam_pos, req_ids, tile_slots, tile_len, cotangent):
    count, owned = params.shape
    blocks = owned // LANES
    chunk = blocks // views
    slots_all = owners * CAP
    vmem = pltpu.VMEM
    dma = pltpu.SemaphoreType.DMA
    anywhere = pl.BlockSpec(memory_space=pl.ANY)
    inside = pl.BlockSpec(memory_space=vmem)
    image, summed = pl.pallas_call(
        functools.partial(kernel, owners, views),
        out_shape=(
            vmem((6 * TILES, LANES), F32),
            vmem((count, chunk, LANES), F32),
        ),
        in_specs=[anywhere] * 6,
        out_specs=(inside, inside),
        scratch_shapes=[
            vmem((count, blocks, LANES), F32),
            vmem((owners, CAP), jnp.int32),
            vmem((1, 3), F32),
            vmem((TILES, ENTRIES), jnp.int32),
            vmem((1, TILES), jnp.int32),
            vmem((6 * TILES, LANES), F32),
            vmem((owners, 1, LANES), jnp.int32),
            vmem((owners, 1, LANES), jnp.int32),
            vmem((8, LANES), F32),
            vmem((views, 8, LANES), F32),
            vmem((736, 256), BF16),
            vmem((256, slots_all), BF16),
            vmem((32, slots_all), BF16),
            vmem((owners, 8, LANES), F32),
            vmem((owners, 8, LANES), F32),
            vmem((576, 3 * LINE * CAP), BF16),
            vmem((288, 256), F32),
            vmem((ROWS, PIXELS), F32),
            vmem((ROWS, PIXELS), F32),
            vmem((ROWS, PIXELS), F32),
            vmem((ROWS, PIXELS), F32),
            vmem((ROWS, PIXELS), BF16),
            vmem((ROWS, PIXELS), BF16),
            vmem((ROWS, PIXELS), BF16),
            vmem((ROWS, PIXELS), BF16),
            vmem((owners, 8, LANES), F32),
            vmem((owners, 8, LANES), F32),
            vmem((9, blocks, LANES), F32),
            vmem((views, 9, chunk, LANES), F32),
            dma((6,)),
        ]
        + [dma((owners,)) for _ in range(6)]
        + [dma((views,)) for _ in range(4)],
        compiler_params=pltpu.CompilerParams(
            collective_id=0, has_side_effects=True, vmem_limit_bytes=60 * 1024 * 1024
        ),
        cost_estimate=pl.CostEstimate(
            flops=2_000_000_000, bytes_accessed=4_000_000, transcendentals=300_000
        ),
    )(
        params,
        cam_pos,
        req_ids,
        tile_slots,
        tile_len,
        cotangent.reshape(6 * TILES, LANES),
    )
    image, grads = pl.pallas_call(
        store_kernel,
        out_shape=(
            pltpu.HBM((6 * TILES, LANES), F32),
            pltpu.HBM((count, owned // views), F32),
        ),
        in_specs=[inside] * 2,
        out_specs=(anywhere, anywhere),
        scratch_shapes=[dma((2,))],
        compiler_params=pltpu.CompilerParams(vmem_limit_bytes=4 * 1024 * 1024),
    )(image, summed)
    return image.reshape(cotangent.shape), grads


def solution(mesh):
    placed = (
        P(None, "gs"),
        P("view", None),
        P("view", "gs", None, None),
        P("view", "gs", None),
        P("view", "gs"),
        P("view", None, "gs"),
    )
    return jax.shard_map(
        functools.partial(local, mesh.shape["gs"], mesh.shape["view"]),
        mesh=mesh,
        in_specs=placed,
        out_specs=(P("view", None, "gs"), P(None, ("gs", "view"))),
        check_vma=False,
    )
```
